128 devices in a mesh: row: 8 (over y, core), col: 16 (over z, x).
Axes of the slice: x: 4, y: 4, z: 4, core: 2. Of those that a mesh axis runs over, the one named last changes fastest.
Arguments:
- latents: bfloat16 [32768, 1024], P(('row', 'col')), may hold values from -24 to 24
- noise: bfloat16 [32768, 1024], P(('col', 'row')), may hold values from -6 to 6
- pairing: int32 [32768], P('row'), may hold values from 0 to 32767, as said below
- time_bucket: int32 [32768], P(('row', 'col')), may hold values from 0 to 999
Outputs:
- potential_f: float32 [32768], P(('row', 'col'))
- potential_g: float32 [32768], P(('col', 'row'))
- interpolant: bfloat16 [32768, 1024], P(('row', 'col'))
- log_weight: float32 [32768], P(('row', 'col'))
The draws below stay inside these ranges and needn't reach their ends.
Inputs may be any that keep to these rules, and one draw needn't show every extreme that they name: pairing is a permutation of 0..32767. Cut the latents into aligned blocks of 256 and the noise draws into aligned blocks of 2048: at most 32 latents of one latent block are paired with one noise block, and this many are reached.
All inputs are finite; a program needn't handle non-finite values.
Results may differ from the reference program's by a relative error of at most 0.001.
Values may be sent and summed in bfloat16 or wider, within the bound.
A program may use at most 128 MiB of HBM per device.

```python
import math
import jax
import jax.numpy as jnp
from jax import lax

D = 1024
B_DEV = 256
ITERS = 4
BUCKETS = 1000
TOTAL = 32768
DATA_BLOCK = 4096
N_ROW = 8
N_COL = 16


def shared_noise(key):
    noise_key = jax.random.fold_in(key, 0)
    values = jnp.clip(jax.random.normal(noise_key, (TOTAL, D), jnp.float32), -6.0, 6.0)
    return values


def draw_noise(key, part):
    values = shared_noise(key)
    return values.astype(jnp.bfloat16)


def draw_latents(key, part):
    own_key = jax.random.fold_in(key, 3)
    value_key = jax.random.fold_in(own_key, 0)
    values = jnp.clip(jax.random.normal(value_key, (TOTAL, D), jnp.float32), -6.0, 6.0)
    block_place = (jnp.arange(TOTAL) // DATA_BLOCK).astype(jnp.float32)
    spread_steps = max(N_ROW - 1, 1)
    rising = 1.0 + 2.0 * block_place / spread_steps
    values = values * rising[:, None]
    return values.astype(jnp.bfloat16)


def draw_pairing(key, part):
    key = jax.random.fold_in(key, 7)
    bins_key, shift_key, order_key, layout_key = jax.random.split(key, 4)
    average = B_DEV // N_COL
    noise_span = B_DEV * N_ROW
    owners = N_ROW * N_COL
    chosen_bins = jax.random.randint(bins_key, (average,), 0, N_COL - 1)
    deficit = jnp.sum((chosen_bins[:, None] == jnp.arange(N_COL - 1)[None, :]).astype(jnp.int32), axis=0)
    excess = jnp.concatenate([jnp.full((1,), average, jnp.int32), -deficit])
    shifts = jax.vmap(lambda subkey: jax.random.permutation(subkey, N_COL))(jax.random.split(shift_key, N_ROW))
    target = jnp.arange(N_COL)
    counts = average + excess[(target[None, None, :] + shifts[:, :, None]) % N_COL]
    counts = counts.reshape(owners, N_COL).astype(jnp.int32)
    position = jnp.arange(B_DEV)
    bounds_end = jnp.cumsum(counts, axis=1)
    lower_bound = bounds_end - counts
    source = jnp.sum((position[None, :, None] >= bounds_end[:, None, :]).astype(jnp.int32), axis=2)
    before = jnp.cumsum(counts, axis=0) - counts
    onehot = source[:, :, None] == target[None, None, :]
    shift_rank = jnp.sum(jnp.where(onehot, (before - lower_bound)[:, None, :], 0), axis=2)
    block_rank = position[None, :] + shift_rank
    orders = jax.vmap(lambda subkey: jax.random.permutation(subkey, noise_span))(jax.random.split(order_key, N_COL))
    noise_index = (source * noise_span + orders[source, block_rank]).astype(jnp.int32)
    layouts = jax.vmap(lambda subkey: jax.random.permutation(subkey, B_DEV))(jax.random.split(layout_key, owners))
    result = jnp.zeros((owners, B_DEV), jnp.int32).at[jnp.arange(owners)[:, None], layouts].set(noise_index)
    return result.reshape(owners * B_DEV)


def set_ends(values, rng, low, top_value):
    shape = values.shape
    place = [jax.random.randint(jax.random.fold_in(rng, axis), (), 0, shape[axis]) for axis in range(len(shape))]
    values = values.at[tuple(place)].set(low)
    longest = shape.index(max(shape))
    place[longest] = (place[longest] + 1) % shape[longest]
    return values.at[tuple(place)].set(top_value)


def setup_inputs(seed: int = 0) -> dict:
    seeds = jax.random.split(jax.random.key(seed), 5)
    return {
        "latents": draw_latents(jax.random.fold_in(seeds[4], 71), 0),
        "noise": draw_noise(jax.random.fold_in(seeds[4], 71), 0),
        "pairing": draw_pairing(jax.random.fold_in(seeds[4], 71), 0),
        "time_bucket": set_ends(jax.random.randint(seeds[3], (TOTAL,), 0, BUCKETS), jax.random.fold_in(seeds[3], 1), 0, BUCKETS - 1).astype(jnp.int32),
    }


entropic = 0.1


def reference(latents, noise, pairing, time_bucket):
    total_rows = latents.shape[0]
    features = latents.shape[1]
    offset = entropic * math.log(total_rows)
    data_values = latents.astype(jnp.float32)
    noise_values = noise.astype(jnp.float32)
    data_norms = jnp.sum(data_values * data_values, axis=1)
    noise_norms = jnp.sum(noise_values * noise_values, axis=1)
    block_size = math.gcd(total_rows, 1024)
    blocks_count = total_rows // block_size
    data_blocks = data_values.reshape(blocks_count, block_size, features)
    norm_blocks = data_norms.reshape(blocks_count, block_size)

    def cost_of(block_rows, norms):
        products = jnp.dot(block_rows, noise_values.T, precision=lax.Precision.HIGHEST, preferred_element_type=jnp.float32)
        return (norms[:, None] + noise_norms[None, :] - 2.0 * products) / features

    def row_pass(potential):
        def block_pass(inputs):
            block_rows, norms = inputs
            scores = (potential[None, :] - cost_of(block_rows, norms)) / entropic
            peak = jnp.max(scores, axis=1)
            return -entropic * (peak + jnp.log(jnp.sum(jnp.exp(scores - peak[:, None]), axis=1))) - offset
        return lax.map(block_pass, (data_blocks, norm_blocks)).reshape(total_rows)

    def column_pass(potential):
        potential_blocks = potential.reshape(blocks_count, block_size)

        def block_pass(carry, inputs):
            peak, running = carry
            block_rows, norms, values = inputs
            scores = (values[:, None] - cost_of(block_rows, norms)) / entropic
            new_peak = jnp.maximum(peak, jnp.max(scores, axis=0))
            running = running * jnp.exp(peak - new_peak) + jnp.sum(jnp.exp(scores - new_peak[None, :]), axis=0)
            return (new_peak, running), None

        start = (jnp.full((total_rows,), -jnp.inf, jnp.float32), jnp.zeros((total_rows,), jnp.float32))
        (peak, running), _ = lax.scan(block_pass, start, (data_blocks, norm_blocks, potential_blocks))
        return -entropic * (peak + jnp.log(running)) - offset

    potential_g = jnp.zeros((total_rows,), jnp.float32)
    potential_f = potential_g
    for iteration in range(ITERS):
        potential_f = row_pass(potential_g)
        potential_g = column_pass(potential_f)
    paired = noise_values[pairing]
    pair_cost = jnp.sum(jnp.square(data_values - paired), axis=1) / features
    log_weight = (potential_f + potential_g[pairing] - pair_cost) / entropic + math.log(total_rows)
    moment = (time_bucket.astype(jnp.float32) + 0.5) / BUCKETS
    interpolant = ((1.0 - moment)[:, None] * data_values + moment[:, None] * paired).astype(jnp.bfloat16)
    return potential_f, potential_g, interpolant, log_weight
```

```python
import functools
import math

import jax
import jax.numpy as jnp
from jax import lax
from jax.experimental import pallas as pl
from jax.experimental.pallas import tpu as pltpu
from jax.sharding import PartitionSpec as P

ITERS = 4
BUCKETS = 1000
MESH = pl.DeviceIdType.MESH
LOW = 2.0**-40
HIGH = 2.0**40
F32 = jnp.float32
BF16 = jnp.bfloat16

entropic = 0.1


def row_update(cost, potential, offset):
    scores = (potential[None, :] - cost) / entropic
    peak = lax.pmax(jnp.max(scores, axis=1), "col")
    running = lax.psum(jnp.sum(jnp.exp(scores - peak[:, None]), axis=1), "col")
    return -entropic * (peak + jnp.log(running)) - offset


def column_update(cost, potential, offset):
    scores = (potential[:, None] - cost) / entropic
    peak = lax.pmax(jnp.max(scores, axis=0), "row")
    running = lax.psum(jnp.sum(jnp.exp(scores - peak[None, :]), axis=0), "row")
    return -entropic * (peak + jnp.log(running)) - offset


def log_domain(latents, noise, pairing):
    own_rows, features = latents.shape
    col_count = lax.axis_size("col")
    total_rows = own_rows * lax.axis_size("row") * col_count
    offset = entropic * math.log(total_rows)
    column = lax.axis_index("col")
    row_place = lax.axis_index("row")
    noise_rows = lax.all_gather(noise, "row", axis=0, tiled=True)
    noise_span = noise_rows.shape[0]
    noise_norms = jnp.sum(jnp.square(noise_rows.astype(F32)), axis=1)
    data_rows = lax.all_gather(latents, "col", axis=0, tiled=True)
    section_norms = jnp.sum(jnp.square(data_rows.astype(F32)), axis=1)
    products = lax.dot_general(
        data_rows, noise_rows, (((1,), (1,)), ((), ())), preferred_element_type=F32
    )
    cost = (section_norms[:, None] + noise_norms[None, :] - 2.0 * products) / features
    potential_g = jnp.zeros((noise_span,), F32)
    potential_f = jnp.zeros((cost.shape[0],), F32)
    for iteration in range(ITERS):
        potential_f = row_update(cost, potential_g, offset)
        potential_g = column_update(cost, potential_f, offset)
    own_f = lax.dynamic_slice_in_dim(potential_f, column * own_rows, own_rows)
    own_g = lax.dynamic_slice_in_dim(potential_g, row_place * own_rows, own_rows)
    all_g = lax.all_gather(potential_g, "col", axis=0, tiled=True)
    own_requests = lax.dynamic_slice_in_dim(pairing, column * own_rows, own_rows)
    return own_f, own_g, all_g[own_requests]


def dot_nt(a, b):
    return lax.dot_general(a, b, (((1,), (1,)), ((), ())), preferred_element_type=F32)


def dot_nn(a, b):
    return lax.dot_general(a, b, (((1,), (0,)), ((), ())), preferred_element_type=F32)


def three_parts(v):
    hi = v.astype(BF16)
    rest = v - hi.astype(F32)
    mid = rest.astype(BF16)
    low = (rest - mid.astype(F32)).astype(BF16)
    return hi, mid, low


def turn_to_lanes(v):
    n = v.shape[0]
    parts = [
        jnp.sum(jnp.transpose(v[q * 128 : (q + 1) * 128, :]), axis=0, keepdims=True)
        for q in range(n // 128)
    ]
    return parts[0] if len(parts) == 1 else jnp.concatenate(parts, axis=1)


def spread_rows(v):
    return jnp.transpose(jnp.broadcast_to(v, (128, 128)))


def kernel(
    n_row, n_col, features, total_rows,
    lat, noi, req, bucket,
    out_f, out_g, out_w, out_c, out_bad, out_i,
    x_buf, y_buf, e_buf, s_buf, norm_y, wide, pick, send_rows, got_rows,
    f_got, g_got, pg_got, peak, scale, tops, sums, rank,
    own_sem, x_send, x_recv, y_send, y_recv, f_send, f_recv, g_send, g_recv,
    p_send, p_recv, q_send, q_recv,
):
    rows = 256
    span = n_row * rows
    row = lax.axis_index("row")
    col = lax.axis_index("col")
    log2e = math.log2(math.e)
    unit = log2e / (features * entropic)

    def col_peer(k):
        return {"col": lax.rem(col + k, n_col)}

    def row_peer(k):
        return {"row": lax.rem(row + k, n_row)}

    barrier = pltpu.get_barrier_semaphore()

    def greet_col(k, _):
        pl.semaphore_signal(barrier, inc=1, device_id=col_peer(k), device_id_type=MESH)
        return 0

    def greet_row(k, _):
        pl.semaphore_signal(barrier, inc=1, device_id=row_peer(k), device_id_type=MESH)
        return 0

    lax.fori_loop(1, n_col, greet_col, 0)
    lax.fori_loop(1, n_row, greet_row, 0)
    own_x = pltpu.make_async_copy(lat, x_buf.at[col], own_sem.at[0])
    own_y = pltpu.make_async_copy(noi, y_buf.at[row], own_sem.at[1])
    own_x.start()
    own_y.start()
    pl.semaphore_wait(barrier, n_col + n_row - 2)

    def x_copy(k):
        return pltpu.make_async_remote_copy(
            src_ref=lat, dst_ref=x_buf.at[col], send_sem=x_send.at[k], recv_sem=x_recv.at[k],
            device_id=col_peer(k), device_id_type=MESH,
        )

    def y_copy(k):
        return pltpu.make_async_remote_copy(
            src_ref=noi, dst_ref=y_buf.at[row], send_sem=y_send.at[k], recv_sem=y_recv.at[k],
            device_id=row_peer(k), device_id_type=MESH,
        )

    def f_copy(it, k):
        return pltpu.make_async_remote_copy(
            src_ref=f_got.at[it, col], dst_ref=f_got.at[it, col],
            send_sem=f_send.at[it, k], recv_sem=f_recv.at[it, k],
            device_id=col_peer(k), device_id_type=MESH,
        )

    def g_copy(it, k):
        return pltpu.make_async_remote_copy(
            src_ref=g_got.at[it, row], dst_ref=g_got.at[it, row],
            send_sem=g_send.at[it, k], recv_sem=g_recv.at[it, k],
            device_id=row_peer(k), device_id_type=MESH,
        )

    def p_copy(k):
        return pltpu.make_async_remote_copy(
            src_ref=send_rows.at[lax.rem(col + k, n_col)], dst_ref=got_rows.at[col],
            send_sem=p_send.at[k], recv_sem=p_recv.at[k],
            device_id=col_peer(k), device_id_type=MESH,
        )

    def q_copy(k):
        return pltpu.make_async_remote_copy(
            src_ref=pg_got.at[n_col + lax.rem(col + k, n_col) // 4], dst_ref=pg_got.at[col],
            send_sem=q_send.at[k], recv_sem=q_recv.at[k],
            device_id=col_peer(k), device_id_type=MESH,
        )

    def each(n, act):
        def step(k, _):
            act(k)
            return 0

        lax.fori_loop(1, n, step, 0)

    each(n_row, lambda k: y_copy(k).start())
    each(n_col, lambda k: x_copy(k).start())

    requests = req[...]
    before = (
        lax.broadcasted_iota(jnp.int32, (rows, rows), 0)
        < lax.broadcasted_iota(jnp.int32, (rows, rows), 1)
    ).astype(F32).astype(BF16)
    wanted = ((requests // span) == col).astype(F32)
    place = dot_nn(wanted.astype(BF16), before)
    rank[0:n_col, :] = jnp.where(wanted > 0.0, place, -1.0)
    rank[n_col : 2 * n_col, :] = (requests - col * span + 1).astype(F32)

    slots = lax.broadcasted_iota(jnp.int32, (32, rows), 0).astype(F32)
    places = lax.broadcasted_iota(jnp.int32, (32, span), 1).astype(F32) + 1.0

    def choose(d, _):
        chosen = rank[pl.ds(d, 1), :] == slots
        index = jnp.sum(jnp.where(chosen, rank[pl.ds(n_col + d, 1), :], 0.0), axis=1, keepdims=True)
        pick[pl.ds(pl.multiple_of(d * 32, 32), 32), :] = (places == index).astype(F32).astype(BF16)
        return 0

    lax.fori_loop(0, n_col, choose, 0)

    own_y.wait()
    each(n_row, lambda k: y_copy(k).wait_recv())

    def norms(r, _):
        v = y_buf[r].astype(F32)
        n = jnp.sum(v * v, axis=1, keepdims=True) * unit
        norm_y[pl.ds(pl.multiple_of(r * rows, rows), rows), :] = jnp.broadcast_to(n, (rows, 128))
        return 0

    lax.fori_loop(0, n_row, norms, 0)

    def fill(q, _):
        at = pl.multiple_of(q * 128, 128)
        total = jnp.zeros((128, features), F32)
        for r in range(n_row):
            total = total + dot_nn(pick[pl.ds(at, 128), r * rows : (r + 1) * rows], y_buf[r])
        send_rows[pl.ds(q * 4, 4)] = total.astype(BF16).reshape(4, 32, features)
        return 0

    lax.fori_loop(0, n_col // 4, fill, 0)
    got_rows[col] = send_rows[col]

    def scores(slot, c, r):
        at = pl.multiple_of(r * rows, rows)
        norm = norm_y[pl.ds(at, rows), :]
        t = dot_nt(y_buf[r], x_buf[c]) * (2.0 * unit) - jnp.concatenate([norm, norm], axis=1)
        s_buf[slot, pl.ds(at, rows), :] = t
        tops[slot] = jnp.maximum(tops[slot], jnp.max(t.reshape(rows // 8, 8, rows), axis=0))

    def powers(slot, c, r):
        at = pl.multiple_of(r * rows, rows)
        v = jnp.exp2(s_buf[slot, pl.ds(at, rows), :] - peak[pl.ds(c, 1), :])
        e_buf[c, pl.ds(at, rows), :] = v
        sums[slot] = sums[slot] + jnp.sum(v.reshape(rows // 8, 8, rows), axis=0)

    def opened(slot):
        tops[slot] = jnp.full((8, rows), -3.0e38, F32)
        sums[slot] = jnp.zeros((8, rows), F32)

    def topped(slot, c):
        peak[pl.ds(c, 1), :] = jnp.max(tops[slot], axis=0, keepdims=True)

    def closed(slot, c):
        total = jnp.sum(sums[slot], axis=0, keepdims=True)
        f_got[0, col, pl.ds(c, 1), :] = peak[pl.ds(c, 1), :] + jnp.log2(total)

    def block_of(k):
        return lax.rem(col + n_col - k, n_col)

    own_x.wait()
    opened(0)
    lax.fori_loop(0, n_row, lambda r, _: (scores(0, col, r), 0)[1], 0)
    topped(0, col)

    def block(k, _):
        x_copy(k).wait_recv()
        slot = lax.rem(k, 2)
        c = block_of(k)
        p = block_of(k - 1)
        opened(slot)

        def both(r, _):
            scores(slot, c, r)
            powers(1 - slot, p, r)
            return 0

        lax.fori_loop(0, n_row, both, 0)
        topped(slot, c)
        closed(1 - slot, p)
        return 0

    lax.fori_loop(1, n_col, block, 0)
    last = (n_col - 1) % 2
    lax.fori_loop(0, n_row, lambda r, _: (powers(last, block_of(n_col - 1), r), 0)[1], 0)
    closed(last, block_of(n_col - 1))

    def in_range(v):
        return (v >= LOW) & (v <= HIGH)

    def column_pass(it):
        def body(q, _):
            at = pl.multiple_of(q * 32, 32)
            total = jnp.zeros((32, rows), F32)
            for c in range(n_col):
                total = total + e_buf[c, pl.ds(at, 32), :] * scale[c : c + 1, :]
            wide[pl.ds(at, 32), :] = total[:, :128] + total[:, 128:]
            return 0

        lax.fori_loop(0, span // 32, body, 0)
        for r in range(n_row):
            g_got[it, row, r : r + 1, :] = turn_to_lanes(wide[r * rows : (r + 1) * rows, :])

    def row_pass(it):
        for q in range(n_col // 4):

            def body(j, acc):
                at = pl.multiple_of(j * 64, 64)
                b = wide[pl.ds(at, 64), :]
                b = jnp.concatenate([b, b], axis=1)
                return tuple(
                    acc[i] + jnp.sum((e_buf[q * 4 + i, pl.ds(at, 64), :] * b).reshape(8, 8, rows), axis=0)
                    for i in range(4)
                )

            acc = lax.fori_loop(0, span // 64, body, tuple(jnp.zeros((8, rows), F32) for _ in range(4)))
            for i in range(4):
                c = q * 4 + i
                f_got[it, col, c : c + 1, :] = jnp.sum(acc[i], axis=0, keepdims=True) * scale[n_col + c : n_col + c + 1, :]

    def summed(ref, it, n):
        total = ref[it, 0]
        for d in range(1, n):
            total = total + ref[it, d]
        return total

    own_lse = None
    own_p = None
    big_q = None
    for it in range(ITERS):
        if it > 0:
            row_pass(it)
        each(n_col, lambda k: f_copy(it, k).start())
        each(n_col, lambda k: f_copy(it, k).wait_recv())
        if it == 0:
            top = f_got[0, 0]
            for d in range(1, n_col):
                top = jnp.maximum(top, f_got[0, d])
            total = jnp.zeros_like(top)
            for d in range(n_col):
                total = total + jnp.exp2(f_got[0, d] - top)
            lse = top + jnp.log2(total)
            rank[0:n_col, :] = lse
            weight = jnp.exp2(peak[...] - lse)
            scale[n_col : 2 * n_col, :] = weight
            scale[0:n_col, :] = weight
        else:
            total = summed(f_got, it, n_col)
            a = jnp.where(in_range(total), 1.0 / total, jnp.nan)
            scale[0:n_col, :] = a * scale[n_col : 2 * n_col, :]
            if it == ITERS - 1:
                rank[n_col : 2 * n_col, :] = total
        column_pass(it)
        each(n_row, lambda k: g_copy(it, k).start())
        if it == 0:
            each(n_col, lambda k: p_copy(k).start())
        if it == ITERS - 1:
            each(n_col, lambda k: p_copy(k).wait_recv())
            mine = req[pl.ds(col, 1), :]
            anchor = mine // span
            marker = lax.broadcasted_iota(jnp.int32, (n_col, rows), 0) == anchor
            marked = marker.astype(F32)
            spot = jnp.sum(marked * dot_nn(marked.astype(BF16), before), axis=0, keepdims=True)
            flat = anchor.astype(F32) * 32.0 + spot
            tick = (bucket[...].astype(F32) + 0.5) / BUCKETS
            lanes = lax.broadcasted_iota(jnp.int32, (128, 32 * n_col), 1).astype(F32)
            costs = []
            squares = []
            for h in range(2):
                flat_h = spread_rows(flat[:, h * 128 : (h + 1) * 128])
                take = (lanes == flat_h[:, :1]).astype(F32).astype(BF16)
                paired = dot_nn(take, got_rows[...].reshape(32 * n_col, features))
                data = x_buf[col, h * 128 : (h + 1) * 128, :].astype(F32)
                t = spread_rows(tick[:, h * 128 : (h + 1) * 128])[:, :1]
                out_i[h * 128 : (h + 1) * 128, :] = ((1.0 - t) * data + t * paired).astype(BF16)
                diff = data - paired
                cost = diff * diff
                square = data * data
                fold_c = cost[:, :128]
                fold_s = square[:, :128]
                for q in range(1, features // 128):
                    fold_c = fold_c + cost[:, q * 128 : (q + 1) * 128]
                    fold_s = fold_s + square[:, q * 128 : (q + 1) * 128]
                costs.append(turn_to_lanes(fold_c))
                squares.append(turn_to_lanes(fold_s))
            pair_cost = jnp.concatenate(costs, axis=1) / features
            norm_x = jnp.concatenate(squares, axis=1) / features
        each(n_row, lambda k: g_copy(it, k).wait_recv())
        big_q = summed(g_got, it, n_row)
        if it < ITERS - 1:
            b = jnp.where(in_range(big_q), 1.0 / big_q, jnp.nan)
            for r in range(n_row):
                for h in range(2):
                    at = r * rows + h * 128
                    wide[at : at + 128, :] = spread_rows(b[r : r + 1, h * 128 : (h + 1) * 128])

    fine = jnp.min(jnp.where(in_range(big_q), 1.0, 0.0), axis=(0, 1), keepdims=True)
    g = jnp.where(fine > 0.0, -entropic * jnp.log(big_q), jnp.nan)
    chosen = [jnp.zeros((8, 32 * n_col), F32)]
    for part in three_parts(g):
        for r in range(n_row):
            one = jnp.broadcast_to(part[r : r + 1, :], (8, rows))
            chosen[0] = chosen[0] + dot_nt(one, pick[:, r * rows : (r + 1) * rows])
    for q in range(n_col // 4):
        pg_got[n_col + q] = chosen[0][:1, q * 128 : (q + 1) * 128]
    each(n_col, lambda k: q_copy(k).start())
    pg_got[col] = pg_got[n_col + col // 4]
    log_total = math.log(total_rows)
    lse = rank[pl.ds(col, 1), :]
    own_p = rank[pl.ds(n_col + col, 1), :]
    f = norm_x - entropic * (lse / log2e + jnp.log(own_p) + log_total)
    out_f[...] = f
    rank[0:n_row, :] = g
    out_g[...] = rank[pl.ds(row, 1), :]
    offset = lax.rem(col, 4) * 32
    grab = (
        lax.broadcasted_iota(jnp.int32, (128, rows), 0).astype(F32) == spot + offset.astype(F32)
    ).astype(F32).astype(BF16)
    each(n_col, lambda k: q_copy(k).wait_recv())
    arrived = jnp.concatenate([pg_got[d] for d in range(n_col)], axis=0)
    paired_g = jnp.zeros((n_col, rows), F32)
    for part in three_parts(arrived):
        paired_g = paired_g + dot_nn(part, grab)
    paired_g = jnp.sum(jnp.where(marker, paired_g, 0.0), axis=0, keepdims=True)
    out_c[...] = pair_cost
    out_w[...] = (f + paired_g - pair_cost) / entropic + log_total
    out_bad[...] = jnp.broadcast_to(
        jnp.max(jnp.where(arrived == arrived, 0.0, 1.0), axis=(0, 1), keepdims=True), (1, 128)
    )

    each(n_row, lambda k: y_copy(k).wait_send())
    each(n_col, lambda k: x_copy(k).wait_send())
    each(n_col, lambda k: p_copy(k).wait_send())
    each(n_col, lambda k: q_copy(k).wait_send())
    for it in range(ITERS):
        each(n_col, lambda k: f_copy(it, k).wait_send())
        each(n_row, lambda k: g_copy(it, k).wait_send())


def shards(latents, noise, pairing, time_bucket):
    own_rows, features = latents.shape
    n_row = lax.axis_size("row")
    n_col = lax.axis_size("col")
    total_rows = own_rows * n_row * n_col
    span = own_rows * n_row
    vmem = pl.BlockSpec(memory_space=pltpu.VMEM)
    hbm = pl.BlockSpec(memory_space=pl.ANY)
    line = jax.ShapeDtypeStruct((1, own_rows), F32)
    dma = pltpu.SemaphoreType.DMA
    f, g, w, pair_cost, bad, interpolant = pl.pallas_call(
        functools.partial(kernel, n_row, n_col, features, total_rows),
        out_shape=(
            line, line, line, line,
            jax.ShapeDtypeStruct((1, 128), F32),
            jax.ShapeDtypeStruct((own_rows, features), BF16),
        ),
        in_specs=[hbm, hbm, vmem, vmem],
        out_specs=(vmem,) * 6,
        scratch_shapes=[
            pltpu.VMEM((n_col, own_rows, features), BF16),
            pltpu.VMEM((n_row, own_rows, features), BF16),
            pltpu.VMEM((n_col, span, own_rows), F32),
            pltpu.VMEM((2, span, own_rows), F32),
            pltpu.VMEM((span, 128), F32),
            pltpu.VMEM((span, 128), F32),
            pltpu.VMEM((32 * n_col, span), BF16),
            pltpu.VMEM((n_col, 32, features), BF16),
            pltpu.VMEM((n_col, 32, features), BF16),
            pltpu.VMEM((ITERS, n_col, n_col, own_rows), F32),
            pltpu.VMEM((ITERS, n_row, n_row, own_rows), F32),
            pltpu.VMEM((n_col + n_col // 4, 1, 128), F32),
            pltpu.VMEM((n_col, own_rows), F32),
            pltpu.VMEM((2 * n_col, own_rows), F32),
            pltpu.VMEM((2, 8, own_rows), F32),
            pltpu.VMEM((2, 8, own_rows), F32),
            pltpu.VMEM((2 * n_col, own_rows), F32),
            dma((2,)),
            dma((n_col,)), dma((n_col,)),
            dma((n_row,)), dma((n_row,)),
            dma((ITERS, n_col)), dma((ITERS, n_col)),
            dma((ITERS, n_row)), dma((ITERS, n_row)),
            dma((n_col,)), dma((n_col,)),
            dma((n_col,)), dma((n_col,)),
        ],
        compiler_params=pltpu.CompilerParams(
            collective_id=0, has_side_effects=True, vmem_limit_bytes=62 * 1024 * 1024
        ),
        name="pairing_plan",
    )(latents, noise, pairing.reshape(n_col, own_rows), time_bucket.reshape(1, own_rows))
    f, g, w, pair_cost = (v.reshape(own_rows) for v in (f, g, w, pair_cost))

    def again():
        exact_f, exact_g, paired_g = log_domain(latents, noise, pairing)
        log_weight = (exact_f + paired_g - pair_cost) / entropic + math.log(total_rows)
        return exact_f, exact_g, log_weight

    f, g, w = lax.cond(bad[0, 0] > 0.0, again, lambda: (f, g, w))
    return f, g, interpolant, w


def solution(mesh):
    placed = (P(("row", "col"), None), P(("col", "row"), None), P("row"), P(("row", "col")))
    return jax.shard_map(
        shards,
        mesh=mesh,
        in_specs=placed,
        out_specs=(
            P(("row", "col")),
            P(("col", "row")),
            P(("row", "col"), None),
            P(("row", "col")),
        ),
        check_vma=False,
    )
```

```python
import functools
import math

import jax
import jax.numpy as jnp
from jax import lax
from jax.experimental import pallas as pl
from jax.experimental.pallas import tpu as pltpu
from jax.sharding import PartitionSpec as P

ITERS = 4
BUCKETS = 1000
MESH = pl.DeviceIdType.MESH
LOW = 2.0**-40
HIGH = 2.0**40
F32 = jnp.float32
BF16 = jnp.bfloat16

entropic = 0.1


def row_update(cost, potential, offset):
    scores = (potential[None, :] - cost) / entropic
    peak = lax.pmax(jnp.max(scores, axis=1), "col")
    running = lax.psum(jnp.sum(jnp.exp(scores - peak[:, None]), axis=1), "col")
    return -entropic * (peak + jnp.log(running)) - offset


def column_update(cost, potential, offset):
    scores = (potential[:, None] - cost) / entropic
    peak = lax.pmax(jnp.max(scores, axis=0), "row")
    running = lax.psum(jnp.sum(jnp.exp(scores - peak[None, :]), axis=0), "row")
    return -entropic * (peak + jnp.log(running)) - offset


def log_domain(latents, noise, pairing):
    own_rows, features = latents.shape
    col_count = lax.axis_size("col")
    total_rows = own_rows * lax.axis_size("row") * col_count
    offset = entropic * math.log(total_rows)
    column = lax.axis_index("col")
    row_place = lax.axis_index("row")
    noise_rows = lax.all_gather(noise, "row", axis=0, tiled=True)
    noise_span = noise_rows.shape[0]
    noise_norms = jnp.sum(jnp.square(noise_rows.astype(F32)), axis=1)
    data_rows = lax.all_gather(latents, "col", axis=0, tiled=True)
    section_norms = jnp.sum(jnp.square(data_rows.astype(F32)), axis=1)
    products = lax.dot_general(
        data_rows, noise_rows, (((1,), (1,)), ((), ())), preferred_element_type=F32
    )
    cost = (section_norms[:, None] + noise_norms[None, :] - 2.0 * products) / features
    potential_g = jnp.zeros((noise_span,), F32)
    potential_f = jnp.zeros((cost.shape[0],), F32)
    for iteration in range(ITERS):
        potential_f = row_update(cost, potential_g, offset)
        potential_g = column_update(cost, potential_f, offset)
    own_f = lax.dynamic_slice_in_dim(potential_f, column * own_rows, own_rows)
    own_g = lax.dynamic_slice_in_dim(potential_g, row_place * own_rows, own_rows)
    all_g = lax.all_gather(potential_g, "col", axis=0, tiled=True)
    own_requests = lax.dynamic_slice_in_dim(pairing, column * own_rows, own_rows)
    return own_f, own_g, all_g[own_requests]


def dot_nt(a, b):
    return lax.dot_general(a, b, (((1,), (1,)), ((), ())), preferred_element_type=F32)


def dot_nn(a, b):
    return lax.dot_general(a, b, (((1,), (0,)), ((), ())), preferred_element_type=F32)


def three_parts(v):
    hi = v.astype(BF16)
    rest = v - hi.astype(F32)
    mid = rest.astype(BF16)
    low = (rest - mid.astype(F32)).astype(BF16)
    return hi, mid, low


def turn_to_lanes(v):
    n = v.shape[0]
    parts = [
        jnp.sum(jnp.transpose(v[q * 128 : (q + 1) * 128, :]), axis=0, keepdims=True)
        for q in range(n // 128)
    ]
    return parts[0] if len(parts) == 1 else jnp.concatenate(parts, axis=1)


def spread_rows(v):
    return jnp.transpose(jnp.broadcast_to(v, (128, 128)))


def kernel(
    n_row, n_col, features, total_rows,
    lat, noi, req, bucket,
    out_f, out_g, out_w, out_c, out_bad, out_i,
    x_buf, y_buf, e_buf, s_buf, norm_y, wide, pick, send_rows, got_rows,
    f_got, g_got, pg_got, peak, scale, rank,
    own_sem, x_send, x_recv, y_send, y_recv, f_send, f_recv, g_send, g_recv,
    p_send, p_recv, q_send, q_recv,
):
    rows = 256
    span = n_row * rows
    row = lax.axis_index("row")
    col = lax.axis_index("col")
    log2e = math.log2(math.e)
    unit = log2e / (features * entropic)

    def col_peer(k):
        return {"col": lax.rem(col + k, n_col)}

    def row_peer(k):
        return {"row": lax.rem(row + k, n_row)}

    barrier = pltpu.get_barrier_semaphore()

    def greet_col(k, _):
        pl.semaphore_signal(barrier, inc=1, device_id=col_peer(k), device_id_type=MESH)
        return 0

    def greet_row(k, _):
        pl.semaphore_signal(barrier, inc=1, device_id=row_peer(k), device_id_type=MESH)
        return 0

    lax.fori_loop(1, n_col, greet_col, 0)
    lax.fori_loop(1, n_row, greet_row, 0)
    own_x = pltpu.make_async_copy(lat, x_buf.at[col], own_sem.at[0])
    own_y = pltpu.make_async_copy(noi, y_buf.at[row], own_sem.at[1])
    own_x.start()
    own_y.start()
    pl.semaphore_wait(barrier, n_col + n_row - 2)

    z, x = col // 4, lax.rem(col, 4)
    y, core = row // 2, lax.rem(row, 2)

    def col_at(dz, dx):
        return lax.rem(z + (dz + 8), 4) * 4 + lax.rem(x + (dx + 8), 4)

    steps = {"x+": (0, 1), "x-": (0, -1), "z+": (1, 0), "z-": (-1, 0)}
    half = rows // 2
    quarter = rows // 4
    x_moves = {}
    for way in steps:
        first = way[1] == "+"
        back = -1 if first else 1
        if way[0] == "x":
            x_moves[way, "A"] = (0, 0, 0, half)
            x_moves[way, "fA"] = (0, back, 0 if first else quarter, quarter)
            x_moves[way, "B"] = (0, 0, half, half)
            for d in (-1, 1, 2):
                x_moves[way, "B", d] = (d, 0, half, half)
            for d in (0, -1, 1, 2):
                x_moves[way, "fB", d] = (d, back, half if first else half + quarter, quarter)
        else:
            x_moves[way, "B"] = (0, 0, half, half)
            x_moves[way, "fB"] = (back, 0, half if first else half + quarter, quarter)
            x_moves[way, "A"] = (0, 0, 0, half)
            for d in (-1, 1, 2):
                x_moves[way, "A", d] = (0, d, 0, half)
            for d in (0, -1, 1, 2):
                x_moves[way, "fA", d] = (back, d, 0 if first else quarter, quarter)
    x_index = {move: i for i, move in enumerate(x_moves)}

    def x_copy(move, arriving):
        way = steps[move[0]]
        dz, dx, start, count = x_moves[move]
        i = x_index[move]
        shift = way if arriving else (0, 0)
        place = x_buf.at[col_at(dz - shift[0], dx - shift[1]), pl.ds(start, count)]
        source = place
        if not arriving and (dz, dx) == (0, 0):
            source = lat.at[pl.ds(start, count)]
        return pltpu.make_async_remote_copy(
            src_ref=source, dst_ref=place, send_sem=x_send.at[i], recv_sem=x_recv.at[i],
            device_id={"col": col_at(*way)}, device_id_type=MESH,
        )

    def x_start(*moves):
        for move in moves:
            x_copy(move, False).start()

    def x_wait(*moves):
        for move in moves:
            x_copy(move, True).wait_recv()

    def row_at(dy, other):
        return lax.rem(y + (dy + 8), 4) * 2 + (1 - core if other else core)

    y_moves = {
        "+0": (1, 0, 0, half), "-1": (-1, 0, half, half),
        "+1": (1, 0, half, half), "-0": (-1, 0, 0, half),
        "+f": (1, -1, 0, half), "-f": (-1, 1, half, half),
        "s": (0, 0, 0, rows), "sm": (0, -1, 0, rows), "sp": (0, 1, 0, rows),
        "s0": (0, 2, 0, half), "s1": (0, 2, half, half),
    }
    y_index = {move: i for i, move in enumerate(y_moves)}

    def y_copy(move, arriving):
        way, dy, start, count = y_moves[move]
        i = y_index[move]
        place = y_buf.at[row_at(dy - (way if arriving else 0), arriving and way == 0), pl.ds(start, count)]
        source = place
        if not arriving and dy == 0:
            source = noi.at[pl.ds(start, count)]
        return pltpu.make_async_remote_copy(
            src_ref=source, dst_ref=place, send_sem=y_send.at[i], recv_sem=y_recv.at[i],
            device_id={"row": row_at(way, way == 0)}, device_id_type=MESH,
        )

    def y_start(*moves):
        for move in moves:
            y_copy(move, False).start()

    def y_wait(*moves):
        for move in moves:
            y_copy(move, True).wait_recv()

    def f_copy(it, k):
        return pltpu.make_async_remote_copy(
            src_ref=f_got.at[it, col], dst_ref=f_got.at[it, col],
            send_sem=f_send.at[it, k], recv_sem=f_recv.at[it, k],
            device_id=col_peer(k), device_id_type=MESH,
        )

    def g_copy(it, k):
        return pltpu.make_async_remote_copy(
            src_ref=g_got.at[it, row], dst_ref=g_got.at[it, row],
            send_sem=g_send.at[it, k], recv_sem=g_recv.at[it, k],
            device_id=row_peer(k), device_id_type=MESH,
        )

    def p_copy(k):
        return pltpu.make_async_remote_copy(
            src_ref=send_rows.at[lax.rem(col + k, n_col)], dst_ref=got_rows.at[col],
            send_sem=p_send.at[k], recv_sem=p_recv.at[k],
            device_id=col_peer(k), device_id_type=MESH,
        )

    def q_copy(k):
        return pltpu.make_async_remote_copy(
            src_ref=pg_got.at[n_col + lax.rem(col + k, n_col) // 4], dst_ref=pg_got.at[col],
            send_sem=q_send.at[k], recv_sem=q_recv.at[k],
            device_id=col_peer(k), device_id_type=MESH,
        )

    def each(n, act):
        for k in range(1, n):
            act(k)

    y_start("+0", "-1", "s")
    x_start(("x+", "A"), ("x-", "A"), ("z+", "B"), ("z-", "B"))
    y_start("+1", "-0")
    x_start(("x+", "B"), ("x-", "B"), ("z+", "A"), ("z-", "A"))

    requests = req[...]
    before = (
        lax.broadcasted_iota(jnp.int32, (rows, rows), 0)
        < lax.broadcasted_iota(jnp.int32, (rows, rows), 1)
    ).astype(F32).astype(BF16)
    wanted = ((requests // span) == col).astype(F32)
    place = dot_nn(wanted.astype(BF16), before)
    rank[0:n_col, :] = jnp.where(wanted > 0.0, place, -1.0)
    rank[n_col : 2 * n_col, :] = (requests - col * span + 1).astype(F32)

    slots = lax.broadcasted_iota(jnp.int32, (32, rows), 0).astype(F32)
    places = lax.broadcasted_iota(jnp.int32, (32, span), 1).astype(F32) + 1.0

    def choose(d, _):
        chosen = rank[pl.ds(d, 1), :] == slots
        index = jnp.sum(jnp.where(chosen, rank[pl.ds(n_col + d, 1), :], 0.0), axis=1, keepdims=True)
        pick[pl.ds(pl.multiple_of(d * 32, 32), 32), :] = (places == index).astype(F32).astype(BF16)
        return 0

    lax.fori_loop(0, n_col, choose, 0)

    own_x.wait()
    own_y.wait()
    y_wait("+0")
    y_start("+f")
    y_wait("-1")
    y_start("-f")
    x_wait(("x+", "A"))
    x_start(("x+", "fA"), ("z+", "A", -1), ("z-", "A", -1))
    x_wait(("x-", "A"))
    x_start(("x-", "fA"), ("z+", "A", 1), ("z-", "A", 1))
    x_wait(("z+", "B"))
    x_start(("z+", "fB"), ("x+", "B", -1), ("x-", "B", -1))
    x_wait(("z-", "B"))
    x_start(("z-", "fB"), ("x+", "B", 1), ("x-", "B", 1))
    y_wait("+1")
    y_start("sm")
    y_wait("-0")
    y_start("sp")
    for way in ("x+", "x-"):
        x_wait((way, "B"))
        x_start((way, "fB", 0))
    for way in ("z+", "z-"):
        x_wait((way, "A"))
        x_start((way, "fA", 0))
    x_wait(("x+", "fA"), ("x-", "fA"))
    x_start(("z+", "A", 2), ("z-", "A", 2))
    x_wait(("z+", "fB"), ("z-", "fB"))
    x_start(("x+", "B", 2), ("x-", "B", 2))
    y_wait("+f")
    y_start("s0")
    y_wait("-f")
    y_start("s1")
    y_wait("s", "sm", "sp", "s0", "s1")

    def norms(r, _):
        v = y_buf[r].astype(F32)
        n = jnp.sum(v * v, axis=1, keepdims=True) * unit
        norm_y[pl.ds(pl.multiple_of(r * rows, rows), rows), :] = jnp.broadcast_to(n, (rows, 128))
        return 0

    lax.fori_loop(0, n_row, norms, 0)

    def block(c):
        latent = x_buf[c]
        norm = norm_y[...]
        t = dot_nt(y_buf[...].reshape(span, features), latent) * (2.0 * unit)
        t = t - jnp.concatenate([norm, norm], axis=1)
        s_buf[...] = t
        top = jnp.max(jnp.max(t.reshape(span // 8, 8, rows), axis=0), axis=0, keepdims=True)
        peak[pl.ds(c, 1), :] = top

        def powers(r, total):
            at = pl.multiple_of(r * 512, 512)
            v = jnp.exp2(s_buf[pl.ds(at, 512), :] - top)
            e_buf[c, pl.ds(at, 512), :] = v
            return total + jnp.sum(v.reshape(64, 8, rows), axis=0)

        total = lax.fori_loop(0, span // 512, powers, jnp.zeros((8, rows), F32))
        f_got[0, col, pl.ds(c, 1), :] = top + jnp.log2(jnp.sum(total, axis=0, keepdims=True))

    near = (-1, 1)
    blocks = ((0, 0), (0, -1), (0, 1), (-1, 0), (1, 0), (-1, -1), (-1, 1), (1, -1), (1, 1),
              (0, 2), (2, 0), (-1, 2), (1, 2), (2, -1), (2, 1), (2, 2))

    def some_blocks(first, last):
        def step(k, _):
            dz = jnp.int32(0)
            dx = jnp.int32(0)
            for i in range(first, last):
                dz = jnp.where(k == i, blocks[i][0], dz)
                dx = jnp.where(k == i, blocks[i][1], dx)
            block(lax.rem(z + dz + 8, 4) * 4 + lax.rem(x + dx + 8, 4))
            return 0

        lax.fori_loop(first, last, step, 0)

    some_blocks(0, 4)
    for d in near:
        for way in ("x+", "x-"):
            x_wait((way, "B", d))
            x_start((way, "fB", d))
        for way in ("z+", "z-"):
            x_wait((way, "A", d))
            x_start((way, "fA", d))
    some_blocks(4, 8)
    for way in ("x+", "x-"):
        x_wait((way, "B", 2))
        x_start((way, "fB", 2))
    for way in ("z+", "z-"):
        x_wait((way, "A", 2))
        x_start((way, "fA", 2))
    some_blocks(8, 9)
    x_wait(("x+", "fB", 0), ("x-", "fB", 0), ("z+", "fA", 0), ("z-", "fA", 0))
    some_blocks(9, 11)
    for d in near:
        x_wait(("x+", "fB", d), ("x-", "fB", d), ("z+", "fA", d), ("z-", "fA", d))
    some_blocks(11, 15)
    x_wait(("x+", "fB", 2), ("x-", "fB", 2), ("z+", "fA", 2), ("z-", "fA", 2))
    some_blocks(15, 16)

    def in_range(v):
        return (v >= LOW) & (v <= HIGH)

    def column_pass(it):
        def body(q, _):
            at = pl.multiple_of(q * 256, 256)
            total = jnp.zeros((256, rows), F32)
            for c in range(n_col):
                total = total + e_buf[c, pl.ds(at, 256), :] * scale[c : c + 1, :]
            wide[pl.ds(at, 256), :] = total[:, :128] + total[:, 128:]
            return 0

        lax.fori_loop(0, span // 256, body, 0)
        for r in range(n_row):
            g_got[it, row, r : r + 1, :] = turn_to_lanes(wide[r * rows : (r + 1) * rows, :])

    def row_pass(it):
        def body(j, acc):
            at = pl.multiple_of(j * 128, 128)
            b = wide[pl.ds(at, 128), :]
            b = jnp.concatenate([b, b], axis=1)
            return tuple(
                acc[c] + jnp.sum((e_buf[c, pl.ds(at, 128), :] * b).reshape(16, 8, rows), axis=0)
                for c in range(n_col)
            )

        acc = lax.fori_loop(0, span // 128, body, tuple(jnp.zeros((8, rows), F32) for _ in range(n_col)))
        for c in range(n_col):
            f_got[it, col, c : c + 1, :] = jnp.sum(acc[c], axis=0, keepdims=True) * scale[n_col + c : n_col + c + 1, :]

    def summed(ref, it, n):
        total = ref[it, 0]
        for d in range(1, n):
            total = total + ref[it, d]
        return total

    def prepare():
        def fill(q, _):
            at = pl.multiple_of(q * 128, 128)
            total = jnp.zeros((128, features), F32)
            for r in range(n_row):
                total = total + dot_nn(pick[pl.ds(at, 128), r * rows : (r + 1) * rows], y_buf[r])
            send_rows[pl.ds(q * 4, 4)] = total.astype(BF16).reshape(4, 32, features)
            return 0

        lax.fori_loop(0, n_col // 4, fill, 0)
        got_rows[col] = send_rows[col]

    big_q = None
    for it in range(ITERS):
        if it > 0:
            row_pass(it)
        each(n_col, lambda k: f_copy(it, k).start())
        if it == 0:
            prepare()
        each(n_col, lambda k: f_copy(it, k).wait_recv())
        if it == 0:
            top = f_got[0, 0]
            for d in range(1, n_col):
                top = jnp.maximum(top, f_got[0, d])
            total = jnp.zeros_like(top)
            for d in range(n_col):
                total = total + jnp.exp2(f_got[0, d] - top)
            lse = top + jnp.log2(total)
            rank[0:n_col, :] = lse
            weight = jnp.exp2(peak[...] - lse)
            scale[n_col : 2 * n_col, :] = weight
            scale[0:n_col, :] = weight
        else:
            total = summed(f_got, it, n_col)
            a = jnp.where(in_range(total), 1.0 / total, jnp.nan)
            scale[0:n_col, :] = a * scale[n_col : 2 * n_col, :]
            if it == ITERS - 1:
                rank[n_col : 2 * n_col, :] = total
        column_pass(it)
        each(n_row, lambda k: g_copy(it, k).start())
        if it < ITERS - 1:
            for k in range(1 + 5 * it, 6 + 5 * it):
                p_copy(k).start()
        if it == ITERS - 1:
            each(n_col, lambda k: p_copy(k).wait_recv())
            mine = req[pl.ds(col, 1), :]
            anchor = mine // span
            marker = lax.broadcasted_iota(jnp.int32, (n_col, rows), 0) == anchor
            marked = marker.astype(F32)
            spot = jnp.sum(marked * dot_nn(marked.astype(BF16), before), axis=0, keepdims=True)
            flat = anchor.astype(F32) * 32.0 + spot
            tick = (bucket[...].astype(F32) + 0.5) / BUCKETS
            lanes = lax.broadcasted_iota(jnp.int32, (128, 32 * n_col), 1).astype(F32)
            costs = []
            squares = []
            for h in range(2):
                flat_h = spread_rows(flat[:, h * 128 : (h + 1) * 128])
                take = (lanes == flat_h[:, :1]).astype(F32).astype(BF16)
                paired = dot_nn(take, got_rows[...].reshape(32 * n_col, features))
                data = x_buf[col, h * 128 : (h + 1) * 128, :].astype(F32)
                t = spread_rows(tick[:, h * 128 : (h + 1) * 128])[:, :1]
                out_i[h * 128 : (h + 1) * 128, :] = ((1.0 - t) * data + t * paired).astype(BF16)
                diff = data - paired
                cost = diff * diff
                square = data * data
                fold_c = cost[:, :128]
                fold_s = square[:, :128]
                for q in range(1, features // 128):
                    fold_c = fold_c + cost[:, q * 128 : (q + 1) * 128]
                    fold_s = fold_s + square[:, q * 128 : (q + 1) * 128]
                costs.append(turn_to_lanes(fold_c))
                squares.append(turn_to_lanes(fold_s))
            pair_cost = jnp.concatenate(costs, axis=1) / features
            norm_x = jnp.concatenate(squares, axis=1) / features
        each(n_row, lambda k: g_copy(it, k).wait_recv())
        big_q = summed(g_got, it, n_row)
        if it < ITERS - 1:
            b = jnp.where(in_range(big_q), 1.0 / big_q, jnp.nan)
            for r in range(n_row):
                for h in range(2):
                    at = r * rows + h * 128
                    wide[at : at + 128, :] = spread_rows(b[r : r + 1, h * 128 : (h + 1) * 128])

    fine = jnp.min(jnp.where(in_range(big_q), 1.0, 0.0), axis=(0, 1), keepdims=True)
    g = jnp.where(fine > 0.0, -entropic * jnp.log(big_q), jnp.nan)
    chosen = [jnp.zeros((8, 32 * n_col), F32)]
    for part in three_parts(g):
        for r in range(n_row):
            one = jnp.broadcast_to(part[r : r + 1, :], (8, rows))
            chosen[0] = chosen[0] + dot_nt(one, pick[:, r * rows : (r + 1) * rows])
    for q in range(n_col // 4):
        pg_got[n_col + q] = chosen[0][:1, q * 128 : (q + 1) * 128]
    each(n_col, lambda k: q_copy(k).start())
    pg_got[col] = pg_got[n_col + col // 4]
    log_total = math.log(total_rows)
    lse = rank[pl.ds(col, 1), :]
    own_p = rank[pl.ds(n_col + col, 1), :]
    f = norm_x - entropic * (lse / log2e + jnp.log(own_p) + log_total)
    out_f[...] = f
    rank[0:n_row, :] = g
    out_g[...] = rank[pl.ds(row, 1), :]
    offset = lax.rem(col, 4) * 32
    grab = (
        lax.broadcasted_iota(jnp.int32, (128, rows), 0).astype(F32) == spot + offset.astype(F32)
    ).astype(F32).astype(BF16)
    each(n_col, lambda k: q_copy(k).wait_recv())
    arrived = jnp.concatenate([pg_got[d] for d in range(n_col)], axis=0)
    paired_g = jnp.zeros((n_col, rows), F32)
    for part in three_parts(arrived):
        paired_g = paired_g + dot_nn(part, grab)
    paired_g = jnp.sum(jnp.where(marker, paired_g, 0.0), axis=0, keepdims=True)
    out_c[...] = pair_cost
    out_w[...] = (f + paired_g - pair_cost) / entropic + log_total
    out_bad[...] = jnp.broadcast_to(
        jnp.max(jnp.where(arrived == arrived, 0.0, 1.0), axis=(0, 1), keepdims=True), (1, 128)
    )

    for move in y_moves:
        y_copy(move, False).wait_send()
    for move in x_moves:
        x_copy(move, False).wait_send()
    each(n_col, lambda k: p_copy(k).wait_send())
    each(n_col, lambda k: q_copy(k).wait_send())
    for it in range(ITERS):
        each(n_col, lambda k: f_copy(it, k).wait_send())
        each(n_row, lambda k: g_copy(it, k).wait_send())


def shards(latents, noise, pairing, time_bucket):
    own_rows, features = latents.shape
    n_row = lax.axis_size("row")
    n_col = lax.axis_size("col")
    total_rows = own_rows * n_row * n_col
    span = own_rows * n_row
    vmem = pl.BlockSpec(memory_space=pltpu.VMEM)
    hbm = pl.BlockSpec(memory_space=pl.ANY)
    line = jax.ShapeDtypeStruct((1, own_rows), F32)
    dma = pltpu.SemaphoreType.DMA
    f, g, w, pair_cost, bad, interpolant = pl.pallas_call(
        functools.partial(kernel, n_row, n_col, features, total_rows),
        out_shape=(
            line, line, line, line,
            jax.ShapeDtypeStruct((1, 128), F32),
            jax.ShapeDtypeStruct((own_rows, features), BF16),
        ),
        in_specs=[hbm, hbm, vmem, vmem],
        out_specs=(vmem,) * 6,
        scratch_shapes=[
            pltpu.VMEM((n_col, own_rows, features), BF16),
            pltpu.VMEM((n_row, own_rows, features), BF16),
            pltpu.VMEM((n_col, span, own_rows), F32),
            pltpu.VMEM((span, own_rows), F32),
            pltpu.VMEM((span, 128), F32),
            pltpu.VMEM((span, 128), F32),
            pltpu.VMEM((32 * n_col, span), BF16),
            pltpu.VMEM((n_col, 32, features), BF16),
            pltpu.VMEM((n_col, 32, features), BF16),
            pltpu.VMEM((ITERS, n_col, n_col, own_rows), F32),
            pltpu.VMEM((ITERS, n_row, n_row, own_rows), F32),
            pltpu.VMEM((n_col + n_col // 4, 1, 128), F32),
            pltpu.VMEM((n_col, own_rows), F32),
            pltpu.VMEM((2 * n_col, own_rows), F32),
            pltpu.VMEM((2 * n_col, own_rows), F32),
            dma((2,)),
            dma((40,)), dma((40,)),
            dma((11,)), dma((11,)),
            dma((ITERS, n_col)), dma((ITERS, n_col)),
            dma((ITERS, n_row)), dma((ITERS, n_row)),
            dma((n_col,)), dma((n_col,)),
            dma((n_col,)), dma((n_col,)),
        ],
        compiler_params=pltpu.CompilerParams(
            collective_id=0, has_side_effects=True, vmem_limit_bytes=62 * 1024 * 1024
        ),
        name="pairing_plan",
    )(latents, noise, pairing.reshape(n_col, own_rows), time_bucket.reshape(1, own_rows))
    f, g, w, pair_cost = (v.reshape(own_rows) for v in (f, g, w, pair_cost))

    def again():
        exact_f, exact_g, paired_g = log_domain(latents, noise, pairing)
        log_weight = (exact_f + paired_g - pair_cost) / entropic + math.log(total_rows)
        return exact_f, exact_g, log_weight

    f, g, w = lax.cond(bad[0, 0] > 0.0, again, lambda: (f, g, w))
    return f, g, interpolant, w


def solution(mesh):
    placed = (P(("row", "col"), None), P(("col", "row"), None), P("row"), P(("row", "col")))
    return jax.shard_map(
        shards,
        mesh=mesh,
        in_specs=placed,
        out_specs=(
            P(("row", "col")),
            P(("col", "row")),
            P(("row", "col"), None),
            P(("row", "col")),
        ),
        check_vma=False,
    )
```

```python
import functools
import math

import jax
import jax.numpy as jnp
from jax import lax
from jax.experimental import pallas as pl
from jax.experimental.pallas import tpu as pltpu
from jax.sharding import PartitionSpec as P

ITERS = 4
BUCKETS = 1000
MESH = pl.DeviceIdType.MESH
LOW = 2.0**-40
HIGH = 2.0**40
F32 = jnp.float32
BF16 = jnp.bfloat16

entropic = 0.1


def next_one(value, axis):
    count = lax.axis_size(axis)
    return lax.ppermute(value, axis, [(i, (i + 1) % count) for i in range(count)])


def over(value, axis, join):
    def step(_, carry):
        passing, total = carry
        passing = next_one(passing, axis)
        return passing, join(total, passing)

    return lax.fori_loop(1, lax.axis_size(axis), step, (value, value))[1]


def whole(value, axis):
    count = lax.axis_size(axis)
    size = value.shape[0]
    place = lax.axis_index(axis)

    def put(out, part, index):
        return lax.dynamic_update_slice_in_dim(out, part, index * size, 0)

    def step(k, carry):
        passing, out = carry
        passing = next_one(passing, axis)
        return passing, put(out, passing, lax.rem(place + count - k, count))

    out = put(jnp.zeros((count * size,) + value.shape[1:], value.dtype), value, place)
    return lax.fori_loop(1, count, step, (value, out))[1]


def row_update(cost, potential, offset):
    scores = (potential[None, :] - cost) / entropic
    peak = over(jnp.max(scores, axis=1), "col", jnp.maximum)
    running = over(jnp.sum(jnp.exp(scores - peak[:, None]), axis=1), "col", jnp.add)
    return -entropic * (peak + jnp.log(running)) - offset


def column_update(cost, potential, offset):
    scores = (potential[:, None] - cost) / entropic
    peak = over(jnp.max(scores, axis=0), "row", jnp.maximum)
    running = over(jnp.sum(jnp.exp(scores - peak[None, :]), axis=0), "row", jnp.add)
    return -entropic * (peak + jnp.log(running)) - offset


def log_domain(latents, noise, pairing):
    own_rows, features = latents.shape
    col_count = lax.axis_size("col")
    total_rows = own_rows * lax.axis_size("row") * col_count
    offset = entropic * math.log(total_rows)
    column = lax.axis_index("col")
    row_place = lax.axis_index("row")
    noise_rows = whole(noise, "row")
    noise_span = noise_rows.shape[0]
    noise_norms = jnp.sum(jnp.square(noise_rows.astype(F32)), axis=1)
    data_rows = whole(latents, "col")
    section_norms = jnp.sum(jnp.square(data_rows.astype(F32)), axis=1)
    products = lax.dot_general(
        data_rows, noise_rows, (((1,), (1,)), ((), ())), preferred_element_type=F32
    )
    cost = (section_norms[:, None] + noise_norms[None, :] - 2.0 * products) / features
    potential_g = jnp.zeros((noise_span,), F32)
    potential_f = jnp.zeros((cost.shape[0],), F32)
    def iterate(_, potentials):
        updated = row_update(cost, potentials[1], offset)
        return updated, column_update(cost, updated, offset)

    potential_f, potential_g = lax.fori_loop(0, ITERS, iterate, (potential_f, potential_g))
    own_f = lax.dynamic_slice_in_dim(potential_f, column * own_rows, own_rows)
    own_g = lax.dynamic_slice_in_dim(potential_g, row_place * own_rows, own_rows)
    all_g = whole(potential_g, "col")
    own_requests = lax.dynamic_slice_in_dim(pairing, column * own_rows, own_rows)
    return own_f, own_g, all_g[own_requests]


def dot_nt(a, b):
    return lax.dot_general(a, b, (((1,), (1,)), ((), ())), preferred_element_type=F32)


def dot_nn(a, b):
    return lax.dot_general(a, b, (((1,), (0,)), ((), ())), preferred_element_type=F32)


def three_parts(v):
    hi = v.astype(BF16)
    rest = v - hi.astype(F32)
    mid = rest.astype(BF16)
    low = (rest - mid.astype(F32)).astype(BF16)
    return hi, mid, low


def turn_to_lanes(v):
    n = v.shape[0]
    parts = [
        jnp.sum(jnp.transpose(v[q * 128 : (q + 1) * 128, :]), axis=0, keepdims=True)
        for q in range(n // 128)
    ]
    return parts[0] if len(parts) == 1 else jnp.concatenate(parts, axis=1)


def spread_rows(v):
    return jnp.transpose(jnp.broadcast_to(v, (128, 128)))


def kernel(
    n_row, n_col, features, total_rows,
    lat, noi, req, bucket,
    out_f, out_g, out_w, out_c, out_bad, out_i,
    x_buf, y_buf, e_buf, s_buf, norm_y, wide, pick, send_rows, got_rows,
    fx_got, fz_got, g_got, pg_got, peak, scale, rank, asked,
    own_sem, x_send, x_recv, y_send, y_recv, fx_send, fx_recv, fz_send, fz_recv, g_send, g_recv,
    p_send, p_recv, q_send, q_recv,
):
    rows = 256
    span = n_row * rows
    row = lax.axis_index("row")
    col = lax.axis_index("col")
    log2e = math.log2(math.e)
    unit = log2e / (features * entropic)

    def col_peer(k):
        return {"col": lax.rem(col + k, n_col)}

    def row_peer(k):
        return {"row": lax.rem(row + k, n_row)}

    barrier = pltpu.get_barrier_semaphore()

    def greet_col(k, _):
        pl.semaphore_signal(barrier, inc=1, device_id=col_peer(k), device_id_type=MESH)
        return 0

    def greet_row(k, _):
        pl.semaphore_signal(barrier, inc=1, device_id=row_peer(k), device_id_type=MESH)
        return 0

    lax.fori_loop(1, n_col, greet_col, 0)
    lax.fori_loop(1, n_row, greet_row, 0)
    own_x = pltpu.make_async_copy(lat, x_buf.at[col], own_sem.at[0])
    own_y = pltpu.make_async_copy(noi, y_buf.at[row], own_sem.at[1])
    own_x.start()
    own_y.start()
    pl.semaphore_wait(barrier, n_col + n_row - 2)

    z, x = col // 4, lax.rem(col, 4)
    y, core = row // 2, lax.rem(row, 2)

    def col_at(dz, dx):
        return lax.rem(z + (dz + 8), 4) * 4 + lax.rem(x + (dx + 8), 4)

    steps = {"x+": (0, 1), "x-": (0, -1), "z+": (1, 0), "z-": (-1, 0)}
    half = rows // 2
    quarter = rows // 4
    x_moves = {}
    for way in steps:
        first = way[1] == "+"
        back = -1 if first else 1
        if way[0] == "x":
            x_moves[way, "A"] = (0, 0, 0, half)
            x_moves[way, "fA"] = (0, back, 0 if first else quarter, quarter)
            x_moves[way, "B"] = (0, 0, half, half)
            for d in (-1, 1, 2):
                x_moves[way, "B", d] = (d, 0, half, half)
            for d in (0, -1, 1, 2):
                x_moves[way, "fB", d] = (d, back, half if first else half + quarter, quarter)
        else:
            x_moves[way, "B"] = (0, 0, half, half)
            x_moves[way, "fB"] = (back, 0, half if first else half + quarter, quarter)
            x_moves[way, "A"] = (0, 0, 0, half)
            for d in (-1, 1, 2):
                x_moves[way, "A", d] = (0, d, 0, half)
            for d in (0, -1, 1, 2):
                x_moves[way, "fA", d] = (back, d, 0 if first else quarter, quarter)
    x_index = {move: i for i, move in enumerate(x_moves)}

    def x_copy(move, arriving):
        way = steps[move[0]]
        dz, dx, start, count = x_moves[move]
        i = x_index[move]
        shift = way if arriving else (0, 0)
        place = x_buf.at[col_at(dz - shift[0], dx - shift[1]), pl.ds(start, count)]
        source = place
        if not arriving and (dz, dx) == (0, 0):
            source = lat.at[pl.ds(start, count)]
        return pltpu.make_async_remote_copy(
            src_ref=source, dst_ref=place, send_sem=x_send.at[i], recv_sem=x_recv.at[i],
            device_id={"col": col_at(*way)}, device_id_type=MESH,
        )

    def x_start(*moves):
        for move in moves:
            x_copy(move, False).start()

    def x_wait(*moves):
        for move in moves:
            x_copy(move, True).wait_recv()

    def row_at(dy, other):
        return lax.rem(y + (dy + 8), 4) * 2 + (1 - core if other else core)

    y_moves = {
        "+0": (1, 0, 0, half), "-1": (-1, 0, half, half),
        "+1": (1, 0, half, half), "-0": (-1, 0, 0, half),
        "+f": (1, -1, 0, half), "-f": (-1, 1, half, half),
        "s": (0, 0, 0, rows), "sm": (0, -1, 0, rows), "sp": (0, 1, 0, rows),
        "s0": (0, 2, 0, half), "s1": (0, 2, half, half),
    }
    y_index = {move: i for i, move in enumerate(y_moves)}

    def y_copy(move, arriving):
        way, dy, start, count = y_moves[move]
        i = y_index[move]
        place = y_buf.at[row_at(dy - (way if arriving else 0), arriving and way == 0), pl.ds(start, count)]
        source = place
        if not arriving and dy == 0:
            source = noi.at[pl.ds(start, count)]
        return pltpu.make_async_remote_copy(
            src_ref=source, dst_ref=place, send_sem=y_send.at[i], recv_sem=y_recv.at[i],
            device_id={"row": row_at(way, way == 0)}, device_id_type=MESH,
        )

    def y_start(*moves):
        for move in moves:
            y_copy(move, False).start()

    def y_wait(*moves):
        for move in moves:
            y_copy(move, True).wait_recv()

    def fx_copy(it, k):
        return pltpu.make_async_remote_copy(
            src_ref=fx_got.at[it, x], dst_ref=fx_got.at[it, x],
            send_sem=fx_send.at[it, k], recv_sem=fx_recv.at[it, k],
            device_id={"col": col_at(0, k)}, device_id_type=MESH,
        )

    def fz_copy(it, k):
        return pltpu.make_async_remote_copy(
            src_ref=fz_got.at[it, z], dst_ref=fz_got.at[it, z],
            send_sem=fz_send.at[it, k], recv_sem=fz_recv.at[it, k],
            device_id={"col": col_at(k, 0)}, device_id_type=MESH,
        )

    def g_copy(it, k):
        return pltpu.make_async_remote_copy(
            src_ref=g_got.at[it, row], dst_ref=g_got.at[it, row],
            send_sem=g_send.at[it, k], recv_sem=g_recv.at[it, k],
            device_id=row_peer(k), device_id_type=MESH,
        )

    def p_copy(k):
        return pltpu.make_async_remote_copy(
            src_ref=send_rows.at[lax.rem(col + k, n_col)], dst_ref=got_rows.at[col],
            send_sem=p_send.at[k], recv_sem=p_recv.at[k],
            device_id=col_peer(k), device_id_type=MESH,
        )

    def q_copy(k):
        return pltpu.make_async_remote_copy(
            src_ref=pg_got.at[n_col + lax.rem(col + k, n_col) // 4], dst_ref=pg_got.at[col],
            send_sem=q_send.at[k], recv_sem=q_recv.at[k],
            device_id=col_peer(k), device_id_type=MESH,
        )

    def each(n, act):
        for k in range(1, n):
            act(k)

    y_start("+0", "-1", "s")
    x_start(("x+", "A"), ("x-", "A"), ("z+", "B"), ("z-", "B"))
    y_start("+1", "-0")
    x_start(("x+", "B"), ("x-", "B"), ("z+", "A"), ("z-", "A"))

    for c in range(n_col):
        asked[c : c + 1, :] = jnp.concatenate([req[2 * c : 2 * c + 1, :], req[2 * c + 1 : 2 * c + 2, :]], axis=1)
    requests = asked[...]
    before = (
        lax.broadcasted_iota(jnp.int32, (rows, rows), 0)
        < lax.broadcasted_iota(jnp.int32, (rows, rows), 1)
    ).astype(F32).astype(BF16)
    wanted = ((requests // span) == col).astype(F32)
    place = dot_nn(wanted.astype(BF16), before)
    rank[0:n_col, :] = jnp.where(wanted > 0.0, place, -1.0)
    rank[n_col : 2 * n_col, :] = (requests - col * span + 1).astype(F32)

    slots = lax.broadcasted_iota(jnp.int32, (32, rows), 0).astype(F32)
    places = lax.broadcasted_iota(jnp.int32, (32, span), 1).astype(F32) + 1.0

    def choose(d, _):
        chosen = rank[pl.ds(d, 1), :] == slots
        index = jnp.sum(jnp.where(chosen, rank[pl.ds(n_col + d, 1), :], 0.0), axis=1, keepdims=True)
        pick[pl.ds(pl.multiple_of(d * 32, 32), 32), :] = (places == index).astype(F32).astype(BF16)
        return 0

    lax.fori_loop(0, n_col, choose, 0)

    own_x.wait()
    own_y.wait()
    y_wait("+0")
    y_start("+f")
    y_wait("-1")
    y_start("-f")
    x_wait(("x+", "A"))
    x_start(("x+", "fA"), ("z+", "A", -1), ("z-", "A", -1))
    x_wait(("x-", "A"))
    x_start(("x-", "fA"), ("z+", "A", 1), ("z-", "A", 1))
    x_wait(("z+", "B"))
    x_start(("z+", "fB"), ("x+", "B", -1), ("x-", "B", -1))
    x_wait(("z-", "B"))
    x_start(("z-", "fB"), ("x+", "B", 1), ("x-", "B", 1))
    y_wait("+1")
    y_start("sm")
    y_wait("-0")
    y_start("sp")
    for way in ("x+", "x-"):
        x_wait((way, "B"))
        x_start((way, "fB", 0))
    for way in ("z+", "z-"):
        x_wait((way, "A"))
        x_start((way, "fA", 0))
    x_wait(("x+", "fA"), ("x-", "fA"))
    x_start(("z+", "A", 2), ("z-", "A", 2))
    x_wait(("z+", "fB"), ("z-", "fB"))
    x_start(("x+", "B", 2), ("x-", "B", 2))
    y_wait("+f")
    y_start("s0")
    y_wait("-f")
    y_start("s1")
    y_wait("s", "sm", "sp", "s0", "s1")

    def norms(r, _):
        v = y_buf[r].astype(F32)
        n = jnp.sum(v * v, axis=1, keepdims=True) * unit
        norm_y[pl.ds(pl.multiple_of(r * rows, rows), rows), :] = jnp.broadcast_to(n, (rows, 128))
        return 0

    lax.fori_loop(0, n_row, norms, 0)

    def block(c):
        latent = x_buf[c]
        norm = norm_y[...]
        t = dot_nt(y_buf[...].reshape(span, features), latent) * (2.0 * unit)
        t = t - jnp.concatenate([norm, norm], axis=1)
        s_buf[...] = t
        top = jnp.max(jnp.max(t.reshape(span // 8, 8, rows), axis=0), axis=0, keepdims=True)
        peak[pl.ds(c, 1), :] = top

        def powers(r, total):
            at = pl.multiple_of(r * 512, 512)
            v = jnp.exp2(s_buf[pl.ds(at, 512), :] - top)
            e_buf[c, pl.ds(at, 512), :] = v
            return total + jnp.sum(v.reshape(64, 8, rows), axis=0)

        total = lax.fori_loop(0, span // 512, powers, jnp.zeros((8, rows), F32))
        fx_got[0, x, pl.ds(c, 1), :] = top + jnp.log2(jnp.sum(total, axis=0, keepdims=True))

    near = (-1, 1)
    blocks = ((0, 0), (0, -1), (0, 1), (-1, 0), (1, 0), (-1, -1), (-1, 1), (1, -1), (1, 1),
              (0, 2), (2, 0), (-1, 2), (1, 2), (2, -1), (2, 1), (2, 2))

    def some_blocks(first, last):
        def step(k, _):
            dz = jnp.int32(0)
            dx = jnp.int32(0)
            for i in range(first, last):
                dz = jnp.where(k == i, blocks[i][0], dz)
                dx = jnp.where(k == i, blocks[i][1], dx)
            block(lax.rem(z + dz + 8, 4) * 4 + lax.rem(x + dx + 8, 4))
            return 0

        lax.fori_loop(first, last, step, 0)

    some_blocks(0, 4)
    for d in near:
        for way in ("x+", "x-"):
            x_wait((way, "B", d))
            x_start((way, "fB", d))
        for way in ("z+", "z-"):
            x_wait((way, "A", d))
            x_start((way, "fA", d))
    some_blocks(4, 8)
    for way in ("x+", "x-"):
        x_wait((way, "B", 2))
        x_start((way, "fB", 2))
    for way in ("z+", "z-"):
        x_wait((way, "A", 2))
        x_start((way, "fA", 2))
    some_blocks(8, 9)
    x_wait(("x+", "fB", 0), ("x-", "fB", 0), ("z+", "fA", 0), ("z-", "fA", 0))
    some_blocks(9, 11)
    for d in near:
        x_wait(("x+", "fB", d), ("x-", "fB", d), ("z+", "fA", d), ("z-", "fA", d))
    some_blocks(11, 15)
    x_wait(("x+", "fB", 2), ("x-", "fB", 2), ("z+", "fA", 2), ("z-", "fA", 2))
    some_blocks(15, 16)

    def in_range(v):
        return (v >= LOW) & (v <= HIGH)

    def column_pass(it):
        def body(q, _):
            at = pl.multiple_of(q * 256, 256)
            total = jnp.zeros((256, rows), F32)
            for c in range(n_col):
                total = total + e_buf[c, pl.ds(at, 256), :] * scale[c : c + 1, :]
            wide[pl.ds(at, 256), :] = total[:, :128] + total[:, 128:]
            return 0

        lax.fori_loop(0, span // 256, body, 0)
        for r in range(n_row):
            g_got[it, row, r : r + 1, :] = turn_to_lanes(wide[r * rows : (r + 1) * rows, :])

    def row_pass(it):
        def body(j, acc):
            at = pl.multiple_of(j * 128, 128)
            b = wide[pl.ds(at, 128), :]
            b = jnp.concatenate([b, b], axis=1)
            return tuple(
                acc[c] + jnp.sum((e_buf[c, pl.ds(at, 128), :] * b).reshape(16, 8, rows), axis=0)
                for c in range(n_col)
            )

        acc = lax.fori_loop(0, span // 128, body, tuple(jnp.zeros((8, rows), F32) for _ in range(n_col)))
        for c in range(n_col):
            fx_got[it, x, c : c + 1, :] = jnp.sum(acc[c], axis=0, keepdims=True) * scale[n_col + c : n_col + c + 1, :]

    def log_sum(ref, it):
        top = jnp.maximum(jnp.maximum(ref[it, 0], ref[it, 1]), jnp.maximum(ref[it, 2], ref[it, 3]))
        total = jnp.exp2(ref[it, 0] - top)
        for d in range(1, 4):
            total = total + jnp.exp2(ref[it, d] - top)
        return top + jnp.log2(total)

    def summed(ref, it, n):
        total = ref[it, 0]
        for d in range(1, n):
            total = total + ref[it, d]
        return total

    def prepare():
        def fill(q, _):
            at = pl.multiple_of(q * 128, 128)
            total = jnp.zeros((128, features), F32)
            for r in range(n_row):
                total = total + dot_nn(pick[pl.ds(at, 128), r * rows : (r + 1) * rows], y_buf[r])
            send_rows[pl.ds(q * 4, 4)] = total.astype(BF16).reshape(4, 32, features)
            return 0

        lax.fori_loop(0, n_col // 4, fill, 0)
        got_rows[col] = send_rows[col]

    big_q = None
    for it in range(ITERS):
        if it > 0:
            row_pass(it)
        each(4, lambda k: fx_copy(it, k).start())
        if it == 0:
            prepare()
        each(4, lambda k: fx_copy(it, k).wait_recv())
        fz_got[it, z] = log_sum(fx_got, it) if it == 0 else summed(fx_got, it, 4)
        each(4, lambda k: fz_copy(it, k).start())
        each(4, lambda k: fz_copy(it, k).wait_recv())
        if it == 0:
            lse = log_sum(fz_got, it)
            rank[0:n_col, :] = lse
            weight = jnp.exp2(peak[...] - lse)
            scale[n_col : 2 * n_col, :] = weight
            scale[0:n_col, :] = weight
        else:
            total = summed(fz_got, it, 4)
            a = jnp.where(in_range(total), 1.0 / total, jnp.nan)
            scale[0:n_col, :] = a * scale[n_col : 2 * n_col, :]
            if it == ITERS - 1:
                rank[n_col : 2 * n_col, :] = total
        column_pass(it)
        each(n_row, lambda k: g_copy(it, k).start())
        if it < ITERS - 1:
            for k in range(1 + 5 * it, 6 + 5 * it):
                p_copy(k).start()
        if it == ITERS - 1:
            each(n_col, lambda k: p_copy(k).wait_recv())
            mine = asked[pl.ds(col, 1), :]
            anchor = mine // span
            marker = lax.broadcasted_iota(jnp.int32, (n_col, rows), 0) == anchor
            marked = marker.astype(F32)
            spot = jnp.sum(marked * dot_nn(marked.astype(BF16), before), axis=0, keepdims=True)
            flat = anchor.astype(F32) * 32.0 + spot
            tick = (bucket[...].astype(F32) + 0.5) / BUCKETS
            lanes = lax.broadcasted_iota(jnp.int32, (128, 32 * n_col), 1).astype(F32)
            costs = []
            squares = []
            for h in range(2):
                flat_h = spread_rows(flat[:, h * 128 : (h + 1) * 128])
                take = (lanes == flat_h[:, :1]).astype(F32).astype(BF16)
                paired = dot_nn(take, got_rows[...].reshape(32 * n_col, features))
                data = x_buf[col, h * 128 : (h + 1) * 128, :].astype(F32)
                t = spread_rows(tick[:, h * 128 : (h + 1) * 128])[:, :1]
                out_i[h * 128 : (h + 1) * 128, :] = ((1.0 - t) * data + t * paired).astype(BF16)
                diff = data - paired
                cost = diff * diff
                square = data * data
                fold_c = cost[:, :128]
                fold_s = square[:, :128]
                for q in range(1, features // 128):
                    fold_c = fold_c + cost[:, q * 128 : (q + 1) * 128]
                    fold_s = fold_s + square[:, q * 128 : (q + 1) * 128]
                costs.append(turn_to_lanes(fold_c))
                squares.append(turn_to_lanes(fold_s))
            pair_cost = jnp.concatenate(costs, axis=1) / features
            norm_x = jnp.concatenate(squares, axis=1) / features
        each(n_row, lambda k: g_copy(it, k).wait_recv())
        big_q = summed(g_got, it, n_row)
        if it < ITERS - 1:
            b = jnp.where(in_range(big_q), 1.0 / big_q, jnp.nan)
            for r in range(n_row):
                for h in range(2):
                    at = r * rows + h * 128
                    wide[at : at + 128, :] = spread_rows(b[r : r + 1, h * 128 : (h + 1) * 128])

    fine = jnp.min(jnp.where(in_range(big_q), 1.0, 0.0), axis=(0, 1), keepdims=True)
    g = jnp.where(fine > 0.0, jnp.log(big_q), jnp.nan)
    chosen = [jnp.zeros((8, 32 * n_col), F32)]
    for part in three_parts(g):
        for r in range(n_row):
            one = jnp.broadcast_to(part[r : r + 1, :], (8, rows))
            chosen[0] = chosen[0] + dot_nt(one, pick[:, r * rows : (r + 1) * rows])
    for q in range(n_col // 4):
        pg_got[n_col + q] = chosen[0][:1, q * 128 : (q + 1) * 128]
    each(n_col, lambda k: q_copy(k).start())
    pg_got[col] = pg_got[n_col + col // 4]
    log_total = math.log(total_rows)
    lse = rank[pl.ds(col, 1), :]
    own_p = rank[pl.ds(n_col + col, 1), :]
    f_scaled = lse / log2e + jnp.log(own_p) + log_total - norm_x / entropic
    out_f[...] = f_scaled
    rank[0:n_row, :] = g
    out_g[...] = rank[pl.ds(row, 1), :]
    offset = lax.rem(col, 4) * 32
    grab = (
        lax.broadcasted_iota(jnp.int32, (128, rows), 0).astype(F32) == spot + offset.astype(F32)
    ).astype(F32).astype(BF16)
    each(n_col, lambda k: q_copy(k).wait_recv())
    arrived = jnp.concatenate([pg_got[d] for d in range(n_col)], axis=0)
    paired_g = jnp.zeros((n_col, rows), F32)
    for part in three_parts(arrived):
        paired_g = paired_g + dot_nn(part, grab)
    paired_g = jnp.sum(jnp.where(marker, paired_g, 0.0), axis=0, keepdims=True)
    out_c[...] = pair_cost
    out_w[...] = f_scaled + paired_g + pair_cost / entropic - log_total
    out_bad[0, 0] = jnp.max(jnp.where(arrived == arrived, 0.0, 1.0)).astype(jnp.int32)

    for move in y_moves:
        y_copy(move, False).wait_send()
    for move in x_moves:
        x_copy(move, False).wait_send()
    each(n_col, lambda k: p_copy(k).wait_send())
    each(n_col, lambda k: q_copy(k).wait_send())
    for it in range(ITERS):
        each(4, lambda k: fx_copy(it, k).wait_send())
        each(4, lambda k: fz_copy(it, k).wait_send())
        each(n_row, lambda k: g_copy(it, k).wait_send())


def shards(latents, noise, pairing, time_bucket):
    own_rows, features = latents.shape
    n_row = lax.axis_size("row")
    n_col = lax.axis_size("col")
    total_rows = own_rows * n_row * n_col
    span = own_rows * n_row
    vmem = pl.BlockSpec(memory_space=pltpu.VMEM)
    hbm = pl.BlockSpec(memory_space=pl.ANY)
    line = jax.ShapeDtypeStruct((1, own_rows), F32)
    dma = pltpu.SemaphoreType.DMA
    f, g, w, pair_cost, bad, interpolant = pl.pallas_call(
        functools.partial(kernel, n_row, n_col, features, total_rows),
        out_shape=(
            line, line, line, line,
            jax.ShapeDtypeStruct((1, 1), jnp.int32),
            jax.ShapeDtypeStruct((own_rows, features), BF16),
        ),
        in_specs=[hbm, hbm, vmem, vmem],
        out_specs=(vmem,) * 4 + (pl.BlockSpec(memory_space=pltpu.SMEM), vmem),
        scratch_shapes=[
            pltpu.VMEM((n_col, own_rows, features), BF16),
            pltpu.VMEM((n_row, own_rows, features), BF16),
            pltpu.VMEM((n_col, span, own_rows), F32),
            pltpu.VMEM((span, own_rows), F32),
            pltpu.VMEM((span, 128), F32),
            pltpu.VMEM((span, 128), F32),
            pltpu.VMEM((32 * n_col, span), BF16),
            pltpu.VMEM((n_col, 32, features), BF16),
            pltpu.VMEM((n_col, 32, features), BF16),
            pltpu.VMEM((ITERS, 4, n_col, own_rows), F32),
            pltpu.VMEM((ITERS, 4, n_col, own_rows), F32),
            pltpu.VMEM((ITERS, n_row, n_row, own_rows), F32),
            pltpu.VMEM((n_col + n_col // 4, 1, 128), F32),
            pltpu.VMEM((n_col, own_rows), F32),
            pltpu.VMEM((2 * n_col, own_rows), F32),
            pltpu.VMEM((2 * n_col, own_rows), F32),
            pltpu.VMEM((n_col, own_rows), jnp.int32),
            dma((2,)),
            dma((40,)), dma((40,)),
            dma((11,)), dma((11,)),
            dma((ITERS, 4)), dma((ITERS, 4)),
            dma((ITERS, 4)), dma((ITERS, 4)),
            dma((ITERS, n_row)), dma((ITERS, n_row)),
            dma((n_col,)), dma((n_col,)),
            dma((n_col,)), dma((n_col,)),
        ],
        compiler_params=pltpu.CompilerParams(
            collective_id=0, has_side_effects=True, vmem_limit_bytes=62 * 1024 * 1024
        ),
        name="pairing_plan",
    )(latents, noise, pairing.reshape(2 * n_col, own_rows // 2), time_bucket.reshape(1, own_rows))
    def again():
        exact_f, exact_g, paired_g = log_domain(latents, noise, pairing)
        log_weight = (exact_f + paired_g - pair_cost.reshape(own_rows)) / entropic + math.log(total_rows)
        return tuple(v.reshape(1, own_rows) for v in (exact_f / -entropic, exact_g / -entropic, -log_weight))

    f, g, w = lax.cond(bad[0, 0] > 0, again, lambda: (f, g, w))
    f, g, w = (v.reshape(own_rows) for v in (f, g, w))
    return f * -entropic, g * -entropic, interpolant, -w


def solution(mesh):
    placed = (P(("row", "col"), None), P(("col", "row"), None), P("row"), P(("row", "col")))
    return jax.shard_map(
        shards,
        mesh=mesh,
        in_specs=placed,
        out_specs=(
            P(("row", "col")),
            P(("col", "row")),
            P(("row", "col"), None),
            P(("row", "col")),
        ),
        check_vma=False,
    )
```

```python
import functools
import math

import jax
import jax.numpy as jnp
from jax import lax
from jax.experimental import pallas as pl
from jax.experimental.pallas import tpu as pltpu
from jax.sharding import PartitionSpec as P

ITERS = 4
BUCKETS = 1000
MESH = pl.DeviceIdType.MESH
LOW = 2.0**-40
HIGH = 2.0**40
F32 = jnp.float32
BF16 = jnp.bfloat16

entropic = 0.1


def next_one(value, axis):
    count = lax.axis_size(axis)
    return lax.ppermute(value, axis, [(i, (i + 1) % count) for i in range(count)])


def over(value, axis, join):
    def step(_, carry):
        passing, total = carry
        passing = next_one(passing, axis)
        return passing, join(total, passing)

    passing = next_one(value, axis)
    return lax.fori_loop(2, lax.axis_size(axis), step, (passing, join(value, passing)))[1]


def whole(value, axis):
    count = lax.axis_size(axis)
    size = value.shape[0]
    place = lax.axis_index(axis)

    def put(out, part, index):
        return lax.dynamic_update_slice_in_dim(out, part, index * size, 0)

    def step(k, carry):
        passing, out = carry
        passing = next_one(passing, axis)
        return passing, put(out, passing, lax.rem(place + count - k, count))

    out = put(jnp.zeros((count * size,) + value.shape[1:], value.dtype), value, place)
    passing = next_one(value, axis)
    out = put(out, passing, lax.rem(place + count - 1, count))
    return lax.fori_loop(2, count, step, (passing, out))[1]


def row_update(cost, potential, offset):
    scores = (potential[None, :] - cost) / entropic
    peak = over(jnp.max(scores, axis=1), "col", jnp.maximum)
    running = over(jnp.sum(jnp.exp(scores - peak[:, None]), axis=1), "col", jnp.add)
    return -entropic * (peak + jnp.log(running)) - offset


def column_update(cost, potential, offset):
    scores = (potential[:, None] - cost) / entropic
    peak = over(jnp.max(scores, axis=0), "row", jnp.maximum)
    running = over(jnp.sum(jnp.exp(scores - peak[None, :]), axis=0), "row", jnp.add)
    return -entropic * (peak + jnp.log(running)) - offset


def log_domain(latents, noise, pairing):
    own_rows, features = latents.shape
    col_count = lax.axis_size("col")
    total_rows = own_rows * lax.axis_size("row") * col_count
    offset = entropic * math.log(total_rows)
    column = lax.axis_index("col")
    row_place = lax.axis_index("row")
    noise_rows = whole(noise, "row")
    noise_span = noise_rows.shape[0]
    noise_norms = jnp.sum(jnp.square(noise_rows.astype(F32)), axis=1)
    data_rows = whole(latents, "col")
    section_norms = jnp.sum(jnp.square(data_rows.astype(F32)), axis=1)
    products = lax.dot_general(
        data_rows, noise_rows, (((1,), (1,)), ((), ())), preferred_element_type=F32
    )
    cost = (section_norms[:, None] + noise_norms[None, :] - 2.0 * products) / features
    potential_g = jnp.zeros((noise_span,), F32)
    potential_f = jnp.zeros((cost.shape[0],), F32)
    def iterate(_, potentials):
        updated = row_update(cost, potentials[1], offset)
        return updated, column_update(cost, updated, offset)

    potential_f, potential_g = lax.fori_loop(0, ITERS, iterate, (potential_f, potential_g))
    own_f = lax.dynamic_slice_in_dim(potential_f, column * own_rows, own_rows)
    own_g = lax.dynamic_slice_in_dim(potential_g, row_place * own_rows, own_rows)
    all_g = whole(potential_g, "col")
    own_requests = lax.dynamic_slice_in_dim(pairing, column * own_rows, own_rows)
    return own_f, own_g, all_g[own_requests]


def dot_nt(a, b):
    return lax.dot_general(a, b, (((1,), (1,)), ((), ())), preferred_element_type=F32)


def dot_nn(a, b):
    return lax.dot_general(a, b, (((1,), (0,)), ((), ())), preferred_element_type=F32)


def three_parts(v):
    hi = v.astype(BF16)
    rest = v - hi.astype(F32)
    mid = rest.astype(BF16)
    low = (rest - mid.astype(F32)).astype(BF16)
    return hi, mid, low


def turn_to_lanes(v):
    n = v.shape[0]
    parts = [
        jnp.sum(jnp.transpose(v[q * 128 : (q + 1) * 128, :]), axis=0, keepdims=True)
        for q in range(n // 128)
    ]
    return parts[0] if len(parts) == 1 else jnp.concatenate(parts, axis=1)


def spread_rows(v):
    return jnp.transpose(jnp.broadcast_to(v, (128, 128)))


def kernel(
    n_row, n_col, features, total_rows,
    lat, noi, req, bucket,
    out_f, out_g, out_w, out_c, out_bad, out_i,
    x_buf, y_buf, e_buf, s_buf, norm_y, wide, pick, send_rows, got_rows,
    f_got, g_got, pg_got, peak, scale, rank, asked,
    own_sem, x_send, x_recv, y_send, y_recv, f_send, f_recv, g_send, g_recv,
    p_send, p_recv, q_send, q_recv,
):
    rows = 256
    span = n_row * rows
    row = lax.axis_index("row")
    col = lax.axis_index("col")
    log2e = math.log2(math.e)
    unit = log2e / (features * entropic)

    def col_peer(k):
        return {"col": lax.rem(col + k, n_col)}

    def row_peer(k):
        return {"row": lax.rem(row + k, n_row)}

    barrier = pltpu.get_barrier_semaphore()

    def greet_col(k, _):
        pl.semaphore_signal(barrier, inc=1, device_id=col_peer(k), device_id_type=MESH)
        return 0

    def greet_row(k, _):
        pl.semaphore_signal(barrier, inc=1, device_id=row_peer(k), device_id_type=MESH)
        return 0

    lax.fori_loop(1, n_col, greet_col, 0)
    lax.fori_loop(1, n_row, greet_row, 0)
    own_x = pltpu.make_async_copy(lat, x_buf.at[col], own_sem.at[0])
    own_y = pltpu.make_async_copy(noi, y_buf.at[row], own_sem.at[1])
    own_x.start()
    own_y.start()
    pl.semaphore_wait(barrier, n_col + n_row - 2)

    z, x = col // 4, lax.rem(col, 4)
    y, core = row // 2, lax.rem(row, 2)

    def col_at(dz, dx):
        return lax.rem(z + (dz + 8), 4) * 4 + lax.rem(x + (dx + 8), 4)

    steps = {"x+": (0, 1), "x-": (0, -1), "z+": (1, 0), "z-": (-1, 0)}
    half = rows // 2
    quarter = rows // 4
    x_moves = {}
    for way in steps:
        first = way[1] == "+"
        back = -1 if first else 1
        if way[0] == "x":
            x_moves[way, "A"] = (0, 0, 0, half)
            x_moves[way, "fA"] = (0, back, 0 if first else quarter, quarter)
            x_moves[way, "B"] = (0, 0, half, half)
            for d in (-1, 1, 2):
                x_moves[way, "B", d] = (d, 0, half, half)
            for d in (0, -1, 1, 2):
                x_moves[way, "fB", d] = (d, back, half if first else half + quarter, quarter)
        else:
            x_moves[way, "B"] = (0, 0, half, half)
            x_moves[way, "fB"] = (back, 0, half if first else half + quarter, quarter)
            x_moves[way, "A"] = (0, 0, 0, half)
            for d in (-1, 1, 2):
                x_moves[way, "A", d] = (0, d, 0, half)
            for d in (0, -1, 1, 2):
                x_moves[way, "fA", d] = (back, d, 0 if first else quarter, quarter)
    x_index = {move: i for i, move in enumerate(x_moves)}

    def x_copy(move, arriving):
        way = steps[move[0]]
        dz, dx, start, count = x_moves[move]
        i = x_index[move]
        shift = way if arriving else (0, 0)
        place = x_buf.at[col_at(dz - shift[0], dx - shift[1]), pl.ds(start, count)]
        source = place
        if not arriving and (dz, dx) == (0, 0):
            source = lat.at[pl.ds(start, count)]
        return pltpu.make_async_remote_copy(
            src_ref=source, dst_ref=place, send_sem=x_send.at[i], recv_sem=x_recv.at[i],
            device_id={"col": col_at(*way)}, device_id_type=MESH,
        )

    def x_start(*moves):
        for move in moves:
            x_copy(move, False).start()

    def x_wait(*moves):
        for move in moves:
            x_copy(move, True).wait_recv()

    def row_at(dy, other):
        return lax.rem(y + (dy + 8), 4) * 2 + (1 - core if other else core)

    y_moves = {
        "+0": (1, 0, 0, half), "-1": (-1, 0, half, half),
        "+1": (1, 0, half, half), "-0": (-1, 0, 0, half),
        "+f": (1, -1, 0, half), "-f": (-1, 1, half, half),
        "s": (0, 0, 0, rows), "sm": (0, -1, 0, rows), "sp": (0, 1, 0, rows),
        "s0": (0, 2, 0, half), "s1": (0, 2, half, half),
    }
    y_index = {move: i for i, move in enumerate(y_moves)}

    def y_copy(move, arriving):
        way, dy, start, count = y_moves[move]
        i = y_index[move]
        place = y_buf.at[row_at(dy - (way if arriving else 0), arriving and way == 0), pl.ds(start, count)]
        source = place
        if not arriving and dy == 0:
            source = noi.at[pl.ds(start, count)]
        return pltpu.make_async_remote_copy(
            src_ref=source, dst_ref=place, send_sem=y_send.at[i], recv_sem=y_recv.at[i],
            device_id={"row": row_at(way, way == 0)}, device_id_type=MESH,
        )

    def y_start(*moves):
        for move in moves:
            y_copy(move, False).start()

    def y_wait(*moves):
        for move in moves:
            y_copy(move, True).wait_recv()

    def f_copy(it, k):
        return pltpu.make_async_remote_copy(
            src_ref=f_got.at[it, col], dst_ref=f_got.at[it, col],
            send_sem=f_send.at[it, k], recv_sem=f_recv.at[it, k],
            device_id=col_peer(k), device_id_type=MESH,
        )

    def g_copy(it, k):
        return pltpu.make_async_remote_copy(
            src_ref=g_got.at[it, row], dst_ref=g_got.at[it, row],
            send_sem=g_send.at[it, k], recv_sem=g_recv.at[it, k],
            device_id=row_peer(k), device_id_type=MESH,
        )

    def p_copy(k):
        return pltpu.make_async_remote_copy(
            src_ref=send_rows.at[lax.rem(col + k, n_col)], dst_ref=got_rows.at[col],
            send_sem=p_send.at[k], recv_sem=p_recv.at[k],
            device_id=col_peer(k), device_id_type=MESH,
        )

    def q_copy(k):
        return pltpu.make_async_remote_copy(
            src_ref=pg_got.at[n_col + lax.rem(col + k, n_col) // 4], dst_ref=pg_got.at[col],
            send_sem=q_send.at[k], recv_sem=q_recv.at[k],
            device_id=col_peer(k), device_id_type=MESH,
        )

    def each(n, act):
        for k in range(1, n):
            act(k)

    y_start("+0", "-1", "s")
    x_start(("x+", "A"), ("x-", "A"), ("z+", "B"), ("z-", "B"))
    y_start("+1", "-0")
    x_start(("x+", "B"), ("x-", "B"), ("z+", "A"), ("z-", "A"))

    for c in range(n_col):
        asked[c : c + 1, :] = jnp.concatenate([req[2 * c : 2 * c + 1, :], req[2 * c + 1 : 2 * c + 2, :]], axis=1)
    requests = asked[...]
    before = (
        lax.broadcasted_iota(jnp.int32, (rows, rows), 0)
        < lax.broadcasted_iota(jnp.int32, (rows, rows), 1)
    ).astype(F32).astype(BF16)
    wanted = ((requests // span) == col).astype(F32)
    place = dot_nn(wanted.astype(BF16), before)
    rank[0:n_col, :] = jnp.where(wanted > 0.0, place, -1.0)
    rank[n_col : 2 * n_col, :] = (requests - col * span + 1).astype(F32)

    slots = lax.broadcasted_iota(jnp.int32, (32, rows), 0).astype(F32)
    places = lax.broadcasted_iota(jnp.int32, (32, span), 1).astype(F32) + 1.0

    def choose(d, _):
        chosen = rank[pl.ds(d, 1), :] == slots
        index = jnp.sum(jnp.where(chosen, rank[pl.ds(n_col + d, 1), :], 0.0), axis=1, keepdims=True)
        pick[pl.ds(pl.multiple_of(d * 32, 32), 32), :] = (places == index).astype(F32).astype(BF16)
        return 0

    lax.fori_loop(0, n_col, choose, 0)

    own_x.wait()
    own_y.wait()

    def norms(dy):
        at = pl.multiple_of(row_at(dy, False) // 2 * (2 * rows), 2 * rows)
        v = y_buf[pl.ds(row_at(dy, False) // 2 * 2, 2)].reshape(2 * rows, features).astype(F32)
        n = jnp.sum(v * v, axis=1, keepdims=True) * unit
        norm_y[pl.ds(at, 2 * rows), :] = jnp.broadcast_to(n, (2 * rows, 128))

    y_wait("+0")
    y_start("+f")
    y_wait("-1")
    y_start("-f")
    x_wait(("x+", "A"))
    x_start(("x+", "fA"), ("z+", "A", -1), ("z-", "A", -1))
    x_wait(("x-", "A"))
    x_start(("x-", "fA"), ("z+", "A", 1), ("z-", "A", 1))
    x_wait(("z+", "B"))
    x_start(("z+", "fB"), ("x+", "B", -1), ("x-", "B", -1))
    x_wait(("z-", "B"))
    x_start(("z-", "fB"), ("x+", "B", 1), ("x-", "B", 1))
    y_wait("+1")
    y_start("sm")
    y_wait("-0")
    y_start("sp")
    y_wait("s")
    norms(0)
    for way in ("x+", "x-"):
        x_wait((way, "B"))
        x_start((way, "fB", 0))
    for way in ("z+", "z-"):
        x_wait((way, "A"))
        x_start((way, "fA", 0))
    y_wait("sm", "sp")
    norms(-1)
    norms(1)

    def score(c, at, count):
        norm = norm_y[pl.ds(at, count), :]
        draws = y_buf[pl.ds(at // rows, count // rows)].reshape(count, features)
        t = dot_nt(draws, x_buf[c]) * (2.0 * unit)
        t = t - jnp.concatenate([norm, norm], axis=1)
        e_buf[c, pl.ds(at, count), :] = t
        return jnp.max(t.reshape(count // 8, 8, rows), axis=0)

    def powers(c, top):
        top = jnp.max(top, axis=0, keepdims=True)
        peak[pl.ds(c, 1), :] = top

        def part(r, total):
            at = pl.multiple_of(r * 512, 512)
            v = jnp.exp2(e_buf[c, pl.ds(at, 512), :] - top)
            e_buf[c, pl.ds(at, 512), :] = v
            return total + jnp.sum(v.reshape(64, 8, rows), axis=0)

        total = lax.fori_loop(0, span // 512, part, jnp.zeros((8, rows), F32))
        f_got[0, col, pl.ds(c, 1), :] = top + jnp.log2(jnp.sum(total, axis=0, keepdims=True))

    def pair_at(dy):
        return pl.multiple_of(row_at(dy, False) // 2 * (2 * rows), 2 * rows)

    def early(c, k):
        def part(d, top):
            at = pl.multiple_of(lax.rem(y + 3 + d, 4) * (2 * rows), 2 * rows)
            return jnp.maximum(top, score(c, at, 2 * rows))

        s_buf[k] = lax.fori_loop(0, 3, part, jnp.full((8, rows), -3.0e38, F32))

    def late(c, k):
        powers(c, jnp.maximum(s_buf[k], score(c, pair_at(2), 2 * rows)))

    def block(c, k):
        powers(c, score(c, 0, span))

    near = (-1, 1)
    blocks = ((0, 0), (0, -1), (0, 1), (-1, 0), (1, 0), (-1, -1), (-1, 1), (1, -1), (1, 1),
              (0, 2), (2, 0), (-1, 2), (2, -1), (1, 2), (2, 1), (2, 2))

    def some_blocks(act, first, last):
        def step(k, _):
            dz = jnp.int32(0)
            dx = jnp.int32(0)
            for i in range(first, last):
                dz = jnp.where(k == i, blocks[i][0], dz)
                dx = jnp.where(k == i, blocks[i][1], dx)
            act(lax.rem(z + dz + 8, 4) * 4 + lax.rem(x + dx + 8, 4), k)
            return 0

        lax.fori_loop(first, last, step, 0)

    some_blocks(early, 0, 2)
    y_wait("+f")
    y_start("s0")
    y_wait("-f")
    y_start("s1")
    some_blocks(early, 2, 5)
    y_wait("s0", "s1")
    norms(2)
    some_blocks(late, 0, 5)
    x_wait(("x+", "fA"), ("x-", "fA"))
    x_start(("z+", "A", 2), ("z-", "A", 2))
    x_wait(("z+", "fB"), ("z-", "fB"))
    x_start(("x+", "B", 2), ("x-", "B", 2))
    for d in near:
        for way in ("x+", "x-"):
            x_wait((way, "B", d))
            x_start((way, "fB", d))
        for way in ("z+", "z-"):
            x_wait((way, "A", d))
            x_start((way, "fA", d))
    some_blocks(block, 5, 9)
    x_wait(("x+", "fB", 0), ("x-", "fB", 0), ("z+", "fA", 0), ("z-", "fA", 0))
    some_blocks(block, 9, 11)
    for way in ("x+", "x-"):
        x_wait((way, "B", 2))
        x_start((way, "fB", 2))
    for way in ("z+", "z-"):
        x_wait((way, "A", 2))
        x_start((way, "fA", 2))
    x_wait(("x+", "fB", -1), ("x-", "fB", -1), ("z+", "fA", -1), ("z-", "fA", -1))
    some_blocks(block, 11, 13)
    x_wait(("x+", "fB", 1), ("x-", "fB", 1), ("z+", "fA", 1), ("z-", "fA", 1))
    some_blocks(block, 13, 15)
    x_wait(("x+", "fB", 2), ("x-", "fB", 2), ("z+", "fA", 2), ("z-", "fA", 2))
    some_blocks(block, 15, 16)

    def in_range(v):
        return (v >= LOW) & (v <= HIGH)

    def column_pass(it):
        def body(q, _):
            at = pl.multiple_of(q * 256, 256)
            total = jnp.zeros((256, rows), F32)
            for c in range(n_col):
                total = total + e_buf[c, pl.ds(at, 256), :] * scale[c : c + 1, :]
            wide[pl.ds(at, 256), :] = total[:, :128] + total[:, 128:]
            return 0

        lax.fori_loop(0, span // 256, body, 0)
        for r in range(n_row):
            g_got[it, row, r : r + 1, :] = turn_to_lanes(wide[r * rows : (r + 1) * rows, :])

    def row_pass(it):
        def body(j, acc):
            at = pl.multiple_of(j * 128, 128)
            b = wide[pl.ds(at, 128), :]
            b = jnp.concatenate([b, b], axis=1)
            return tuple(
                acc[c] + jnp.sum((e_buf[c, pl.ds(at, 128), :] * b).reshape(16, 8, rows), axis=0)
                for c in range(n_col)
            )

        acc = lax.fori_loop(0, span // 128, body, tuple(jnp.zeros((8, rows), F32) for _ in range(n_col)))
        for c in range(n_col):
            f_got[it, col, c : c + 1, :] = jnp.sum(acc[c], axis=0, keepdims=True) * scale[n_col + c : n_col + c + 1, :]

    def log_sum(ref, it):
        top = ref[it, 0]
        for d in range(1, n_col):
            top = jnp.maximum(top, ref[it, d])
        total = jnp.exp2(ref[it, 0] - top)
        for d in range(1, n_col):
            total = total + jnp.exp2(ref[it, d] - top)
        return top + jnp.log2(total)

    def summed(ref, it, n):
        total = ref[it, 0]
        for d in range(1, n):
            total = total + ref[it, d]
        return total

    def prepare():
        def fill(q, _):
            at = pl.multiple_of(q * 128, 128)
            total = jnp.zeros((128, features), F32)
            for r in range(n_row):
                total = total + dot_nn(pick[pl.ds(at, 128), r * rows : (r + 1) * rows], y_buf[r])
            send_rows[pl.ds(q * 4, 4)] = total.astype(BF16).reshape(4, 32, features)
            return 0

        lax.fori_loop(0, n_col // 4, fill, 0)
        got_rows[col] = send_rows[col]

    def unpack():
        each(n_col, lambda k: p_copy(k).wait_recv())
        mine = asked[pl.ds(col, 1), :]
        anchor = mine // span
        marker = lax.broadcasted_iota(jnp.int32, (n_col, rows), 0) == anchor
        marked = marker.astype(F32)
        spot = jnp.sum(marked * dot_nn(marked.astype(BF16), before), axis=0, keepdims=True)
        flat = anchor.astype(F32) * 32.0 + spot
        tick = (bucket[...].astype(F32) + 0.5) / BUCKETS
        lanes = lax.broadcasted_iota(jnp.int32, (128, 32 * n_col), 1).astype(F32)
        costs = []
        squares = []
        for h in range(2):
            flat_h = spread_rows(flat[:, h * 128 : (h + 1) * 128])
            take = (lanes == flat_h[:, :1]).astype(F32).astype(BF16)
            paired = dot_nn(take, got_rows[...].reshape(32 * n_col, features))
            data = x_buf[col, h * 128 : (h + 1) * 128, :].astype(F32)
            t = spread_rows(tick[:, h * 128 : (h + 1) * 128])[:, :1]
            out_i[h * 128 : (h + 1) * 128, :] = ((1.0 - t) * data + t * paired).astype(BF16)
            diff = data - paired
            cost = diff * diff
            square = data * data
            fold_c = cost[:, :128]
            fold_s = square[:, :128]
            for q in range(1, features // 128):
                fold_c = fold_c + cost[:, q * 128 : (q + 1) * 128]
                fold_s = fold_s + square[:, q * 128 : (q + 1) * 128]
            costs.append(turn_to_lanes(fold_c))
            squares.append(turn_to_lanes(fold_s))
        pair_cost = jnp.concatenate(costs, axis=1) / features
        norm_x = jnp.concatenate(squares, axis=1) / features
        return spot, marker, pair_cost, norm_x

    big_q = None
    for it in range(ITERS):
        if it > 0:
            row_pass(it)
        each(n_col, lambda k: f_copy(it, k).start())
        if it == 0:
            prepare()
        if it == ITERS - 1:
            spot, marker, pair_cost, norm_x = unpack()
        each(n_col, lambda k: f_copy(it, k).wait_recv())
        if it == 0:
            lse = log_sum(f_got, it)
            rank[0:n_col, :] = lse
            weight = jnp.exp2(peak[...] - lse)
            scale[n_col : 2 * n_col, :] = weight
            scale[0:n_col, :] = weight
        else:
            total = summed(f_got, it, n_col)
            a = jnp.where(in_range(total), 1.0 / total, jnp.nan)
            scale[0:n_col, :] = a * scale[n_col : 2 * n_col, :]
            if it == ITERS - 1:
                rank[n_col : 2 * n_col, :] = total
        column_pass(it)
        each(n_row, lambda k: g_copy(it, k).start())
        if it < ITERS - 1:
            for k in range(1 + 5 * it, 6 + 5 * it):
                p_copy(k).start()
        each(n_row, lambda k: g_copy(it, k).wait_recv())
        big_q = summed(g_got, it, n_row)
        if it < ITERS - 1:
            b = jnp.where(in_range(big_q), 1.0 / big_q, jnp.nan)
            for r in range(n_row):
                for h in range(2):
                    at = r * rows + h * 128
                    wide[at : at + 128, :] = spread_rows(b[r : r + 1, h * 128 : (h + 1) * 128])

    fine = jnp.min(jnp.where(in_range(big_q), 1.0, 0.0), axis=(0, 1), keepdims=True)
    g = jnp.where(fine > 0.0, jnp.log(big_q), jnp.nan)
    parts = three_parts(g)
    chosen = jnp.zeros((8, 32 * n_col), F32)
    for r in range(n_row):
        three = jnp.concatenate(
            [p[r : r + 1, :].astype(F32) for p in parts] + [jnp.zeros((5, rows), F32)], axis=0
        ).astype(BF16)
        chosen = chosen + dot_nt(three, pick[:, r * rows : (r + 1) * rows])
    chosen = jnp.sum(chosen, axis=0, keepdims=True)
    for q in range(n_col // 4):
        pg_got[n_col + q] = chosen[:, q * 128 : (q + 1) * 128]
    each(n_col, lambda k: q_copy(k).start())
    pg_got[col] = pg_got[n_col + col // 4]
    log_total = math.log(total_rows)
    lse = rank[pl.ds(col, 1), :]
    own_p = rank[pl.ds(n_col + col, 1), :]
    f_scaled = lse / log2e + jnp.log(own_p) + log_total - norm_x / entropic
    out_f[...] = f_scaled
    rank[0:n_row, :] = g
    out_g[...] = rank[pl.ds(row, 1), :]
    offset = lax.rem(col, 4) * 32
    grab = (
        lax.broadcasted_iota(jnp.int32, (128, rows), 0).astype(F32) == spot + offset.astype(F32)
    ).astype(F32).astype(BF16)
    each(n_col, lambda k: q_copy(k).wait_recv())
    arrived = jnp.concatenate([pg_got[d] for d in range(n_col)], axis=0)
    paired_g = jnp.zeros((n_col, rows), F32)
    for part in three_parts(arrived):
        paired_g = paired_g + dot_nn(part, grab)
    paired_g = jnp.sum(jnp.where(marker, paired_g, 0.0), axis=0, keepdims=True)
    out_c[...] = pair_cost
    out_w[...] = f_scaled + paired_g + pair_cost / entropic - log_total
    out_bad[0, 0] = jnp.max(jnp.where(arrived == arrived, 0.0, 1.0)).astype(jnp.int32)

    for move in y_moves:
        y_copy(move, False).wait_send()
    for move in x_moves:
        x_copy(move, False).wait_send()
    each(n_col, lambda k: p_copy(k).wait_send())
    each(n_col, lambda k: q_copy(k).wait_send())
    for it in range(ITERS):
        each(n_col, lambda k: f_copy(it, k).wait_send())
        each(n_row, lambda k: g_copy(it, k).wait_send())


def shards(latents, noise, pairing, time_bucket):
    own_rows, features = latents.shape
    n_row = lax.axis_size("row")
    n_col = lax.axis_size("col")
    total_rows = own_rows * n_row * n_col
    span = own_rows * n_row
    vmem = pl.BlockSpec(memory_space=pltpu.VMEM)
    hbm = pl.BlockSpec(memory_space=pl.ANY)
    line = jax.ShapeDtypeStruct((1, own_rows), F32)
    dma = pltpu.SemaphoreType.DMA
    f, g, w, pair_cost, bad, interpolant = pl.pallas_call(
        functools.partial(kernel, n_row, n_col, features, total_rows),
        out_shape=(
            line, line, line, line,
            jax.ShapeDtypeStruct((1, 1), jnp.int32),
            jax.ShapeDtypeStruct((own_rows, features), BF16),
        ),
        in_specs=[hbm, hbm, vmem, vmem],
        out_specs=(vmem,) * 4 + (pl.BlockSpec(memory_space=pltpu.SMEM), vmem),
        scratch_shapes=[
            pltpu.VMEM((n_col, own_rows, features), BF16),
            pltpu.VMEM((n_row, own_rows, features), BF16),
            pltpu.VMEM((n_col, span, own_rows), F32),
            pltpu.VMEM((8, 8, own_rows), F32),
            pltpu.VMEM((span, 128), F32),
            pltpu.VMEM((span, 128), F32),
            pltpu.VMEM((32 * n_col, span), BF16),
            pltpu.VMEM((n_col, 32, features), BF16),
            pltpu.VMEM((n_col, 32, features), BF16),
            pltpu.VMEM((ITERS, n_col, n_col, own_rows), F32),
            pltpu.VMEM((ITERS, n_row, n_row, own_rows), F32),
            pltpu.VMEM((n_col + n_col // 4, 1, 128), F32),
            pltpu.VMEM((n_col, own_rows), F32),
            pltpu.VMEM((2 * n_col, own_rows), F32),
            pltpu.VMEM((2 * n_col, own_rows), F32),
            pltpu.VMEM((n_col, own_rows), jnp.int32),
            dma((2,)),
            dma((40,)), dma((40,)),
            dma((11,)), dma((11,)),
            dma((ITERS, n_col)), dma((ITERS, n_col)),
            dma((ITERS, n_row)), dma((ITERS, n_row)),
            dma((n_col,)), dma((n_col,)),
            dma((n_col,)), dma((n_col,)),
        ],
        compiler_params=pltpu.CompilerParams(
            collective_id=0, has_side_effects=True, vmem_limit_bytes=62 * 1024 * 1024
        ),
        name="pairing_plan",
    )(latents, noise, pairing.reshape(2 * n_col, own_rows // 2), time_bucket.reshape(1, own_rows))
    def again():
        exact_f, exact_g, paired_g = log_domain(latents, noise, pairing)
        log_weight = (exact_f + paired_g - pair_cost.reshape(own_rows)) / entropic + math.log(total_rows)
        return tuple(v.reshape(1, own_rows) for v in (exact_f / -entropic, exact_g / -entropic, -log_weight))

    f, g, w = lax.cond(bad[0, 0] > 0, again, lambda: (f, g, w))
    f, g, w = (v.reshape(own_rows) for v in (f, g, w))
    return f * -entropic, g * -entropic, interpolant, -w


def solution(mesh):
    placed = (P(("row", "col"), None), P(("col", "row"), None), P("row"), P(("row", "col")))
    return jax.shard_map(
        shards,
        mesh=mesh,
        in_specs=placed,
        out_specs=(
            P(("row", "col")),
            P(("col", "row")),
            P(("row", "col"), None),
            P(("row", "col")),
        ),
        check_vma=False,
    )
```

```python
import functools
import math

import jax
import jax.numpy as jnp
from jax import lax
from jax.experimental import pallas as pl
from jax.experimental.pallas import tpu as pltpu
from jax.sharding import PartitionSpec as P

ITERS = 4
BUCKETS = 1000
MESH = pl.DeviceIdType.MESH
LOW = 2.0**-40
HIGH = 2.0**40
F32 = jnp.float32
BF16 = jnp.bfloat16

entropic = 0.1


def next_one(value, axis):
    count = lax.axis_size(axis)
    return lax.ppermute(value, axis, [(i, (i + 1) % count) for i in range(count)])


def over(value, axis, join):
    def step(_, carry):
        passing, total = carry
        passing = next_one(passing, axis)
        return passing, join(total, passing)

    passing = next_one(value, axis)
    return lax.fori_loop(2, lax.axis_size(axis), step, (passing, join(value, passing)))[1]


def whole(value, axis):
    count = lax.axis_size(axis)
    size = value.shape[0]
    place = lax.axis_index(axis)

    def put(out, part, index):
        return lax.dynamic_update_slice_in_dim(out, part, index * size, 0)

    def step(k, carry):
        passing, out = carry
        passing = next_one(passing, axis)
        return passing, put(out, passing, lax.rem(place + count - k, count))

    out = put(jnp.zeros((count * size,) + value.shape[1:], value.dtype), value, place)
    passing = next_one(value, axis)
    out = put(out, passing, lax.rem(place + count - 1, count))
    return lax.fori_loop(2, count, step, (passing, out))[1]


def row_update(cost, potential, offset):
    scores = (potential[None, :] - cost) / entropic
    peak = over(jnp.max(scores, axis=1), "col", jnp.maximum)
    running = over(jnp.sum(jnp.exp(scores - peak[:, None]), axis=1), "col", jnp.add)
    return -entropic * (peak + jnp.log(running)) - offset


def column_update(cost, potential, offset):
    scores = (potential[:, None] - cost) / entropic
    peak = over(jnp.max(scores, axis=0), "row", jnp.maximum)
    running = over(jnp.sum(jnp.exp(scores - peak[None, :]), axis=0), "row", jnp.add)
    return -entropic * (peak + jnp.log(running)) - offset


def log_domain(latents, noise, pairing):
    own_rows, features = latents.shape
    col_count = lax.axis_size("col")
    total_rows = own_rows * lax.axis_size("row") * col_count
    offset = entropic * math.log(total_rows)
    column = lax.axis_index("col")
    row_place = lax.axis_index("row")
    noise_rows = whole(noise, "row")
    noise_span = noise_rows.shape[0]
    noise_norms = jnp.sum(jnp.square(noise_rows.astype(F32)), axis=1)
    data_rows = whole(latents, "col")
    section_norms = jnp.sum(jnp.square(data_rows.astype(F32)), axis=1)
    products = lax.dot_general(
        data_rows, noise_rows, (((1,), (1,)), ((), ())), preferred_element_type=F32
    )
    cost = (section_norms[:, None] + noise_norms[None, :] - 2.0 * products) / features
    potential_g = jnp.zeros((noise_span,), F32)
    potential_f = jnp.zeros((cost.shape[0],), F32)
    def iterate(_, potentials):
        updated = row_update(cost, potentials[1], offset)
        return updated, column_update(cost, updated, offset)

    potential_f, potential_g = lax.fori_loop(0, ITERS, iterate, (potential_f, potential_g))
    own_f = lax.dynamic_slice_in_dim(potential_f, column * own_rows, own_rows)
    own_g = lax.dynamic_slice_in_dim(potential_g, row_place * own_rows, own_rows)
    all_g = whole(potential_g, "col")
    own_requests = lax.dynamic_slice_in_dim(pairing, column * own_rows, own_rows)
    return own_f, own_g, all_g[own_requests]


def dot_nt(a, b):
    return lax.dot_general(a, b, (((1,), (1,)), ((), ())), preferred_element_type=F32)


def dot_nn(a, b):
    return lax.dot_general(a, b, (((1,), (0,)), ((), ())), preferred_element_type=F32)


def three_parts(v):
    hi = v.astype(BF16)
    rest = v - hi.astype(F32)
    mid = rest.astype(BF16)
    low = (rest - mid.astype(F32)).astype(BF16)
    return hi, mid, low


def turn_to_lanes(v):
    n = v.shape[0]
    parts = [
        jnp.sum(jnp.transpose(v[q * 128 : (q + 1) * 128, :]), axis=0, keepdims=True)
        for q in range(n // 128)
    ]
    return parts[0] if len(parts) == 1 else jnp.concatenate(parts, axis=1)


def spread_rows(v):
    return jnp.transpose(jnp.broadcast_to(v, (128, 128)))


def kernel(
    n_row, n_col, features, total_rows,
    lat, noi, req, bucket,
    out_f, out_g, out_w, out_c, out_bad, out_i,
    x_buf, y_buf, e_buf, s_buf, norm_y, wide, pick, send_rows, got_rows,
    f_got, g_got, pg_got, peak, scale, rank, asked,
    own_sem, x_send, x_recv, y_send, y_recv, f_send, f_recv, g_send, g_recv,
    p_send, p_recv, q_send, q_recv,
):
    rows = 256
    span = n_row * rows
    f_half = n_col // 2
    g_half = n_row // 2
    row = lax.axis_index("row")
    col = lax.axis_index("col")
    log2e = math.log2(math.e)
    unit = log2e / (features * entropic)

    def col_peer(k):
        return {"col": lax.rem(col + k, n_col)}

    def row_peer(k):
        return {"row": lax.rem(row + k, n_row)}

    barrier = pltpu.get_barrier_semaphore()

    def greet_col(k, _):
        pl.semaphore_signal(barrier, inc=1, device_id=col_peer(k), device_id_type=MESH)
        return 0

    def greet_row(k, _):
        pl.semaphore_signal(barrier, inc=1, device_id=row_peer(k), device_id_type=MESH)
        return 0

    lax.fori_loop(1, n_col, greet_col, 0)
    lax.fori_loop(1, n_row, greet_row, 0)
    own_x = pltpu.make_async_copy(lat, x_buf.at[col], own_sem.at[0])
    own_y = pltpu.make_async_copy(noi, y_buf.at[row], own_sem.at[1])
    own_x.start()
    own_y.start()
    pl.semaphore_wait(barrier, n_col + n_row - 2)

    z, x = col // 4, lax.rem(col, 4)
    y, core = row // 2, lax.rem(row, 2)

    def col_at(dz, dx):
        return lax.rem(z + (dz + 8), 4) * 4 + lax.rem(x + (dx + 8), 4)

    steps = {"x+": (0, 1), "x-": (0, -1), "z+": (1, 0), "z-": (-1, 0)}
    half = rows // 2
    quarter = rows // 4
    x_moves = {}
    for way in steps:
        first = way[1] == "+"
        back = -1 if first else 1
        if way[0] == "x":
            x_moves[way, "A"] = (0, 0, 0, half)
            x_moves[way, "fA"] = (0, back, 0 if first else quarter, quarter)
            x_moves[way, "B"] = (0, 0, half, half)
            for d in (-1, 1, 2):
                x_moves[way, "B", d] = (d, 0, half, half)
            for d in (0, -1, 1, 2):
                x_moves[way, "fB", d] = (d, back, half if first else half + quarter, quarter)
        else:
            x_moves[way, "B"] = (0, 0, half, half)
            x_moves[way, "fB"] = (back, 0, half if first else half + quarter, quarter)
            x_moves[way, "A"] = (0, 0, 0, half)
            for d in (-1, 1, 2):
                x_moves[way, "A", d] = (0, d, 0, half)
            for d in (0, -1, 1, 2):
                x_moves[way, "fA", d] = (back, d, 0 if first else quarter, quarter)
    x_index = {move: i for i, move in enumerate(x_moves)}

    def x_copy(move, arriving):
        way = steps[move[0]]
        dz, dx, start, count = x_moves[move]
        i = x_index[move]
        shift = way if arriving else (0, 0)
        place = x_buf.at[col_at(dz - shift[0], dx - shift[1]), pl.ds(start, count)]
        source = place
        if not arriving and (dz, dx) == (0, 0):
            source = lat.at[pl.ds(start, count)]
        return pltpu.make_async_remote_copy(
            src_ref=source, dst_ref=place, send_sem=x_send.at[i], recv_sem=x_recv.at[i],
            device_id={"col": col_at(*way)}, device_id_type=MESH,
        )

    def x_start(*moves):
        for move in moves:
            x_copy(move, False).start()

    def x_wait(*moves):
        for move in moves:
            x_copy(move, True).wait_recv()

    def row_at(dy, other):
        return lax.rem(y + (dy + 8), 4) * 2 + (1 - core if other else core)

    y_moves = {
        "+0": (1, 0, 0, half), "-1": (-1, 0, half, half),
        "+1": (1, 0, half, half), "-0": (-1, 0, 0, half),
        "+f": (1, -1, 0, half), "-f": (-1, 1, half, half),
        "s": (0, 0, 0, rows), "sm": (0, -1, 0, rows), "sp": (0, 1, 0, rows),
        "s0": (0, 2, 0, half), "s1": (0, 2, half, half),
    }
    y_index = {move: i for i, move in enumerate(y_moves)}

    def y_copy(move, arriving):
        way, dy, start, count = y_moves[move]
        i = y_index[move]
        place = y_buf.at[row_at(dy - (way if arriving else 0), arriving and way == 0), pl.ds(start, count)]
        source = place
        if not arriving and dy == 0:
            source = noi.at[pl.ds(start, count)]
        return pltpu.make_async_remote_copy(
            src_ref=source, dst_ref=place, send_sem=y_send.at[i], recv_sem=y_recv.at[i],
            device_id={"row": row_at(way, way == 0)}, device_id_type=MESH,
        )

    def y_start(*moves):
        for move in moves:
            y_copy(move, False).start()

    def y_wait(*moves):
        for move in moves:
            y_copy(move, True).wait_recv()

    def f_copy(it, k, h):
        place = f_got.at[it, col, pl.ds(h * f_half, f_half)]
        return pltpu.make_async_remote_copy(
            src_ref=place, dst_ref=place,
            send_sem=f_send.at[it, 2 * k + h], recv_sem=f_recv.at[it, 2 * k + h],
            device_id=col_peer(k), device_id_type=MESH,
        )

    def g_copy(it, k, h):
        place = g_got.at[it, h, row]
        return pltpu.make_async_remote_copy(
            src_ref=place, dst_ref=place,
            send_sem=g_send.at[it, 2 * k + h], recv_sem=g_recv.at[it, 2 * k + h],
            device_id=row_peer(k), device_id_type=MESH,
        )

    def p_copy(k):
        return pltpu.make_async_remote_copy(
            src_ref=send_rows.at[lax.rem(col + k, n_col)], dst_ref=got_rows.at[col],
            send_sem=p_send.at[k], recv_sem=p_recv.at[k],
            device_id=col_peer(k), device_id_type=MESH,
        )

    def q_copy(k):
        return pltpu.make_async_remote_copy(
            src_ref=pg_got.at[n_col + lax.rem(col + k, n_col) // 4], dst_ref=pg_got.at[col],
            send_sem=q_send.at[k], recv_sem=q_recv.at[k],
            device_id=col_peer(k), device_id_type=MESH,
        )

    def each(n, act):
        for k in range(1, n):
            act(k)

    y_start("+0", "-1", "s")
    x_start(("x+", "A"), ("x-", "A"), ("z+", "B"), ("z-", "B"))
    y_start("+1", "-0")
    x_start(("x+", "B"), ("x-", "B"), ("z+", "A"), ("z-", "A"))

    for c in range(n_col):
        asked[c : c + 1, :] = jnp.concatenate([req[2 * c : 2 * c + 1, :], req[2 * c + 1 : 2 * c + 2, :]], axis=1)
    requests = asked[...]
    before = (
        lax.broadcasted_iota(jnp.int32, (rows, rows), 0)
        < lax.broadcasted_iota(jnp.int32, (rows, rows), 1)
    ).astype(F32).astype(BF16)
    wanted = ((requests // span) == col).astype(F32)
    place = dot_nn(wanted.astype(BF16), before)
    rank[0:n_col, :] = jnp.where(wanted > 0.0, place, -1.0)
    rank[n_col : 2 * n_col, :] = (requests - col * span + 1).astype(F32)

    slots = lax.broadcasted_iota(jnp.int32, (32, rows), 0).astype(F32)
    places = lax.broadcasted_iota(jnp.int32, (32, span), 1).astype(F32) + 1.0

    def choose(d, _):
        chosen = rank[pl.ds(d, 1), :] == slots
        index = jnp.sum(jnp.where(chosen, rank[pl.ds(n_col + d, 1), :], 0.0), axis=1, keepdims=True)
        pick[pl.ds(pl.multiple_of(d * 32, 32), 32), :] = (places == index).astype(F32).astype(BF16)
        return 0

    lax.fori_loop(0, n_col, choose, 0)

    own_x.wait()
    own_y.wait()

    def norms(dy):
        at = pl.multiple_of(row_at(dy, False) // 2 * (2 * rows), 2 * rows)
        v = y_buf[pl.ds(row_at(dy, False) // 2 * 2, 2)].reshape(2 * rows, features).astype(F32)
        n = jnp.sum(v * v, axis=1, keepdims=True) * unit
        norm_y[pl.ds(at, 2 * rows), :] = jnp.broadcast_to(n, (2 * rows, 128))

    y_wait("+0")
    y_start("+f")
    y_wait("-1")
    y_start("-f")
    x_wait(("x+", "A"))
    x_start(("x+", "fA"), ("z+", "A", -1), ("z-", "A", -1))
    x_wait(("x-", "A"))
    x_start(("x-", "fA"), ("z+", "A", 1), ("z-", "A", 1))
    x_wait(("z+", "B"))
    x_start(("z+", "fB"), ("x+", "B", -1), ("x-", "B", -1))
    x_wait(("z-", "B"))
    x_start(("z-", "fB"), ("x+", "B", 1), ("x-", "B", 1))
    y_wait("+1")
    y_start("sm")
    y_wait("-0")
    y_start("sp")
    y_wait("s")
    norms(0)
    for way in ("x+", "x-"):
        x_wait((way, "B"))
        x_start((way, "fB", 0))
    for way in ("z+", "z-"):
        x_wait((way, "A"))
        x_start((way, "fA", 0))
    y_wait("sm", "sp")
    norms(-1)
    norms(1)

    def score(c, at, count):
        norm = norm_y[pl.ds(at, count), :]
        draws = y_buf[pl.ds(at // rows, count // rows)].reshape(count, features)
        t = dot_nt(draws, x_buf[c]) * (2.0 * unit)
        t = t - jnp.concatenate([norm, norm], axis=1)
        e_buf[c, pl.ds(at, count), :] = t
        return jnp.max(t.reshape(count // 8, 8, rows), axis=0)

    def powers(c, top):
        top = jnp.max(top, axis=0, keepdims=True)
        peak[pl.ds(c, 1), :] = top

        def part(r, total):
            at = pl.multiple_of(r * 512, 512)
            v = jnp.exp2(e_buf[c, pl.ds(at, 512), :] - top)
            e_buf[c, pl.ds(at, 512), :] = v
            return total + jnp.sum(v.reshape(64, 8, rows), axis=0)

        total = lax.fori_loop(0, span // 512, part, jnp.zeros((8, rows), F32))
        f_got[0, col, pl.ds(c, 1), :] = top + jnp.log2(jnp.sum(total, axis=0, keepdims=True))

    def pair_at(dy):
        return pl.multiple_of(row_at(dy, False) // 2 * (2 * rows), 2 * rows)

    def early(c, k):
        def part(d, top):
            at = pl.multiple_of(lax.rem(y + 3 + d, 4) * (2 * rows), 2 * rows)
            return jnp.maximum(top, score(c, at, 2 * rows))

        s_buf[k] = lax.fori_loop(0, 3, part, jnp.full((8, rows), -3.0e38, F32))

    def late(c, k):
        powers(c, jnp.maximum(s_buf[k], score(c, pair_at(2), 2 * rows)))

    def block(c, k):
        powers(c, score(c, 0, span))

    near = (-1, 1)
    blocks = ((0, 0), (0, -1), (0, 1), (-1, 0), (1, 0), (-1, -1), (-1, 1), (1, -1), (1, 1),
              (0, 2), (2, 0), (-1, 2), (2, -1), (1, 2), (2, 1), (2, 2))

    def some_blocks(act, first, last):
        def step(k, _):
            dz = jnp.int32(0)
            dx = jnp.int32(0)
            for i in range(first, last):
                dz = jnp.where(k == i, blocks[i][0], dz)
                dx = jnp.where(k == i, blocks[i][1], dx)
            act(lax.rem(z + dz + 8, 4) * 4 + lax.rem(x + dx + 8, 4), k)
            return 0

        lax.fori_loop(first, last, step, 0)

    some_blocks(early, 0, 2)
    y_wait("+f")
    y_start("s0")
    y_wait("-f")
    y_start("s1")
    some_blocks(early, 2, 5)
    y_wait("s0", "s1")
    norms(2)
    some_blocks(late, 0, 5)
    x_wait(("x+", "fA"), ("x-", "fA"))
    x_start(("z+", "A", 2), ("z-", "A", 2))
    x_wait(("z+", "fB"), ("z-", "fB"))
    x_start(("x+", "B", 2), ("x-", "B", 2))
    for d in near:
        for way in ("x+", "x-"):
            x_wait((way, "B", d))
            x_start((way, "fB", d))
        for way in ("z+", "z-"):
            x_wait((way, "A", d))
            x_start((way, "fA", d))
    some_blocks(block, 5, 9)
    x_wait(("x+", "fB", 0), ("x-", "fB", 0), ("z+", "fA", 0), ("z-", "fA", 0))
    some_blocks(block, 9, 11)
    for way in ("x+", "x-"):
        x_wait((way, "B", 2))
        x_start((way, "fB", 2))
    for way in ("z+", "z-"):
        x_wait((way, "A", 2))
        x_start((way, "fA", 2))
    x_wait(("x+", "fB", -1), ("x-", "fB", -1), ("z+", "fA", -1), ("z-", "fA", -1))
    some_blocks(block, 11, 13)
    x_wait(("x+", "fB", 1), ("x-", "fB", 1), ("z+", "fA", 1), ("z-", "fA", 1))
    some_blocks(block, 13, 15)
    x_wait(("x+", "fB", 2), ("x-", "fB", 2), ("z+", "fA", 2), ("z-", "fA", 2))
    some_blocks(block, 15, 16)

    def in_range(v):
        return (v >= LOW) & (v <= HIGH)

    def column_sums(first, last, start, count):
        def body(q, _):
            at = pl.multiple_of(start + q * 256, 256)
            total = jnp.zeros((256, rows), F32)
            for c in range(first, last):
                total = total + e_buf[c, pl.ds(at, 256), :] * scale[c : c + 1, :]
            total = total[:, :128] + total[:, 128:]
            if first > 0:
                total = total + wide[pl.ds(at, 256), :]
            wide[pl.ds(at, 256), :] = total
            return 0

        lax.fori_loop(0, count // 256, body, 0)

    def row_sums(first, last, start, count, acc):
        def body(j, acc):
            at = pl.multiple_of(start + j * 128, 128)
            b = wide[pl.ds(at, 128), :]
            b = jnp.concatenate([b, b], axis=1)
            return tuple(
                acc[c - first] + jnp.sum((e_buf[c, pl.ds(at, 128), :] * b).reshape(16, 8, rows), axis=0)
                for c in range(first, last)
            )

        return lax.fori_loop(0, count // 128, body, acc)

    def log_sum(parts):
        top = parts[0]
        for part in parts[1:]:
            top = jnp.maximum(top, part)
        total = jnp.exp2(parts[0] - top)
        for part in parts[1:]:
            total = total + jnp.exp2(part - top)
        return top + jnp.log2(total)

    def summed(parts):
        total = parts[0]
        for part in parts[1:]:
            total = total + part
        return total

    def f_arrived(it, h):
        each(n_col, lambda k: f_copy(it, k, h).wait_recv())
        lo, hi = h * f_half, (h + 1) * f_half
        parts = [f_got[it, d, lo:hi] for d in range(n_col)]
        if it == 0:
            lse = log_sum(parts)
            rank[lo:hi, :] = lse
            weight = jnp.exp2(peak[lo:hi, :] - lse)
            scale[n_col + lo : n_col + hi, :] = weight
            scale[lo:hi, :] = weight
        else:
            total = summed(parts)
            a = jnp.where(in_range(total), 1.0 / total, jnp.nan)
            scale[lo:hi, :] = a * scale[n_col + lo : n_col + hi, :]
            if it == ITERS - 1:
                rank[n_col + lo : n_col + hi, :] = total

    def g_arrived(it, h):
        each(n_row, lambda k: g_copy(it, k, h).wait_recv())
        return summed([g_got[it, h, d] for d in range(n_row)])

    def g_spread(it, h):
        total = g_arrived(it, h)
        b = jnp.where(in_range(total), 1.0 / total, jnp.nan)
        for r in range(g_half):
            for q in range(2):
                at = (h * g_half + r) * rows + q * 128
                wide[at : at + 128, :] = spread_rows(b[r : r + 1, q * 128 : (q + 1) * 128])

    def f_leave(it, h, acc):
        for i in range(f_half):
            c = h * f_half + i
            f_got[it, col, c : c + 1, :] = (
                jnp.sum(acc[i], axis=0, keepdims=True) * scale[n_col + c : n_col + c + 1, :]
            )
        each(n_col, lambda k: f_copy(it, k, h).start())

    def g_leave(it, h):
        for i in range(g_half):
            at = (h * g_half + i) * rows
            g_got[it, h, row, i : i + 1, :] = turn_to_lanes(wide[at : at + rows, :])
        each(n_row, lambda k: g_copy(it, k, h).start())

    def prepare():
        def fill(q, _):
            at = pl.multiple_of(q * 128, 128)
            total = jnp.zeros((128, features), F32)
            for r in range(n_row):
                total = total + dot_nn(pick[pl.ds(at, 128), r * rows : (r + 1) * rows], y_buf[r])
            send_rows[pl.ds(q * 4, 4)] = total.astype(BF16).reshape(4, 32, features)
            return 0

        lax.fori_loop(0, n_col // 4, fill, 0)
        got_rows[col] = send_rows[col]

    def own_slots():
        mine = asked[pl.ds(col, 1), :]
        anchor = mine // span
        marker = lax.broadcasted_iota(jnp.int32, (n_col, rows), 0) == anchor
        marked = marker.astype(F32)
        spot = jnp.sum(marked * dot_nn(marked.astype(BF16), before), axis=0, keepdims=True)
        return marker, spot, anchor.astype(F32) * 32.0 + spot

    def unpack(h, flat):
        tick = (bucket[:, h * 128 : (h + 1) * 128].astype(F32) + 0.5) / BUCKETS
        lanes = lax.broadcasted_iota(jnp.int32, (128, 32 * n_col), 1).astype(F32)
        flat_h = spread_rows(flat[:, h * 128 : (h + 1) * 128])
        take = (lanes == flat_h[:, :1]).astype(F32).astype(BF16)
        paired = dot_nn(take, got_rows[...].reshape(32 * n_col, features))
        data = x_buf[col, h * 128 : (h + 1) * 128, :].astype(F32)
        t = spread_rows(tick)[:, :1]
        out_i[h * 128 : (h + 1) * 128, :] = ((1.0 - t) * data + t * paired).astype(BF16)
        diff = data - paired
        cost = diff * diff
        square = data * data
        fold_c = cost[:, :128]
        fold_s = square[:, :128]
        for q in range(1, features // 128):
            fold_c = fold_c + cost[:, q * 128 : (q + 1) * 128]
            fold_s = fold_s + square[:, q * 128 : (q + 1) * 128]
        return turn_to_lanes(fold_c) / features, turn_to_lanes(fold_s) / features

    half_span = span // 2
    empty = tuple(jnp.zeros((8, rows), F32) for _ in range(n_col))
    for it in range(ITERS):
        if it == 0:
            for h in range(2):
                each(n_col, lambda k: f_copy(it, k, h).start())
            prepare()
        else:
            g_spread(it - 1, 0)
            acc = row_sums(0, n_col, 0, half_span, empty)
            g_spread(it - 1, 1)
            f_leave(it, 0, row_sums(0, f_half, half_span, half_span, acc[:f_half]))
            f_leave(it, 1, row_sums(f_half, n_col, half_span, half_span, acc[f_half:]))
        if it == ITERS - 1:
            each(n_col, lambda k: p_copy(k).wait_recv())
            marker, spot, flat = own_slots()
            cost_a, square_a = unpack(0, flat)
        f_arrived(it, 0)
        column_sums(0, f_half, 0, span)
        f_arrived(it, 1)
        column_sums(f_half, n_col, 0, half_span)
        g_leave(it, 0)
        column_sums(f_half, n_col, half_span, half_span)
        g_leave(it, 1)
        if it < ITERS - 1:
            for k in range(1 + 5 * it, 6 + 5 * it):
                p_copy(k).start()
    cost_b, square_b = unpack(1, flat)
    pair_cost = jnp.concatenate([cost_a, cost_b], axis=1)
    norm_x = jnp.concatenate([square_a, square_b], axis=1)
    big_q = jnp.concatenate([g_arrived(ITERS - 1, 0), g_arrived(ITERS - 1, 1)], axis=0)

    fine = jnp.min(jnp.where(in_range(big_q), 1.0, 0.0), axis=(0, 1), keepdims=True)
    g = jnp.where(fine > 0.0, jnp.log(big_q), jnp.nan)
    parts = three_parts(g)
    chosen = jnp.zeros((8, 32 * n_col), F32)
    for r in range(n_row):
        three = jnp.concatenate(
            [p[r : r + 1, :].astype(F32) for p in parts] + [jnp.zeros((5, rows), F32)], axis=0
        ).astype(BF16)
        chosen = chosen + dot_nt(three, pick[:, r * rows : (r + 1) * rows])
    chosen = jnp.sum(chosen, axis=0, keepdims=True)
    for q in range(n_col // 4):
        pg_got[n_col + q] = chosen[:, q * 128 : (q + 1) * 128]
    each(n_col, lambda k: q_copy(k).start())
    pg_got[col] = pg_got[n_col + col // 4]
    log_total = math.log(total_rows)
    lse = rank[pl.ds(col, 1), :]
    own_p = rank[pl.ds(n_col + col, 1), :]
    f_scaled = lse / log2e + jnp.log(own_p) + log_total - norm_x / entropic
    out_f[...] = f_scaled
    rank[0:n_row, :] = g
    out_g[...] = rank[pl.ds(row, 1), :]
    offset = lax.rem(col, 4) * 32
    grab = (
        lax.broadcasted_iota(jnp.int32, (128, rows), 0).astype(F32) == spot + offset.astype(F32)
    ).astype(F32).astype(BF16)
    each(n_col, lambda k: q_copy(k).wait_recv())
    arrived = jnp.concatenate([pg_got[d] for d in range(n_col)], axis=0)
    paired_g = jnp.zeros((n_col, rows), F32)
    for part in three_parts(arrived):
        paired_g = paired_g + dot_nn(part, grab)
    paired_g = jnp.sum(jnp.where(marker, paired_g, 0.0), axis=0, keepdims=True)
    out_c[...] = pair_cost
    out_w[...] = f_scaled + paired_g + pair_cost / entropic - log_total
    out_bad[0, 0] = jnp.max(jnp.where(arrived == arrived, 0.0, 1.0)).astype(jnp.int32)

    for move in y_moves:
        y_copy(move, False).wait_send()
    for move in x_moves:
        x_copy(move, False).wait_send()
    each(n_col, lambda k: p_copy(k).wait_send())
    each(n_col, lambda k: q_copy(k).wait_send())
    for it in range(ITERS):
        for h in range(2):
            each(n_col, lambda k: f_copy(it, k, h).wait_send())
            each(n_row, lambda k: g_copy(it, k, h).wait_send())


def shards(latents, noise, pairing, time_bucket):
    own_rows, features = latents.shape
    n_row = lax.axis_size("row")
    n_col = lax.axis_size("col")
    total_rows = own_rows * n_row * n_col
    span = own_rows * n_row
    vmem = pl.BlockSpec(memory_space=pltpu.VMEM)
    hbm = pl.BlockSpec(memory_space=pl.ANY)
    line = jax.ShapeDtypeStruct((1, own_rows), F32)
    dma = pltpu.SemaphoreType.DMA
    f, g, w, pair_cost, bad, interpolant = pl.pallas_call(
        functools.partial(kernel, n_row, n_col, features, total_rows),
        out_shape=(
            line, line, line, line,
            jax.ShapeDtypeStruct((1, 1), jnp.int32),
            jax.ShapeDtypeStruct((own_rows, features), BF16),
        ),
        in_specs=[hbm, hbm, vmem, vmem],
        out_specs=(vmem,) * 4 + (pl.BlockSpec(memory_space=pltpu.SMEM), vmem),
        scratch_shapes=[
            pltpu.VMEM((n_col, own_rows, features), BF16),
            pltpu.VMEM((n_row, own_rows, features), BF16),
            pltpu.VMEM((n_col, span, own_rows), F32),
            pltpu.VMEM((8, 8, own_rows), F32),
            pltpu.VMEM((span, 128), F32),
            pltpu.VMEM((span, 128), F32),
            pltpu.VMEM((32 * n_col, span), BF16),
            pltpu.VMEM((n_col, 32, features), BF16),
            pltpu.VMEM((n_col, 32, features), BF16),
            pltpu.VMEM((ITERS, n_col, n_col, own_rows), F32),
            pltpu.VMEM((ITERS, 2, n_row, n_row // 2, own_rows), F32),
            pltpu.VMEM((n_col + n_col // 4, 1, 128), F32),
            pltpu.VMEM((n_col, own_rows), F32),
            pltpu.VMEM((2 * n_col, own_rows), F32),
            pltpu.VMEM((2 * n_col, own_rows), F32),
            pltpu.VMEM((n_col, own_rows), jnp.int32),
            dma((2,)),
            dma((40,)), dma((40,)),
            dma((11,)), dma((11,)),
            dma((ITERS, 2 * n_col)), dma((ITERS, 2 * n_col)),
            dma((ITERS, 2 * n_row)), dma((ITERS, 2 * n_row)),
            dma((n_col,)), dma((n_col,)),
            dma((n_col,)), dma((n_col,)),
        ],
        compiler_params=pltpu.CompilerParams(
            collective_id=0, has_side_effects=True, vmem_limit_bytes=62 * 1024 * 1024
        ),
        name="pairing_plan",
    )(latents, noise, pairing.reshape(2 * n_col, own_rows // 2), time_bucket.reshape(1, own_rows))
    def again():
        exact_f, exact_g, paired_g = log_domain(latents, noise, pairing)
        log_weight = (exact_f + paired_g - pair_cost.reshape(own_rows)) / entropic + math.log(total_rows)
        return tuple(v.reshape(1, own_rows) for v in (exact_f / -entropic, exact_g / -entropic, -log_weight))

    f, g, w = lax.cond(bad[0, 0] > 0, again, lambda: (f, g, w))
    f, g, w = (v.reshape(own_rows) for v in (f, g, w))
    return f * -entropic, g * -entropic, interpolant, -w


def solution(mesh):
    placed = (P(("row", "col"), None), P(("col", "row"), None), P("row"), P(("row", "col")))
    return jax.shard_map(
        shards,
        mesh=mesh,
        in_specs=placed,
        out_specs=(
            P(("row", "col")),
            P(("col", "row")),
            P(("row", "col"), None),
            P(("row", "col")),
        ),
        check_vma=False,
    )
```

```python
import functools
import math

import jax
import jax.numpy as jnp
from jax import lax
from jax.experimental import pallas as pl
from jax.experimental.pallas import tpu as pltpu
from jax.sharding import PartitionSpec as P

ITERS = 4
BUCKETS = 1000
MESH = pl.DeviceIdType.MESH
LOW = 2.0**-40
HIGH = 2.0**40
F32 = jnp.float32
BF16 = jnp.bfloat16

entropic = 0.1


def next_one(value, axis):
    count = lax.axis_size(axis)
    return lax.ppermute(value, axis, [(i, (i + 1) % count) for i in range(count)])


def over(value, axis, join):
    def step(_, carry):
        passing, total = carry
        passing = next_one(passing, axis)
        return passing, join(total, passing)

    passing = next_one(value, axis)
    return lax.fori_loop(2, lax.axis_size(axis), step, (passing, join(value, passing)))[1]


def whole(value, axis):
    count = lax.axis_size(axis)
    size = value.shape[0]
    place = lax.axis_index(axis)

    def put(out, part, index):
        return lax.dynamic_update_slice_in_dim(out, part, index * size, 0)

    def step(k, carry):
        passing, out = carry
        passing = next_one(passing, axis)
        return passing, put(out, passing, lax.rem(place + count - k, count))

    out = put(jnp.zeros((count * size,) + value.shape[1:], value.dtype), value, place)
    passing = next_one(value, axis)
    out = put(out, passing, lax.rem(place + count - 1, count))
    return lax.fori_loop(2, count, step, (passing, out))[1]


def row_update(cost, potential, offset):
    scores = (potential[None, :] - cost) / entropic
    peak = over(jnp.max(scores, axis=1), "col", jnp.maximum)
    running = over(jnp.sum(jnp.exp(scores - peak[:, None]), axis=1), "col", jnp.add)
    return -entropic * (peak + jnp.log(running)) - offset


def column_update(cost, potential, offset):
    scores = (potential[:, None] - cost) / entropic
    peak = over(jnp.max(scores, axis=0), "row", jnp.maximum)
    running = over(jnp.sum(jnp.exp(scores - peak[None, :]), axis=0), "row", jnp.add)
    return -entropic * (peak + jnp.log(running)) - offset


def log_domain(latents, noise, pairing):
    own_rows, features = latents.shape
    col_count = lax.axis_size("col")
    total_rows = own_rows * lax.axis_size("row") * col_count
    offset = entropic * math.log(total_rows)
    column = lax.axis_index("col")
    row_place = lax.axis_index("row")
    noise_rows = whole(noise, "row")
    noise_span = noise_rows.shape[0]
    noise_norms = jnp.sum(jnp.square(noise_rows.astype(F32)), axis=1)
    data_rows = whole(latents, "col")
    section_norms = jnp.sum(jnp.square(data_rows.astype(F32)), axis=1)
    products = lax.dot_general(
        data_rows, noise_rows, (((1,), (1,)), ((), ())), preferred_element_type=F32
    )
    cost = (section_norms[:, None] + noise_norms[None, :] - 2.0 * products) / features
    potential_g = jnp.zeros((noise_span,), F32)
    potential_f = jnp.zeros((cost.shape[0],), F32)
    def iterate(_, potentials):
        updated = row_update(cost, potentials[1], offset)
        return updated, column_update(cost, updated, offset)

    potential_f, potential_g = lax.fori_loop(0, ITERS, iterate, (potential_f, potential_g))
    own_f = lax.dynamic_slice_in_dim(potential_f, column * own_rows, own_rows)
    own_g = lax.dynamic_slice_in_dim(potential_g, row_place * own_rows, own_rows)
    all_g = whole(potential_g, "col")
    own_requests = lax.dynamic_slice_in_dim(pairing, column * own_rows, own_rows)
    return own_f, own_g, all_g[own_requests]


def dot_nt(a, b):
    return lax.dot_general(a, b, (((1,), (1,)), ((), ())), preferred_element_type=F32)


def dot_nn(a, b):
    return lax.dot_general(a, b, (((1,), (0,)), ((), ())), preferred_element_type=F32)


def three_parts(v):
    hi = v.astype(BF16)
    rest = v - hi.astype(F32)
    mid = rest.astype(BF16)
    low = (rest - mid.astype(F32)).astype(BF16)
    return hi, mid, low


def turn_to_lanes(v):
    n = v.shape[0]
    parts = [
        jnp.sum(jnp.transpose(v[q * 128 : (q + 1) * 128, :]), axis=0, keepdims=True)
        for q in range(n // 128)
    ]
    return parts[0] if len(parts) == 1 else jnp.concatenate(parts, axis=1)


def spread_rows(v):
    return jnp.transpose(jnp.broadcast_to(v, (128, 128)))


def kernel(
    n_row, n_col, features, total_rows,
    lat, noi, req_in, bucket_in,
    out_f, out_g, out_w, out_c, out_bad, out_all,
    x_buf, y_buf, e_buf, s_buf, norm_y, wide, pick, send_rows, got_rows,
    f_got, g_got, pg_got, peak, scale, rank, asked, req, bucket, out_i,
    own_sem, x_send, x_recv, y_send, y_recv, f_send, f_recv, g_send, g_recv,
    p_send, p_recv, q_send, q_recv,
):
    rows = 256
    span = n_row * rows
    f_half = n_col // 2
    g_half = n_row // 2
    row = lax.axis_index("row")
    col = lax.axis_index("col")
    log2e = math.log2(math.e)
    unit = log2e / (features * entropic)

    z, x = col // 4, lax.rem(col, 4)
    y, core = row // 2, lax.rem(row, 2)

    def col_at(dz, dx):
        return lax.rem(z + (dz + 8), 4) * 4 + lax.rem(x + (dx + 8), 4)

    def row_at(dy, other):
        return lax.rem(y + (dy + 8), 4) * 2 + (1 - core if other else core)

    col_order = sorted(range(1, n_col), key=lambda k: -(min(k // 4, 4 - k // 4) + min(k % 4, 4 - k % 4)))
    row_order = sorted(range(1, n_row), key=lambda k: -(2 * min(k // 2, 4 - k // 2) + k % 2))

    def col_of(k):
        return col_at(k // 4, k % 4)

    def col_peer(k):
        return {"col": col_of(k)}

    def row_peer(k):
        return {"row": row_at(k // 2, k % 2 == 1)}

    barrier = pltpu.get_barrier_semaphore()

    for peer in [col_peer(k) for k in col_order] + [row_peer(k) for k in row_order]:
        pl.semaphore_signal(barrier, inc=1, device_id=peer, device_id_type=MESH)
    own_x = pltpu.make_async_copy(lat, x_buf.at[col], own_sem.at[0])
    own_y = pltpu.make_async_copy(noi, y_buf.at[row], own_sem.at[1])
    own_req = pltpu.make_async_copy(req_in, req, own_sem.at[2])
    own_bucket = pltpu.make_async_copy(bucket_in, bucket, own_sem.at[3])
    own_x.start()
    own_y.start()
    own_req.start()
    own_bucket.start()
    pl.semaphore_wait(barrier, n_col + n_row - 2)

    steps = {"x+": (0, 1), "x-": (0, -1), "z+": (1, 0), "z-": (-1, 0)}
    half = rows // 2
    quarter = rows // 4
    x_moves = {}
    for way in steps:
        first = way[1] == "+"
        back = -1 if first else 1
        if way[0] == "x":
            x_moves[way, "A"] = (0, 0, 0, half)
            x_moves[way, "fA"] = (0, back, 0 if first else quarter, quarter)
            x_moves[way, "B"] = (0, 0, half, half)
            for d in (-1, 1, 2):
                x_moves[way, "B", d] = (d, 0, half, half)
            for d in (0, -1, 1, 2):
                x_moves[way, "fB", d] = (d, back, half if first else half + quarter, quarter)
        else:
            x_moves[way, "B"] = (0, 0, half, half)
            x_moves[way, "fB"] = (back, 0, half if first else half + quarter, quarter)
            x_moves[way, "A"] = (0, 0, 0, half)
            for d in (-1, 1, 2):
                x_moves[way, "A", d] = (0, d, 0, half)
            for d in (0, -1, 1, 2):
                x_moves[way, "fA", d] = (back, d, 0 if first else quarter, quarter)
    x_index = {move: i for i, move in enumerate(x_moves)}

    def x_copy(move, arriving):
        way = steps[move[0]]
        dz, dx, start, count = x_moves[move]
        i = x_index[move]
        shift = way if arriving else (0, 0)
        place = x_buf.at[col_at(dz - shift[0], dx - shift[1]), pl.ds(start, count)]
        source = place
        if not arriving and (dz, dx) == (0, 0):
            source = lat.at[pl.ds(start, count)]
        return pltpu.make_async_remote_copy(
            src_ref=source, dst_ref=place, send_sem=x_send.at[i], recv_sem=x_recv.at[i],
            device_id={"col": col_at(*way)}, device_id_type=MESH,
        )

    def x_start(*moves):
        for move in moves:
            x_copy(move, False).start()

    def x_wait(*moves):
        for move in moves:
            x_copy(move, True).wait_recv()

    y_moves = {
        "+0": (1, 0, 0, half), "-1": (-1, 0, half, half),
        "+1": (1, 0, half, half), "-0": (-1, 0, 0, half),
        "+f": (1, -1, 0, half), "-f": (-1, 1, half, half),
        "s": (0, 0, 0, rows), "sm": (0, -1, 0, rows), "sp": (0, 1, 0, rows),
        "s0": (0, 2, 0, half), "s1": (0, 2, half, half),
    }
    y_index = {move: i for i, move in enumerate(y_moves)}

    def y_copy(move, arriving):
        way, dy, start, count = y_moves[move]
        i = y_index[move]
        place = y_buf.at[row_at(dy - (way if arriving else 0), arriving and way == 0), pl.ds(start, count)]
        source = place
        if not arriving and dy == 0:
            source = noi.at[pl.ds(start, count)]
        return pltpu.make_async_remote_copy(
            src_ref=source, dst_ref=place, send_sem=y_send.at[i], recv_sem=y_recv.at[i],
            device_id={"row": row_at(way, way == 0)}, device_id_type=MESH,
        )

    def y_start(*moves):
        for move in moves:
            y_copy(move, False).start()

    def y_wait(*moves):
        for move in moves:
            y_copy(move, True).wait_recv()

    def f_copy(it, k, h):
        place = f_got.at[it, col, pl.ds(h * f_half, f_half)]
        return pltpu.make_async_remote_copy(
            src_ref=place, dst_ref=place,
            send_sem=f_send.at[it, 2 * k + h], recv_sem=f_recv.at[it, 2 * k + h],
            device_id=col_peer(k), device_id_type=MESH,
        )

    def g_copy(it, k, h):
        place = g_got.at[it, h, row]
        return pltpu.make_async_remote_copy(
            src_ref=place, dst_ref=place,
            send_sem=g_send.at[it, 2 * k + h], recv_sem=g_recv.at[it, 2 * k + h],
            device_id=row_peer(k), device_id_type=MESH,
        )

    def p_copy(k):
        return pltpu.make_async_remote_copy(
            src_ref=send_rows.at[col_of(k)], dst_ref=got_rows.at[col],
            send_sem=p_send.at[k], recv_sem=p_recv.at[k],
            device_id=col_peer(k), device_id_type=MESH,
        )

    def q_copy(k):
        return pltpu.make_async_remote_copy(
            src_ref=pg_got.at[n_col + col_of(k) // 4], dst_ref=pg_got.at[col],
            send_sem=q_send.at[k], recv_sem=q_recv.at[k],
            device_id=col_peer(k), device_id_type=MESH,
        )

    def each(n, act):
        for k in col_order if n == n_col else row_order:
            act(k)

    y_start("+0", "-1", "s")
    x_start(("x+", "A"), ("x-", "A"), ("z+", "B"), ("z-", "B"))
    y_start("+1", "-0")
    x_start(("x+", "B"), ("x-", "B"), ("z+", "A"), ("z-", "A"))

    own_req.wait()
    own_bucket.wait()
    for c in range(n_col):
        asked[c : c + 1, :] = jnp.concatenate([req[2 * c : 2 * c + 1, :], req[2 * c + 1 : 2 * c + 2, :]], axis=1)
    requests = asked[...]
    before = (
        lax.broadcasted_iota(jnp.int32, (rows, rows), 0)
        < lax.broadcasted_iota(jnp.int32, (rows, rows), 1)
    ).astype(F32).astype(BF16)
    wanted = ((requests // span) == col).astype(F32)
    place = dot_nn(wanted.astype(BF16), before)
    rank[0:n_col, :] = jnp.where(wanted > 0.0, place, -1.0)
    rank[n_col : 2 * n_col, :] = (requests - col * span + 1).astype(F32)

    slots = lax.broadcasted_iota(jnp.int32, (32, rows), 0).astype(F32)
    places = lax.broadcasted_iota(jnp.int32, (32, span), 1).astype(F32) + 1.0

    def choose(d, _):
        chosen = rank[pl.ds(d, 1), :] == slots
        index = jnp.sum(jnp.where(chosen, rank[pl.ds(n_col + d, 1), :], 0.0), axis=1, keepdims=True)
        pick[pl.ds(pl.multiple_of(d * 32, 32), 32), :] = (places == index).astype(F32).astype(BF16)
        return 0

    lax.fori_loop(0, n_col, choose, 0)

    own_x.wait()
    own_y.wait()

    def norms(dy):
        at = pl.multiple_of(row_at(dy, False) // 2 * (2 * rows), 2 * rows)
        v = y_buf[pl.ds(row_at(dy, False) // 2 * 2, 2)].reshape(2 * rows, features).astype(F32)
        n = jnp.sum(v * v, axis=1, keepdims=True) * unit
        norm_y[pl.ds(at, 2 * rows), :] = jnp.broadcast_to(n, (2 * rows, 128))

    y_wait("+0")
    y_start("+f")
    y_wait("-1")
    y_start("-f")
    x_wait(("x+", "A"))
    x_start(("x+", "fA"), ("z+", "A", -1), ("z-", "A", -1))
    x_wait(("x-", "A"))
    x_start(("x-", "fA"), ("z+", "A", 1), ("z-", "A", 1))
    x_wait(("z+", "B"))
    x_start(("z+", "fB"), ("x+", "B", -1), ("x-", "B", -1))
    x_wait(("z-", "B"))
    x_start(("z-", "fB"), ("x+", "B", 1), ("x-", "B", 1))
    y_wait("+1")
    y_start("sm")
    y_wait("-0")
    y_start("sp")
    y_wait("s")
    norms(0)
    for way in ("x+", "x-"):
        x_wait((way, "B"))
        x_start((way, "fB", 0))
    for way in ("z+", "z-"):
        x_wait((way, "A"))
        x_start((way, "fA", 0))
    y_wait("sm", "sp")
    norms(-1)
    norms(1)

    def score(c, at, count):
        norm = norm_y[pl.ds(at, count), :]
        draws = y_buf[pl.ds(at // rows, count // rows)].reshape(count, features)
        t = dot_nt(draws, x_buf[c]) * (2.0 * unit)
        t = t - jnp.concatenate([norm, norm], axis=1)
        e_buf[c, pl.ds(at, count), :] = t
        return jnp.max(t.reshape(count // 8, 8, rows), axis=0)

    def powers(c, top):
        top = jnp.max(top, axis=0, keepdims=True)
        peak[pl.ds(c, 1), :] = top

        def part(r, total):
            at = pl.multiple_of(r * 512, 512)
            v = jnp.exp2(e_buf[c, pl.ds(at, 512), :] - top)
            e_buf[c, pl.ds(at, 512), :] = v
            return total + jnp.sum(v.reshape(64, 8, rows), axis=0)

        total = lax.fori_loop(0, span // 512, part, jnp.zeros((8, rows), F32))
        f_got[0, col, pl.ds(c, 1), :] = top + jnp.log2(jnp.sum(total, axis=0, keepdims=True))

    def pair_at(dy):
        return pl.multiple_of(row_at(dy, False) // 2 * (2 * rows), 2 * rows)

    def early(c, k):
        def part(d, top):
            at = pl.multiple_of(lax.rem(y + 3 + d, 4) * (2 * rows), 2 * rows)
            return jnp.maximum(top, score(c, at, 2 * rows))

        s_buf[k] = lax.fori_loop(0, 3, part, jnp.full((8, rows), -3.0e38, F32))

    def late(c, k):
        powers(c, jnp.maximum(s_buf[k], score(c, pair_at(2), 2 * rows)))

    def block(c, k):
        powers(c, score(c, 0, span))

    near = (-1, 1)
    blocks = ((0, 0), (0, -1), (0, 1), (-1, 0), (1, 0), (-1, -1), (-1, 1), (1, -1), (1, 1),
              (0, 2), (2, 0), (-1, 2), (2, -1), (1, 2), (2, 1), (2, 2))

    def some_blocks(act, first, last):
        def step(k, _):
            dz = jnp.int32(0)
            dx = jnp.int32(0)
            for i in range(first, last):
                dz = jnp.where(k == i, blocks[i][0], dz)
                dx = jnp.where(k == i, blocks[i][1], dx)
            act(lax.rem(z + dz + 8, 4) * 4 + lax.rem(x + dx + 8, 4), k)
            return 0

        lax.fori_loop(first, last, step, 0)

    some_blocks(early, 0, 2)
    y_wait("+f")
    y_start("s0")
    y_wait("-f")
    y_start("s1")
    some_blocks(early, 2, 5)
    y_wait("s0", "s1")
    norms(2)
    some_blocks(late, 0, 5)
    x_wait(("x+", "fA"), ("x-", "fA"))
    x_start(("z+", "A", 2), ("z-", "A", 2))
    x_wait(("z+", "fB"), ("z-", "fB"))
    x_start(("x+", "B", 2), ("x-", "B", 2))
    x_wait(("x+", "fB", 0), ("x-", "fB", 0), ("z+", "fA", 0), ("z-", "fA", 0))
    some_blocks(block, 9, 11)
    for d in near:
        for way in ("x+", "x-"):
            x_wait((way, "B", d))
            x_start((way, "fB", d))
        for way in ("z+", "z-"):
            x_wait((way, "A", d))
            x_start((way, "fA", d))
    some_blocks(block, 5, 9)
    for way in ("x+", "x-"):
        x_wait((way, "B", 2))
        x_start((way, "fB", 2))
    for way in ("z+", "z-"):
        x_wait((way, "A", 2))
        x_start((way, "fA", 2))
    x_wait(("x+", "fB", -1), ("x-", "fB", -1), ("z+", "fA", -1), ("z-", "fA", -1))
    some_blocks(block, 11, 13)
    x_wait(("x+", "fB", 1), ("x-", "fB", 1), ("z+", "fA", 1), ("z-", "fA", 1))
    some_blocks(block, 13, 15)
    x_wait(("x+", "fB", 2), ("x-", "fB", 2), ("z+", "fA", 2), ("z-", "fA", 2))
    some_blocks(block, 15, 16)

    def in_range(v):
        return (v >= LOW) & (v <= HIGH)

    def column_sums(first, last, start, count):
        def body(q, _):
            at = pl.multiple_of(start + q * 256, 256)
            total = jnp.zeros((256, 128), F32) if first == 0 else wide[pl.ds(at, 256), :]
            for c in range(first, last, 2):
                four = [
                    e_buf[d, pl.ds(at, 256), h : h + 128] * scale[d : d + 1, h : h + 128]
                    for d in (c, c + 1)
                    for h in (0, 128)
                ]
                total = total + ((four[0] + four[1]) + (four[2] + four[3]))
            wide[pl.ds(at, 256), :] = total
            return 0

        lax.fori_loop(0, count // 256, body, 0)

    def row_sums(first, last, start, count, acc):
        def body(j, acc):
            at = pl.multiple_of(start + j * 128, 128)
            b = wide[pl.ds(at, 128), :]
            b = jnp.concatenate([b, b], axis=1)
            return tuple(
                acc[c - first] + jnp.sum((e_buf[c, pl.ds(at, 128), :] * b).reshape(16, 8, rows), axis=0)
                for c in range(first, last)
            )

        return lax.fori_loop(0, count // 128, body, acc)

    def log_sum(parts):
        top = parts[0]
        for part in parts[1:]:
            top = jnp.maximum(top, part)
        total = jnp.exp2(parts[0] - top)
        for part in parts[1:]:
            total = total + jnp.exp2(part - top)
        return top + jnp.log2(total)

    def summed(parts):
        total = parts[0]
        for part in parts[1:]:
            total = total + part
        return total

    def f_arrived(it, h):
        each(n_col, lambda k: f_copy(it, k, h).wait_recv())
        lo, hi = h * f_half, (h + 1) * f_half
        parts = [f_got[it, d, lo:hi] for d in range(n_col)]
        if it == 0:
            lse = log_sum(parts)
            rank[lo:hi, :] = lse
            weight = jnp.exp2(peak[lo:hi, :] - lse)
            scale[n_col + lo : n_col + hi, :] = weight
            scale[lo:hi, :] = weight
        else:
            total = summed(parts)
            a = jnp.where(in_range(total), 1.0 / total, jnp.nan)
            scale[lo:hi, :] = a * scale[n_col + lo : n_col + hi, :]
            if it == ITERS - 1:
                rank[n_col + lo : n_col + hi, :] = total

    def g_arrived(it, h):
        each(n_row, lambda k: g_copy(it, k, h).wait_recv())
        return summed([g_got[it, h, d] for d in range(n_row)])

    def g_spread(it, h):
        total = g_arrived(it, h)
        b = jnp.where(in_range(total), 1.0 / total, jnp.nan)
        for r in range(g_half):
            for q in range(2):
                at = (h * g_half + r) * rows + q * 128
                wide[at : at + 128, :] = spread_rows(b[r : r + 1, q * 128 : (q + 1) * 128])

    def f_leave(it, h, acc):
        for i in range(f_half):
            c = h * f_half + i
            f_got[it, col, c : c + 1, :] = (
                jnp.sum(acc[i], axis=0, keepdims=True) * scale[n_col + c : n_col + c + 1, :]
            )
        each(n_col, lambda k: f_copy(it, k, h).start())

    def g_leave(it, h):
        for i in range(g_half):
            at = (h * g_half + i) * rows
            g_got[it, h, row, i : i + 1, :] = turn_to_lanes(wide[at : at + rows, :])
        each(n_row, lambda k: g_copy(it, k, h).start())

    def prepare():
        def fill(q, _):
            at = pl.multiple_of(q * 128, 128)
            total = jnp.zeros((128, features), F32)
            for r in range(n_row):
                total = total + dot_nn(pick[pl.ds(at, 128), r * rows : (r + 1) * rows], y_buf[r])
            send_rows[pl.ds(q * 4, 4)] = total.astype(BF16).reshape(4, 32, features)
            return 0

        lax.fori_loop(0, n_col // 4, fill, 0)
        got_rows[col] = send_rows[col]

    def own_slots():
        mine = asked[pl.ds(col, 1), :]
        anchor = mine // span
        marker = lax.broadcasted_iota(jnp.int32, (n_col, rows), 0) == anchor
        marked = marker.astype(F32)
        spot = jnp.sum(marked * dot_nn(marked.astype(BF16), before), axis=0, keepdims=True)
        return marker, spot, anchor.astype(F32) * 32.0 + spot

    def unpack(h, flat):
        tick = (bucket[:, h * 128 : (h + 1) * 128].astype(F32) + 0.5) / BUCKETS
        lanes = lax.broadcasted_iota(jnp.int32, (128, 32 * n_col), 1).astype(F32)
        flat_h = spread_rows(flat[:, h * 128 : (h + 1) * 128])
        take = (lanes == flat_h[:, :1]).astype(F32).astype(BF16)
        paired = dot_nn(take, got_rows[...].reshape(32 * n_col, features))
        data = x_buf[col, h * 128 : (h + 1) * 128, :].astype(F32)
        t = spread_rows(tick)[:, :1]
        out_i[h * 128 : (h + 1) * 128, :] = ((1.0 - t) * data + t * paired).astype(BF16)
        diff = data - paired
        cost = diff * diff
        square = data * data
        fold_c = cost[:, :128]
        fold_s = square[:, :128]
        for q in range(1, features // 128):
            fold_c = fold_c + cost[:, q * 128 : (q + 1) * 128]
            fold_s = fold_s + square[:, q * 128 : (q + 1) * 128]
        return turn_to_lanes(fold_c) / features, turn_to_lanes(fold_s) / features

    half_span = span // 2
    empty = tuple(jnp.zeros((8, rows), F32) for _ in range(n_col))
    for it in range(ITERS):
        if it == 0:
            for h in range(2):
                each(n_col, lambda k: f_copy(it, k, h).start())
            prepare()
        else:
            g_spread(it - 1, 0)
            acc = row_sums(0, n_col, 0, half_span, empty)
            g_spread(it - 1, 1)
            f_leave(it, 0, row_sums(0, f_half, half_span, half_span, acc[:f_half]))
            f_leave(it, 1, row_sums(f_half, n_col, half_span, half_span, acc[f_half:]))
        if it == ITERS - 1:
            each(n_col, lambda k: p_copy(k).wait_recv())
            marker, spot, flat = own_slots()
            cost_a, square_a = unpack(0, flat)
        f_arrived(it, 0)
        column_sums(0, f_half, 0, span)
        f_arrived(it, 1)
        column_sums(f_half, n_col, 0, half_span)
        g_leave(it, 0)
        column_sums(f_half, n_col, half_span, half_span)
        g_leave(it, 1)
        if it < ITERS - 1:
            for k in col_order[5 * it : 5 * it + 5]:
                p_copy(k).start()
    cost_b, square_b = unpack(1, flat)
    leave_i = pltpu.make_async_copy(out_i, out_all, own_sem.at[4])
    leave_i.start()
    pair_cost = jnp.concatenate([cost_a, cost_b], axis=1)
    norm_x = jnp.concatenate([square_a, square_b], axis=1)
    big_q = jnp.concatenate([g_arrived(ITERS - 1, 0), g_arrived(ITERS - 1, 1)], axis=0)

    fine = jnp.min(jnp.where(in_range(big_q), 1.0, 0.0), axis=(0, 1), keepdims=True)
    g = jnp.where(fine > 0.0, jnp.log(big_q), jnp.nan)
    parts = three_parts(g)
    chosen = jnp.zeros((8, 32 * n_col), F32)
    for r in range(n_row):
        three = jnp.concatenate(
            [p[r : r + 1, :].astype(F32) for p in parts] + [jnp.zeros((5, rows), F32)], axis=0
        ).astype(BF16)
        chosen = chosen + dot_nt(three, pick[:, r * rows : (r + 1) * rows])
    chosen = jnp.sum(chosen, axis=0, keepdims=True)
    for q in range(n_col // 4):
        pg_got[n_col + q] = chosen[:, q * 128 : (q + 1) * 128]
    each(n_col, lambda k: q_copy(k).start())
    pg_got[col] = pg_got[n_col + col // 4]
    log_total = math.log(total_rows)
    lse = rank[pl.ds(col, 1), :]
    own_p = rank[pl.ds(n_col + col, 1), :]
    f_scaled = lse / log2e + jnp.log(own_p) + log_total - norm_x / entropic
    out_f[...] = f_scaled
    rank[0:n_row, :] = g
    out_g[...] = rank[pl.ds(row, 1), :]
    offset = lax.rem(col, 4) * 32
    grab = (
        lax.broadcasted_iota(jnp.int32, (128, rows), 0).astype(F32) == spot + offset.astype(F32)
    ).astype(F32).astype(BF16)
    each(n_col, lambda k: q_copy(k).wait_recv())
    arrived = jnp.concatenate([pg_got[d] for d in range(n_col)], axis=0)
    paired_g = jnp.zeros((n_col, rows), F32)
    for part in three_parts(arrived):
        paired_g = paired_g + dot_nn(part, grab)
    paired_g = jnp.sum(jnp.where(marker, paired_g, 0.0), axis=0, keepdims=True)
    out_c[...] = pair_cost
    out_w[...] = f_scaled + paired_g + pair_cost / entropic - log_total
    out_bad[0, 0] = jnp.max(jnp.where(arrived == arrived, 0.0, 1.0)).astype(jnp.int32)

    leave_i.wait()
    for move in y_moves:
        y_copy(move, False).wait_send()
    for move in x_moves:
        x_copy(move, False).wait_send()
    each(n_col, lambda k: p_copy(k).wait_send())
    each(n_col, lambda k: q_copy(k).wait_send())
    for it in range(ITERS):
        for h in range(2):
            each(n_col, lambda k: f_copy(it, k, h).wait_send())
            each(n_row, lambda k: g_copy(it, k, h).wait_send())


def shards(latents, noise, pairing, time_bucket):
    own_rows, features = latents.shape
    n_row = lax.axis_size("row")
    n_col = lax.axis_size("col")
    total_rows = own_rows * n_row * n_col
    span = own_rows * n_row
    vmem = pl.BlockSpec(memory_space=pltpu.VMEM)
    hbm = pl.BlockSpec(memory_space=pl.ANY)
    line = jax.ShapeDtypeStruct((1, own_rows), F32)
    dma = pltpu.SemaphoreType.DMA
    f, g, w, pair_cost, bad, interpolant = pl.pallas_call(
        functools.partial(kernel, n_row, n_col, features, total_rows),
        out_shape=(
            line, line, line, line,
            jax.ShapeDtypeStruct((1, 1), jnp.int32),
            jax.ShapeDtypeStruct((own_rows, features), BF16),
        ),
        in_specs=[hbm, hbm, hbm, hbm],
        out_specs=(vmem,) * 4 + (pl.BlockSpec(memory_space=pltpu.SMEM), hbm),
        scratch_shapes=[
            pltpu.VMEM((n_col, own_rows, features), BF16),
            pltpu.VMEM((n_row, own_rows, features), BF16),
            pltpu.VMEM((n_col, span, own_rows), F32),
            pltpu.VMEM((8, 8, own_rows), F32),
            pltpu.VMEM((span, 128), F32),
            pltpu.VMEM((span, 128), F32),
            pltpu.VMEM((32 * n_col, span), BF16),
            pltpu.VMEM((n_col, 32, features), BF16),
            pltpu.VMEM((n_col, 32, features), BF16),
            pltpu.VMEM((ITERS, n_col, n_col, own_rows), F32),
            pltpu.VMEM((ITERS, 2, n_row, n_row // 2, own_rows), F32),
            pltpu.VMEM((n_col + n_col // 4, 1, 128), F32),
            pltpu.VMEM((n_col, own_rows), F32),
            pltpu.VMEM((2 * n_col, own_rows), F32),
            pltpu.VMEM((2 * n_col, own_rows), F32),
            pltpu.VMEM((n_col, own_rows), jnp.int32),
            pltpu.VMEM((2 * n_col, own_rows // 2), jnp.int32),
            pltpu.VMEM((1, own_rows), jnp.int32),
            pltpu.VMEM((own_rows, features), BF16),
            dma((5,)),
            dma((40,)), dma((40,)),
            dma((11,)), dma((11,)),
            dma((ITERS, 2 * n_col)), dma((ITERS, 2 * n_col)),
            dma((ITERS, 2 * n_row)), dma((ITERS, 2 * n_row)),
            dma((n_col,)), dma((n_col,)),
            dma((n_col,)), dma((n_col,)),
        ],
        compiler_params=pltpu.CompilerParams(
            collective_id=0, has_side_effects=True, vmem_limit_bytes=62 * 1024 * 1024
        ),
        name="pairing_plan",
    )(latents, noise, pairing.reshape(2 * n_col, own_rows // 2), time_bucket.reshape(1, own_rows))
    def again():
        exact_f, exact_g, paired_g = log_domain(latents, noise, pairing)
        log_weight = (exact_f + paired_g - pair_cost.reshape(own_rows)) / entropic + math.log(total_rows)
        return tuple(v.reshape(1, own_rows) for v in (exact_f / -entropic, exact_g / -entropic, -log_weight))

    f, g, w = lax.cond(bad[0, 0] > 0, again, lambda: (f, g, w))
    f, g, w = (v.reshape(own_rows) for v in (f, g, w))
    return f * -entropic, g * -entropic, interpolant, -w


def solution(mesh):
    placed = (P(("row", "col"), None), P(("col", "row"), None), P("row"), P(("row", "col")))
    return jax.shard_map(
        shards,
        mesh=mesh,
        in_specs=placed,
        out_specs=(
            P(("row", "col")),
            P(("col", "row")),
            P(("row", "col"), None),
            P(("row", "col")),
        ),
        check_vma=False,
    )
```

```python
import functools
import math

import jax
import jax.numpy as jnp
from jax import lax
from jax.experimental import pallas as pl
from jax.experimental.pallas import tpu as pltpu
from jax.sharding import PartitionSpec as P

ITERS = 4
BUCKETS = 1000
MESH = pl.DeviceIdType.MESH
LOW = 2.0**-40
HIGH = 2.0**40
F32 = jnp.float32
BF16 = jnp.bfloat16

entropic = 0.1


def next_one(value, axis):
    count = lax.axis_size(axis)
    return lax.ppermute(value, axis, [(i, (i + 1) % count) for i in range(count)])


def over(value, axis, join):
    def step(_, carry):
        passing, total = carry
        passing = next_one(passing, axis)
        return passing, join(total, passing)

    passing = next_one(value, axis)
    return lax.fori_loop(2, lax.axis_size(axis), step, (passing, join(value, passing)))[1]


def whole(value, axis):
    count = lax.axis_size(axis)
    size = value.shape[0]
    place = lax.axis_index(axis)

    def put(out, part, index):
        return lax.dynamic_update_slice_in_dim(out, part, index * size, 0)

    def step(k, carry):
        passing, out = carry
        passing = next_one(passing, axis)
        return passing, put(out, passing, lax.rem(place + count - k, count))

    out = put(jnp.zeros((count * size,) + value.shape[1:], value.dtype), value, place)
    passing = next_one(value, axis)
    out = put(out, passing, lax.rem(place + count - 1, count))
    return lax.fori_loop(2, count, step, (passing, out))[1]


def row_update(cost, potential, offset):
    scores = (potential[None, :] - cost) / entropic
    peak = over(jnp.max(scores, axis=1), "col", jnp.maximum)
    running = over(jnp.sum(jnp.exp(scores - peak[:, None]), axis=1), "col", jnp.add)
    return -entropic * (peak + jnp.log(running)) - offset


def column_update(cost, potential, offset):
    scores = (potential[:, None] - cost) / entropic
    peak = over(jnp.max(scores, axis=0), "row", jnp.maximum)
    running = over(jnp.sum(jnp.exp(scores - peak[None, :]), axis=0), "row", jnp.add)
    return -entropic * (peak + jnp.log(running)) - offset


def log_domain(latents, noise, pairing):
    own_rows, features = latents.shape
    col_count = lax.axis_size("col")
    total_rows = own_rows * lax.axis_size("row") * col_count
    offset = entropic * math.log(total_rows)
    column = lax.axis_index("col")
    row_place = lax.axis_index("row")
    noise_rows = whole(noise, "row")
    noise_span = noise_rows.shape[0]
    noise_norms = jnp.sum(jnp.square(noise_rows.astype(F32)), axis=1)
    data_rows = whole(latents, "col")
    section_norms = jnp.sum(jnp.square(data_rows.astype(F32)), axis=1)
    products = lax.dot_general(
        data_rows, noise_rows, (((1,), (1,)), ((), ())), preferred_element_type=F32
    )
    cost = (section_norms[:, None] + noise_norms[None, :] - 2.0 * products) / features
    potential_g = jnp.zeros((noise_span,), F32)
    potential_f = jnp.zeros((cost.shape[0],), F32)
    def iterate(_, potentials):
        updated = row_update(cost, potentials[1], offset)
        return updated, column_update(cost, updated, offset)

    potential_f, potential_g = lax.fori_loop(0, ITERS, iterate, (potential_f, potential_g))
    own_f = lax.dynamic_slice_in_dim(potential_f, column * own_rows, own_rows)
    own_g = lax.dynamic_slice_in_dim(potential_g, row_place * own_rows, own_rows)
    all_g = whole(potential_g, "col")
    own_requests = lax.dynamic_slice_in_dim(pairing, column * own_rows, own_rows)
    return own_f, own_g, all_g[own_requests]


def dot_nt(a, b):
    return lax.dot_general(a, b, (((1,), (1,)), ((), ())), preferred_element_type=F32)


def dot_nn(a, b):
    return lax.dot_general(a, b, (((1,), (0,)), ((), ())), preferred_element_type=F32)


def three_parts(v):
    hi = v.astype(BF16)
    rest = v - hi.astype(F32)
    mid = rest.astype(BF16)
    low = (rest - mid.astype(F32)).astype(BF16)
    return hi, mid, low


def turn_to_lanes(v):
    n = v.shape[0]
    parts = [
        jnp.sum(jnp.transpose(v[q * 128 : (q + 1) * 128, :]), axis=0, keepdims=True)
        for q in range(n // 128)
    ]
    return parts[0] if len(parts) == 1 else jnp.concatenate(parts, axis=1)


def spread_rows(v):
    return jnp.transpose(jnp.broadcast_to(v, (128, 128)))


def kernel(
    n_row, n_col, features, total_rows,
    lat, noi, req_in, bucket_in,
    out_lines, out_bad, out_all,
    x_buf, y_buf, e_buf, s_buf, norm_y, wide, pick, send_rows, got_rows,
    f_got, g_got, pg_got, peak, scale, rank, asked, req, bucket, out_i,
    own_sem, x_send, x_recv, y_send, y_recv, f_send, f_recv, g_send, g_recv,
    p_send, p_recv, q_send, q_recv,
):
    rows = 256
    span = n_row * rows
    f_half = n_col // 2
    g_half = n_row // 2
    row = lax.axis_index("row")
    col = lax.axis_index("col")
    log2e = math.log2(math.e)
    unit = log2e / (features * entropic)

    z, x = col // 4, lax.rem(col, 4)
    y, core = row // 2, lax.rem(row, 2)

    def col_at(dz, dx):
        return lax.rem(z + (dz + 8), 4) * 4 + lax.rem(x + (dx + 8), 4)

    def row_at(dy, other):
        return lax.rem(y + (dy + 8), 4) * 2 + (1 - core if other else core)

    col_order = sorted(range(1, n_col), key=lambda k: -(min(k // 4, 4 - k // 4) + min(k % 4, 4 - k % 4)))
    row_order = sorted(range(1, n_row), key=lambda k: -(2 * min(k // 2, 4 - k // 2) + k % 2))

    def col_of(k):
        return col_at(k // 4, k % 4)

    def col_peer(k):
        return {"col": col_of(k)}

    def row_peer(k):
        return {"row": row_at(k // 2, k % 2 == 1)}

    barrier = pltpu.get_barrier_semaphore()

    for peer in [col_peer(k) for k in col_order] + [row_peer(k) for k in row_order]:
        pl.semaphore_signal(barrier, inc=1, device_id=peer, device_id_type=MESH)
    own_x = pltpu.make_async_copy(lat, x_buf.at[col], own_sem.at[0])
    own_y = pltpu.make_async_copy(noi, y_buf.at[row], own_sem.at[1])
    own_req = pltpu.make_async_copy(req_in, req, own_sem.at[2])
    own_bucket = pltpu.make_async_copy(bucket_in, bucket, own_sem.at[3])
    own_x.start()
    own_y.start()
    own_req.start()
    own_bucket.start()
    pl.semaphore_wait(barrier, n_col + n_row - 2)

    steps = {"x+": (0, 1), "x-": (0, -1), "z+": (1, 0), "z-": (-1, 0)}
    half = rows // 2
    quarter = rows // 4
    x_moves = {}
    for way in steps:
        first = way[1] == "+"
        back = -1 if first else 1
        if way[0] == "x":
            x_moves[way, "A"] = (0, 0, 0, half)
            x_moves[way, "fA"] = (0, back, 0 if first else quarter, quarter)
            x_moves[way, "B"] = (0, 0, half, half)
            for d in (-1, 1, 2):
                x_moves[way, "B", d] = (d, 0, half, half)
            for d in (0, -1, 1, 2):
                x_moves[way, "fB", d] = (d, back, half if first else half + quarter, quarter)
        else:
            x_moves[way, "B"] = (0, 0, half, half)
            x_moves[way, "fB"] = (back, 0, half if first else half + quarter, quarter)
            x_moves[way, "A"] = (0, 0, 0, half)
            for d in (-1, 1, 2):
                x_moves[way, "A", d] = (0, d, 0, half)
            for d in (0, -1, 1, 2):
                x_moves[way, "fA", d] = (back, d, 0 if first else quarter, quarter)
    x_index = {move: i for i, move in enumerate(x_moves)}

    def x_copy(move, arriving):
        way = steps[move[0]]
        dz, dx, start, count = x_moves[move]
        i = x_index[move]
        shift = way if arriving else (0, 0)
        place = x_buf.at[col_at(dz - shift[0], dx - shift[1]), pl.ds(start, count)]
        source = place
        if not arriving and (dz, dx) == (0, 0):
            source = lat.at[pl.ds(start, count)]
        return pltpu.make_async_remote_copy(
            src_ref=source, dst_ref=place, send_sem=x_send.at[i], recv_sem=x_recv.at[i],
            device_id={"col": col_at(*way)}, device_id_type=MESH,
        )

    def x_start(*moves):
        for move in moves:
            x_copy(move, False).start()

    def x_wait(*moves):
        for move in moves:
            x_copy(move, True).wait_recv()

    y_moves = {
        "+0": (1, 0, 0, half), "-1": (-1, 0, half, half),
        "+1": (1, 0, half, half), "-0": (-1, 0, 0, half),
        "+f": (1, -1, 0, half), "-f": (-1, 1, half, half),
        "s": (0, 0, 0, rows), "sm": (0, -1, 0, rows), "sp": (0, 1, 0, rows),
        "s0": (0, 2, 0, half), "s1": (0, 2, half, half),
    }
    y_index = {move: i for i, move in enumerate(y_moves)}

    def y_copy(move, arriving):
        way, dy, start, count = y_moves[move]
        i = y_index[move]
        place = y_buf.at[row_at(dy - (way if arriving else 0), arriving and way == 0), pl.ds(start, count)]
        source = place
        if not arriving and dy == 0:
            source = noi.at[pl.ds(start, count)]
        return pltpu.make_async_remote_copy(
            src_ref=source, dst_ref=place, send_sem=y_send.at[i], recv_sem=y_recv.at[i],
            device_id={"row": row_at(way, way == 0)}, device_id_type=MESH,
        )

    def y_start(*moves):
        for move in moves:
            y_copy(move, False).start()

    def y_wait(*moves):
        for move in moves:
            y_copy(move, True).wait_recv()

    def f_copy(it, k, h):
        place = f_got.at[it, col, pl.ds(h * f_half, f_half)]
        return pltpu.make_async_remote_copy(
            src_ref=place, dst_ref=place,
            send_sem=f_send.at[it, 2 * k + h], recv_sem=f_recv.at[it, 2 * k + h],
            device_id=col_peer(k), device_id_type=MESH,
        )

    def g_copy(it, k, h):
        place = g_got.at[it, h, row]
        return pltpu.make_async_remote_copy(
            src_ref=place, dst_ref=place,
            send_sem=g_send.at[it, 2 * k + h], recv_sem=g_recv.at[it, 2 * k + h],
            device_id=row_peer(k), device_id_type=MESH,
        )

    def p_copy(k):
        return pltpu.make_async_remote_copy(
            src_ref=send_rows.at[col_of(k)], dst_ref=got_rows.at[col],
            send_sem=p_send.at[k], recv_sem=p_recv.at[k],
            device_id=col_peer(k), device_id_type=MESH,
        )

    def q_copy(k):
        return pltpu.make_async_remote_copy(
            src_ref=pg_got.at[n_col + col_of(k) // 4], dst_ref=pg_got.at[col],
            send_sem=q_send.at[k], recv_sem=q_recv.at[k],
            device_id=col_peer(k), device_id_type=MESH,
        )

    def each(n, act):
        for k in col_order if n == n_col else row_order:
            act(k)

    y_start("+0", "-1", "s")
    x_start(("x+", "A"), ("x-", "A"), ("z+", "B"), ("z-", "B"))
    y_start("+1", "-0")
    x_start(("x+", "B"), ("x-", "B"), ("z+", "A"), ("z-", "A"))

    own_req.wait()
    own_bucket.wait()
    for c in range(n_col):
        asked[c : c + 1, :] = jnp.concatenate([req[2 * c : 2 * c + 1, :], req[2 * c + 1 : 2 * c + 2, :]], axis=1)
    requests = asked[...]
    before = (
        lax.broadcasted_iota(jnp.int32, (rows, rows), 0)
        < lax.broadcasted_iota(jnp.int32, (rows, rows), 1)
    ).astype(F32).astype(BF16)
    wanted = ((requests // span) == col).astype(F32)
    place = dot_nn(wanted.astype(BF16), before)
    rank[0:n_col, :] = jnp.where(wanted > 0.0, place, -1.0)
    rank[n_col : 2 * n_col, :] = (requests - col * span + 1).astype(F32)

    slots = lax.broadcasted_iota(jnp.int32, (32, rows), 0).astype(F32)
    places = lax.broadcasted_iota(jnp.int32, (32, span), 1).astype(F32) + 1.0

    def choose(d, _):
        chosen = rank[pl.ds(d, 1), :] == slots
        index = jnp.sum(jnp.where(chosen, rank[pl.ds(n_col + d, 1), :], 0.0), axis=1, keepdims=True)
        pick[pl.ds(pl.multiple_of(d * 32, 32), 32), :] = (places == index).astype(F32).astype(BF16)
        return 0

    lax.fori_loop(0, n_col, choose, 0)

    own_x.wait()
    own_y.wait()

    def norms(dy):
        at = pl.multiple_of(row_at(dy, False) // 2 * (2 * rows), 2 * rows)
        v = y_buf[pl.ds(row_at(dy, False) // 2 * 2, 2)].reshape(2 * rows, features).astype(F32)
        n = jnp.sum(v * v, axis=1, keepdims=True) * unit
        norm_y[pl.ds(at, 2 * rows), :] = jnp.broadcast_to(n, (2 * rows, 128))

    y_wait("+0")
    y_start("+f")
    y_wait("-1")
    y_start("-f")
    x_wait(("x+", "A"))
    x_start(("x+", "fA"), ("z+", "A", -1), ("z-", "A", -1))
    x_wait(("x-", "A"))
    x_start(("x-", "fA"), ("z+", "A", 1), ("z-", "A", 1))
    x_wait(("z+", "B"))
    x_start(("z+", "fB"), ("x+", "B", -1), ("x-", "B", -1))
    x_wait(("z-", "B"))
    x_start(("z-", "fB"), ("x+", "B", 1), ("x-", "B", 1))
    y_wait("+1")
    y_start("sm")
    y_wait("-0")
    y_start("sp")
    y_wait("s")
    norms(0)
    for way in ("x+", "x-"):
        x_wait((way, "B"))
        x_start((way, "fB", 0))
    for way in ("z+", "z-"):
        x_wait((way, "A"))
        x_start((way, "fA", 0))
    y_wait("sm", "sp")
    norms(-1)
    norms(1)

    def score(c, at, count):
        norm = norm_y[pl.ds(at, count), :]
        draws = y_buf[pl.ds(at // rows, count // rows)].reshape(count, features)
        t = dot_nt(draws, x_buf[c]) * (2.0 * unit)
        t = t - jnp.concatenate([norm, norm], axis=1)
        e_buf[c, pl.ds(at, count), :] = t
        return jnp.max(t.reshape(count // 8, 8, rows), axis=0)

    def powers(c, top):
        top = jnp.max(top, axis=0, keepdims=True)
        peak[pl.ds(c, 1), :] = top

        def part(r, total):
            at = pl.multiple_of(r * 512, 512)
            v = jnp.exp2(e_buf[c, pl.ds(at, 512), :] - top)
            e_buf[c, pl.ds(at, 512), :] = v
            return total + jnp.sum(v.reshape(64, 8, rows), axis=0)

        total = lax.fori_loop(0, span // 512, part, jnp.zeros((8, rows), F32))
        f_got[0, col, pl.ds(c, 1), :] = top + jnp.log2(jnp.sum(total, axis=0, keepdims=True))

    def pair_at(dy):
        return pl.multiple_of(row_at(dy, False) // 2 * (2 * rows), 2 * rows)

    def early(c, k):
        def part(d, top):
            at = pl.multiple_of(lax.rem(y + 3 + d, 4) * (2 * rows), 2 * rows)
            return jnp.maximum(top, score(c, at, 2 * rows))

        s_buf[k] = lax.fori_loop(0, 3, part, jnp.full((8, rows), -3.0e38, F32))

    def late(c, k):
        powers(c, jnp.maximum(s_buf[k], score(c, pair_at(2), 2 * rows)))

    def block(c, k):
        powers(c, score(c, 0, span))

    near = (-1, 1)
    blocks = ((0, 0), (0, -1), (0, 1), (-1, 0), (1, 0), (-1, -1), (-1, 1), (1, -1), (1, 1),
              (0, 2), (2, 0), (-1, 2), (2, -1), (1, 2), (2, 1), (2, 2))

    def some_blocks(act, first, last):
        def step(k, _):
            dz = jnp.int32(0)
            dx = jnp.int32(0)
            for i in range(first, last):
                dz = jnp.where(k == i, blocks[i][0], dz)
                dx = jnp.where(k == i, blocks[i][1], dx)
            act(lax.rem(z + dz + 8, 4) * 4 + lax.rem(x + dx + 8, 4), k)
            return 0

        lax.fori_loop(first, last, step, 0)

    some_blocks(early, 0, 2)
    y_wait("+f")
    y_start("s0")
    y_wait("-f")
    y_start("s1")
    some_blocks(early, 2, 5)
    y_wait("s0", "s1")
    norms(2)
    some_blocks(late, 0, 5)
    x_wait(("x+", "fA"), ("x-", "fA"))
    x_start(("z+", "A", 2), ("z-", "A", 2))
    x_wait(("z+", "fB"), ("z-", "fB"))
    x_start(("x+", "B", 2), ("x-", "B", 2))
    x_wait(("x+", "fB", 0), ("x-", "fB", 0), ("z+", "fA", 0), ("z-", "fA", 0))
    some_blocks(block, 9, 11)
    for d in near:
        for way in ("x+", "x-"):
            x_wait((way, "B", d))
            x_start((way, "fB", d))
        for way in ("z+", "z-"):
            x_wait((way, "A", d))
            x_start((way, "fA", d))
    some_blocks(block, 5, 9)
    for way in ("x+", "x-"):
        x_wait((way, "B", 2))
        x_start((way, "fB", 2))
    for way in ("z+", "z-"):
        x_wait((way, "A", 2))
        x_start((way, "fA", 2))
    x_wait(("x+", "fB", -1), ("x-", "fB", -1), ("z+", "fA", -1), ("z-", "fA", -1))
    some_blocks(block, 11, 13)
    x_wait(("x+", "fB", 1), ("x-", "fB", 1), ("z+", "fA", 1), ("z-", "fA", 1))
    some_blocks(block, 13, 15)
    x_wait(("x+", "fB", 2), ("x-", "fB", 2), ("z+", "fA", 2), ("z-", "fA", 2))
    some_blocks(block, 15, 16)

    def in_range(v):
        return (v >= LOW) & (v <= HIGH)

    def column_sums(first, last, start, count):
        def body(q, _):
            at = pl.multiple_of(start + q * 256, 256)
            total = jnp.zeros((256, 128), F32) if first == 0 else wide[pl.ds(at, 256), :]
            for c in range(first, last, 2):
                four = [
                    e_buf[d, pl.ds(at, 256), h : h + 128] * scale[d : d + 1, h : h + 128]
                    for d in (c, c + 1)
                    for h in (0, 128)
                ]
                total = total + ((four[0] + four[1]) + (four[2] + four[3]))
            wide[pl.ds(at, 256), :] = total
            return 0

        lax.fori_loop(0, count // 256, body, 0)

    def row_sums(first, last, start, count, acc):
        def body(j, acc):
            at = pl.multiple_of(start + j * 128, 128)
            b = wide[pl.ds(at, 128), :]
            b = jnp.concatenate([b, b], axis=1)
            return tuple(
                acc[c - first] + jnp.sum((e_buf[c, pl.ds(at, 128), :] * b).reshape(16, 8, rows), axis=0)
                for c in range(first, last)
            )

        return lax.fori_loop(0, count // 128, body, acc)

    def log_sum(parts):
        top = parts[0]
        for part in parts[1:]:
            top = jnp.maximum(top, part)
        total = jnp.exp2(parts[0] - top)
        for part in parts[1:]:
            total = total + jnp.exp2(part - top)
        return top + jnp.log2(total)

    def summed(parts):
        total = parts[0]
        for part in parts[1:]:
            total = total + part
        return total

    def f_arrived(it, h):
        each(n_col, lambda k: f_copy(it, k, h).wait_recv())
        lo, hi = h * f_half, (h + 1) * f_half
        parts = [f_got[it, d, lo:hi] for d in range(n_col)]
        if it == 0:
            lse = log_sum(parts)
            rank[lo:hi, :] = lse
            weight = jnp.exp2(peak[lo:hi, :] - lse)
            scale[n_col + lo : n_col + hi, :] = weight
            scale[lo:hi, :] = weight
        else:
            total = summed(parts)
            a = jnp.where(in_range(total), 1.0 / total, jnp.nan)
            scale[lo:hi, :] = a * scale[n_col + lo : n_col + hi, :]
            if it == ITERS - 1:
                rank[n_col + lo : n_col + hi, :] = total

    def g_arrived(it, h):
        each(n_row, lambda k: g_copy(it, k, h).wait_recv())
        return summed([g_got[it, h, d] for d in range(n_row)])

    def g_spread(it, h):
        total = g_arrived(it, h)
        b = jnp.where(in_range(total), 1.0 / total, jnp.nan)
        for r in range(g_half):
            for q in range(2):
                at = (h * g_half + r) * rows + q * 128
                wide[at : at + 128, :] = spread_rows(b[r : r + 1, q * 128 : (q + 1) * 128])

    def f_leave(it, h, acc):
        for i in range(f_half):
            c = h * f_half + i
            f_got[it, col, c : c + 1, :] = (
                jnp.sum(acc[i], axis=0, keepdims=True) * scale[n_col + c : n_col + c + 1, :]
            )
        each(n_col, lambda k: f_copy(it, k, h).start())

    def g_leave(it, h):
        for i in range(g_half):
            at = (h * g_half + i) * rows
            g_got[it, h, row, i : i + 1, :] = turn_to_lanes(wide[at : at + rows, :])
        each(n_row, lambda k: g_copy(it, k, h).start())

    def prepare():
        def fill(q, _):
            at = pl.multiple_of(q * 128, 128)
            total = jnp.zeros((128, features), F32)
            for r in range(n_row):
                total = total + dot_nn(pick[pl.ds(at, 128), r * rows : (r + 1) * rows], y_buf[r])
            send_rows[pl.ds(q * 4, 4)] = total.astype(BF16).reshape(4, 32, features)
            return 0

        lax.fori_loop(0, n_col // 4, fill, 0)
        got_rows[col] = send_rows[col]

    def own_slots():
        mine = asked[pl.ds(col, 1), :]
        anchor = mine // span
        marker = lax.broadcasted_iota(jnp.int32, (n_col, rows), 0) == anchor
        marked = marker.astype(F32)
        spot = jnp.sum(marked * dot_nn(marked.astype(BF16), before), axis=0, keepdims=True)
        return marker, spot, anchor.astype(F32) * 32.0 + spot

    def unpack(h, flat):
        tick = (bucket[:, h * 128 : (h + 1) * 128].astype(F32) + 0.5) / BUCKETS
        lanes = lax.broadcasted_iota(jnp.int32, (128, 32 * n_col), 1).astype(F32)
        flat_h = spread_rows(flat[:, h * 128 : (h + 1) * 128])
        take = (lanes == flat_h[:, :1]).astype(F32).astype(BF16)
        paired = dot_nn(take, got_rows[...].reshape(32 * n_col, features))
        data = x_buf[col, h * 128 : (h + 1) * 128, :].astype(F32)
        t = spread_rows(tick)[:, :1]
        out_i[h * 128 : (h + 1) * 128, :] = ((1.0 - t) * data + t * paired).astype(BF16)
        diff = data - paired
        cost = diff * diff
        square = data * data
        fold_c = cost[:, :128]
        fold_s = square[:, :128]
        for q in range(1, features // 128):
            fold_c = fold_c + cost[:, q * 128 : (q + 1) * 128]
            fold_s = fold_s + square[:, q * 128 : (q + 1) * 128]
        return turn_to_lanes(fold_c) / features, turn_to_lanes(fold_s) / features

    half_span = span // 2
    empty = tuple(jnp.zeros((8, rows), F32) for _ in range(n_col))
    for it in range(ITERS):
        if it == 0:
            for h in range(2):
                each(n_col, lambda k: f_copy(it, k, h).start())
            prepare()
        else:
            g_spread(it - 1, 0)
            acc = row_sums(0, n_col, 0, half_span, empty)
            g_spread(it - 1, 1)
            f_leave(it, 0, row_sums(0, f_half, half_span, half_span, acc[:f_half]))
            f_leave(it, 1, row_sums(f_half, n_col, half_span, half_span, acc[f_half:]))
        if it == ITERS - 1:
            each(n_col, lambda k: p_copy(k).wait_recv())
            marker, spot, flat = own_slots()
            cost_a, square_a = unpack(0, flat)
        f_arrived(it, 0)
        column_sums(0, f_half, 0, span)
        f_arrived(it, 1)
        column_sums(f_half, n_col, 0, half_span)
        g_leave(it, 0)
        column_sums(f_half, n_col, half_span, half_span)
        g_leave(it, 1)
        if it < ITERS - 1:
            for k in col_order[5 * it : 5 * it + 5]:
                p_copy(k).start()
    cost_b, square_b = unpack(1, flat)
    leave_i = pltpu.make_async_copy(out_i, out_all, own_sem.at[4])
    leave_i.start()
    pair_cost = jnp.concatenate([cost_a, cost_b], axis=1)
    norm_x = jnp.concatenate([square_a, square_b], axis=1)
    big_q = jnp.concatenate([g_arrived(ITERS - 1, 0), g_arrived(ITERS - 1, 1)], axis=0)

    fine = jnp.min(jnp.where(in_range(big_q), 1.0, 0.0), axis=(0, 1), keepdims=True)
    g = jnp.where(fine > 0.0, jnp.log(big_q), jnp.nan)
    parts = three_parts(g)
    chosen = jnp.zeros((8, 32 * n_col), F32)
    for r in range(n_row):
        three = jnp.concatenate(
            [p[r : r + 1, :].astype(F32) for p in parts] + [jnp.zeros((5, rows), F32)], axis=0
        ).astype(BF16)
        chosen = chosen + dot_nt(three, pick[:, r * rows : (r + 1) * rows])
    chosen = jnp.sum(chosen, axis=0, keepdims=True)
    for q in range(n_col // 4):
        pg_got[n_col + q] = chosen[:, q * 128 : (q + 1) * 128]
    each(n_col, lambda k: q_copy(k).start())
    pg_got[col] = pg_got[n_col + col // 4]
    log_total = math.log(total_rows)
    lse = rank[pl.ds(col, 1), :]
    own_p = rank[pl.ds(n_col + col, 1), :]
    f_scaled = lse / log2e + jnp.log(own_p) + log_total - norm_x / entropic
    out_lines[0:1, :] = f_scaled
    rank[0:n_row, :] = g
    out_lines[1:2, :] = rank[pl.ds(row, 1), :]
    offset = lax.rem(col, 4) * 32
    grab = (
        lax.broadcasted_iota(jnp.int32, (128, rows), 0).astype(F32) == spot + offset.astype(F32)
    ).astype(F32).astype(BF16)
    each(n_col, lambda k: q_copy(k).wait_recv())
    arrived = jnp.concatenate([pg_got[d] for d in range(n_col)], axis=0)
    paired_g = jnp.zeros((n_col, rows), F32)
    for part in three_parts(arrived):
        paired_g = paired_g + dot_nn(part, grab)
    paired_g = jnp.sum(jnp.where(marker, paired_g, 0.0), axis=0, keepdims=True)
    out_lines[3:4, :] = pair_cost
    out_lines[2:3, :] = f_scaled + paired_g + pair_cost / entropic - log_total
    out_bad[0, 0] = jnp.max(jnp.where(arrived == arrived, 0.0, 1.0)).astype(jnp.int32)

    leave_i.wait()
    for move in y_moves:
        y_copy(move, False).wait_send()
    for move in x_moves:
        x_copy(move, False).wait_send()
    each(n_col, lambda k: p_copy(k).wait_send())
    each(n_col, lambda k: q_copy(k).wait_send())
    for it in range(ITERS):
        for h in range(2):
            each(n_col, lambda k: f_copy(it, k, h).wait_send())
            each(n_row, lambda k: g_copy(it, k, h).wait_send())


def shards(latents, noise, pairing, time_bucket):
    own_rows, features = latents.shape
    n_row = lax.axis_size("row")
    n_col = lax.axis_size("col")
    total_rows = own_rows * n_row * n_col
    span = own_rows * n_row
    vmem = pl.BlockSpec(memory_space=pltpu.VMEM)
    hbm = pl.BlockSpec(memory_space=pl.ANY)
    dma = pltpu.SemaphoreType.DMA
    lines, bad, interpolant = pl.pallas_call(
        functools.partial(kernel, n_row, n_col, features, total_rows),
        out_shape=(
            jax.ShapeDtypeStruct((4, own_rows), F32),
            jax.ShapeDtypeStruct((1, 1), jnp.int32),
            jax.ShapeDtypeStruct((own_rows, features), BF16),
        ),
        in_specs=[hbm, hbm, hbm, hbm],
        out_specs=(vmem, pl.BlockSpec(memory_space=pltpu.SMEM), hbm),
        scratch_shapes=[
            pltpu.VMEM((n_col, own_rows, features), BF16),
            pltpu.VMEM((n_row, own_rows, features), BF16),
            pltpu.VMEM((n_col, span, own_rows), F32),
            pltpu.VMEM((8, 8, own_rows), F32),
            pltpu.VMEM((span, 128), F32),
            pltpu.VMEM((span, 128), F32),
            pltpu.VMEM((32 * n_col, span), BF16),
            pltpu.VMEM((n_col, 32, features), BF16),
            pltpu.VMEM((n_col, 32, features), BF16),
            pltpu.VMEM((ITERS, n_col, n_col, own_rows), F32),
            pltpu.VMEM((ITERS, 2, n_row, n_row // 2, own_rows), F32),
            pltpu.VMEM((n_col + n_col // 4, 1, 128), F32),
            pltpu.VMEM((n_col, own_rows), F32),
            pltpu.VMEM((2 * n_col, own_rows), F32),
            pltpu.VMEM((2 * n_col, own_rows), F32),
            pltpu.VMEM((n_col, own_rows), jnp.int32),
            pltpu.VMEM((2 * n_col, own_rows // 2), jnp.int32),
            pltpu.VMEM((1, own_rows), jnp.int32),
            pltpu.VMEM((own_rows, features), BF16),
            dma((5,)),
            dma((40,)), dma((40,)),
            dma((11,)), dma((11,)),
            dma((ITERS, 2 * n_col)), dma((ITERS, 2 * n_col)),
            dma((ITERS, 2 * n_row)), dma((ITERS, 2 * n_row)),
            dma((n_col,)), dma((n_col,)),
            dma((n_col,)), dma((n_col,)),
        ],
        compiler_params=pltpu.CompilerParams(
            collective_id=0, has_side_effects=True, vmem_limit_bytes=62 * 1024 * 1024
        ),
        name="pairing_plan",
    )(latents, noise, pairing.reshape(2 * n_col, own_rows // 2), time_bucket.reshape(1, own_rows))

    def again():
        exact_f, exact_g, paired_g = log_domain(latents, noise, pairing)
        log_weight = (exact_f + paired_g - lines[3]) / entropic + math.log(total_rows)
        return jnp.stack([exact_f / -entropic, exact_g / -entropic, -log_weight, lines[3]])

    lines = lax.cond(bad[0, 0] > 0, again, lambda: lines)
    return lines[0] * -entropic, lines[1] * -entropic, interpolant, -lines[2]


def solution(mesh):
    placed = (P(("row", "col"), None), P(("col", "row"), None), P("row"), P(("row", "col")))
    return jax.shard_map(
        shards,
        mesh=mesh,
        in_specs=placed,
        out_specs=(
            P(("row", "col")),
            P(("col", "row")),
            P(("row", "col"), None),
            P(("row", "col")),
        ),
        check_vma=False,
    )
```

```python
import functools
import math

import jax
import jax.numpy as jnp
from jax import lax
from jax.experimental import pallas as pl
from jax.experimental.pallas import tpu as pltpu
from jax.sharding import PartitionSpec as P

ITERS = 4
BUCKETS = 1000
MESH = pl.DeviceIdType.MESH
LOW = 2.0**-40
HIGH = 2.0**40
F32 = jnp.float32
BF16 = jnp.bfloat16

entropic = 0.1


def next_one(value, axis):
    count = lax.axis_size(axis)
    return lax.ppermute(value, axis, [(i, (i + 1) % count) for i in range(count)])


def over(value, axis, join):
    def step(_, carry):
        passing, total = carry
        passing = next_one(passing, axis)
        return passing, join(total, passing)

    passing = next_one(value, axis)
    return lax.fori_loop(2, lax.axis_size(axis), step, (passing, join(value, passing)))[1]


def whole(value, axis):
    count = lax.axis_size(axis)
    size = value.shape[0]
    place = lax.axis_index(axis)

    def put(out, part, index):
        return lax.dynamic_update_slice_in_dim(out, part, index * size, 0)

    def step(k, carry):
        passing, out = carry
        passing = next_one(passing, axis)
        return passing, put(out, passing, lax.rem(place + count - k, count))

    out = put(jnp.zeros((count * size,) + value.shape[1:], value.dtype), value, place)
    passing = next_one(value, axis)
    out = put(out, passing, lax.rem(place + count - 1, count))
    return lax.fori_loop(2, count, step, (passing, out))[1]


def row_update(cost, potential, offset):
    scores = (potential[None, :] - cost) / entropic
    peak = over(jnp.max(scores, axis=1), "col", jnp.maximum)
    running = over(jnp.sum(jnp.exp(scores - peak[:, None]), axis=1), "col", jnp.add)
    return -entropic * (peak + jnp.log(running)) - offset


def column_update(cost, potential, offset):
    scores = (potential[:, None] - cost) / entropic
    peak = over(jnp.max(scores, axis=0), "row", jnp.maximum)
    running = over(jnp.sum(jnp.exp(scores - peak[None, :]), axis=0), "row", jnp.add)
    return -entropic * (peak + jnp.log(running)) - offset


def log_domain(latents, noise, pairing):
    own_rows, features = latents.shape
    col_count = lax.axis_size("col")
    total_rows = own_rows * lax.axis_size("row") * col_count
    offset = entropic * math.log(total_rows)
    column = lax.axis_index("col")
    row_place = lax.axis_index("row")
    noise_rows = whole(noise, "row")
    noise_span = noise_rows.shape[0]
    noise_norms = jnp.sum(jnp.square(noise_rows.astype(F32)), axis=1)
    data_rows = whole(latents, "col")
    section_norms = jnp.sum(jnp.square(data_rows.astype(F32)), axis=1)
    products = lax.dot_general(
        data_rows, noise_rows, (((1,), (1,)), ((), ())), preferred_element_type=F32
    )
    cost = (section_norms[:, None] + noise_norms[None, :] - 2.0 * products) / features
    potential_g = jnp.zeros((noise_span,), F32)
    potential_f = jnp.zeros((cost.shape[0],), F32)
    def iterate(_, potentials):
        updated = row_update(cost, potentials[1], offset)
        return updated, column_update(cost, updated, offset)

    potential_f, potential_g = lax.fori_loop(0, ITERS, iterate, (potential_f, potential_g))
    own_f = lax.dynamic_slice_in_dim(potential_f, column * own_rows, own_rows)
    own_g = lax.dynamic_slice_in_dim(potential_g, row_place * own_rows, own_rows)
    all_g = whole(potential_g, "col")
    own_requests = lax.dynamic_slice_in_dim(pairing, column * own_rows, own_rows)
    return own_f, own_g, all_g[own_requests]


def dot_nt(a, b):
    return lax.dot_general(a, b, (((1,), (1,)), ((), ())), preferred_element_type=F32)


def dot_nn(a, b):
    return lax.dot_general(a, b, (((1,), (0,)), ((), ())), preferred_element_type=F32)


def three_parts(v):
    hi = v.astype(BF16)
    rest = v - hi.astype(F32)
    mid = rest.astype(BF16)
    low = (rest - mid.astype(F32)).astype(BF16)
    return hi, mid, low


def turn_to_lanes(v):
    n = v.shape[0]
    parts = [
        jnp.sum(jnp.transpose(v[q * 128 : (q + 1) * 128, :]), axis=0, keepdims=True)
        for q in range(n // 128)
    ]
    return parts[0] if len(parts) == 1 else jnp.concatenate(parts, axis=1)


def spread_rows(v):
    return jnp.transpose(jnp.broadcast_to(v, (128, 128)))


def kernel(
    n_row, n_col, features, total_rows,
    lat, noi, req_in, bucket_in,
    out_lines, out_bad, out_all,
    x_buf, y_buf, e_buf, s_buf, norm_y, wide, pick, send_rows, got_rows,
    f_got, g_got, pg_got, peak, scale, rank, asked, req, bucket, out_i,
    own_sem, x_send, x_recv, y_send, y_recv, f_send, f_recv, g_send, g_recv,
    p_send, p_recv, q_send, q_recv,
):
    rows = 256
    span = n_row * rows
    f_half = n_col // 2
    g_half = n_row // 2
    row = lax.axis_index("row")
    col = lax.axis_index("col")
    log2e = math.log2(math.e)
    unit = log2e / (features * entropic)

    z, x = col // 4, lax.rem(col, 4)
    y, core = row // 2, lax.rem(row, 2)

    def col_at(dz, dx):
        return lax.rem(z + (dz + 8), 4) * 4 + lax.rem(x + (dx + 8), 4)

    def row_at(dy, other):
        return lax.rem(y + (dy + 8), 4) * 2 + (1 - core if other else core)

    col_order = sorted(range(1, n_col), key=lambda k: -(min(k // 4, 4 - k // 4) + min(k % 4, 4 - k % 4)))
    row_order = sorted(range(1, n_row), key=lambda k: -(2 * min(k // 2, 4 - k // 2) + k % 2))

    def col_of(k):
        return col_at(k // 4, k % 4)

    def col_peer(k):
        return {"col": col_of(k)}

    def row_peer(k):
        return {"row": row_at(k // 2, k % 2 == 1)}

    barrier = pltpu.get_barrier_semaphore()

    for peer in [col_peer(k) for k in col_order] + [row_peer(k) for k in row_order]:
        pl.semaphore_signal(barrier, inc=1, device_id=peer, device_id_type=MESH)
    own_x = pltpu.make_async_copy(lat, x_buf.at[col], own_sem.at[0])
    own_y = pltpu.make_async_copy(noi, y_buf.at[row], own_sem.at[1])
    own_req = pltpu.make_async_copy(req_in, req, own_sem.at[2])
    own_bucket = pltpu.make_async_copy(bucket_in, bucket, own_sem.at[3])
    own_x.start()
    own_y.start()
    own_req.start()
    own_bucket.start()
    pl.semaphore_wait(barrier, n_col + n_row - 2)

    steps = {"x+": (0, 1), "x-": (0, -1), "z+": (1, 0), "z-": (-1, 0)}
    half = rows // 2
    quarter = rows // 4
    x_moves = {}
    for way in steps:
        first = way[1] == "+"
        back = -1 if first else 1
        if way[0] == "x":
            x_moves[way, "A"] = (0, 0, 0, half)
            x_moves[way, "fA"] = (0, back, 0 if first else quarter, quarter)
            x_moves[way, "B"] = (0, 0, half, half)
            for d in (-1, 1, 2):
                x_moves[way, "B", d] = (d, 0, half, half)
            for d in (0, -1, 1, 2):
                x_moves[way, "fB", d] = (d, back, half if first else half + quarter, quarter)
        else:
            x_moves[way, "B"] = (0, 0, half, half)
            x_moves[way, "fB"] = (back, 0, half if first else half + quarter, quarter)
            x_moves[way, "A"] = (0, 0, 0, half)
            for d in (-1, 1, 2):
                x_moves[way, "A", d] = (0, d, 0, half)
            for d in (0, -1, 1, 2):
                x_moves[way, "fA", d] = (back, d, 0 if first else quarter, quarter)
    x_index = {move: i for i, move in enumerate(x_moves)}

    def x_copy(move, arriving):
        way = steps[move[0]]
        dz, dx, start, count = x_moves[move]
        i = x_index[move]
        shift = way if arriving else (0, 0)
        place = x_buf.at[col_at(dz - shift[0], dx - shift[1]), pl.ds(start, count)]
        source = place
        if not arriving and (dz, dx) == (0, 0):
            source = lat.at[pl.ds(start, count)]
        return pltpu.make_async_remote_copy(
            src_ref=source, dst_ref=place, send_sem=x_send.at[i], recv_sem=x_recv.at[i],
            device_id={"col": col_at(*way)}, device_id_type=MESH,
        )

    def x_start(*moves):
        for move in moves:
            x_copy(move, False).start()

    def x_wait(*moves):
        for move in moves:
            x_copy(move, True).wait_recv()

    y_moves = {
        "+0": (1, 0, 0, half), "-1": (-1, 0, half, half),
        "+1": (1, 0, half, half), "-0": (-1, 0, 0, half),
        "+f": (1, -1, 0, half), "-f": (-1, 1, half, half),
        "s": (0, 0, 0, rows), "sm": (0, -1, 0, rows), "sp": (0, 1, 0, rows),
        "s0": (0, 2, 0, half), "s1": (0, 2, half, half),
    }
    y_index = {move: i for i, move in enumerate(y_moves)}

    def y_copy(move, arriving):
        way, dy, start, count = y_moves[move]
        i = y_index[move]
        place = y_buf.at[row_at(dy - (way if arriving else 0), arriving and way == 0), pl.ds(start, count)]
        source = place
        if not arriving and dy == 0:
            source = noi.at[pl.ds(start, count)]
        return pltpu.make_async_remote_copy(
            src_ref=source, dst_ref=place, send_sem=y_send.at[i], recv_sem=y_recv.at[i],
            device_id={"row": row_at(way, way == 0)}, device_id_type=MESH,
        )

    def y_start(*moves):
        for move in moves:
            y_copy(move, False).start()

    def y_wait(*moves):
        for move in moves:
            y_copy(move, True).wait_recv()

    def f_copy(it, k, h):
        place = f_got.at[it, col, pl.ds(h * f_half, f_half)]
        return pltpu.make_async_remote_copy(
            src_ref=place, dst_ref=place,
            send_sem=f_send.at[it, 2 * k + h], recv_sem=f_recv.at[it, 2 * k + h],
            device_id=col_peer(k), device_id_type=MESH,
        )

    def g_copy(it, k, h):
        place = g_got.at[it, h, row]
        return pltpu.make_async_remote_copy(
            src_ref=place, dst_ref=place,
            send_sem=g_send.at[it, 2 * k + h], recv_sem=g_recv.at[it, 2 * k + h],
            device_id=row_peer(k), device_id_type=MESH,
        )

    def p_copy(k):
        return pltpu.make_async_remote_copy(
            src_ref=send_rows.at[col_of(k)], dst_ref=got_rows.at[col],
            send_sem=p_send.at[k], recv_sem=p_recv.at[k],
            device_id=col_peer(k), device_id_type=MESH,
        )

    def q_copy(k):
        return pltpu.make_async_remote_copy(
            src_ref=pg_got.at[n_col + col_of(k) // 4], dst_ref=pg_got.at[col],
            send_sem=q_send.at[k], recv_sem=q_recv.at[k],
            device_id=col_peer(k), device_id_type=MESH,
        )

    def each(n, act):
        for k in col_order if n == n_col else row_order:
            act(k)

    y_start("+0", "-1", "s")
    x_start(("x+", "A"), ("x-", "A"), ("z+", "B"), ("z-", "B"))
    y_start("+1", "-0")
    x_start(("x+", "B"), ("x-", "B"), ("z+", "A"), ("z-", "A"))

    own_req.wait()
    own_bucket.wait()
    for c in range(n_col):
        asked[c : c + 1, :] = jnp.concatenate([req[2 * c : 2 * c + 1, :], req[2 * c + 1 : 2 * c + 2, :]], axis=1)
    requests = asked[...]
    before = (
        lax.broadcasted_iota(jnp.int32, (rows, rows), 0)
        < lax.broadcasted_iota(jnp.int32, (rows, rows), 1)
    ).astype(F32).astype(BF16)
    wanted = ((requests // span) == col).astype(F32)
    place = dot_nn(wanted.astype(BF16), before)
    rank[0:n_col, :] = jnp.where(wanted > 0.0, place, -1.0)
    rank[n_col : 2 * n_col, :] = (requests - col * span + 1).astype(F32)

    slots = lax.broadcasted_iota(jnp.int32, (32, rows), 0).astype(F32)
    places = lax.broadcasted_iota(jnp.int32, (32, span), 1).astype(F32) + 1.0

    def choose(d, _):
        chosen = rank[pl.ds(d, 1), :] == slots
        index = jnp.sum(jnp.where(chosen, rank[pl.ds(n_col + d, 1), :], 0.0), axis=1, keepdims=True)
        pick[pl.ds(pl.multiple_of(d * 32, 32), 32), :] = (places == index).astype(F32).astype(BF16)
        return 0

    lax.fori_loop(0, n_col, choose, 0)

    own_x.wait()
    own_y.wait()

    def norms(dy):
        at = pl.multiple_of(row_at(dy, False) // 2 * (2 * rows), 2 * rows)
        v = y_buf[pl.ds(row_at(dy, False) // 2 * 2, 2)].reshape(2 * rows, features).astype(F32)
        n = jnp.sum(v * v, axis=1, keepdims=True) * unit
        norm_y[pl.ds(at, 2 * rows), :] = jnp.broadcast_to(n, (2 * rows, 128))

    y_wait("+0")
    y_start("+f")
    y_wait("-1")
    y_start("-f")
    x_wait(("x+", "A"))
    x_start(("x+", "fA"), ("z+", "A", -1), ("z-", "A", -1))
    x_wait(("x-", "A"))
    x_start(("x-", "fA"), ("z+", "A", 1), ("z-", "A", 1))
    x_wait(("z+", "B"))
    x_start(("z+", "fB"), ("x+", "B", -1), ("x-", "B", -1))
    x_wait(("z-", "B"))
    x_start(("z-", "fB"), ("x+", "B", 1), ("x-", "B", 1))
    y_wait("+1")
    y_start("sm")
    y_wait("-0")
    y_start("sp")
    y_wait("s")
    norms(0)
    for way in ("x+", "x-"):
        x_wait((way, "B"))
        x_start((way, "fB", 0))
    for way in ("z+", "z-"):
        x_wait((way, "A"))
        x_start((way, "fA", 0))
    y_wait("sm", "sp")
    norms(-1)
    norms(1)

    def score(c, at, count):
        norm = norm_y[pl.ds(at, count), :]
        draws = y_buf[pl.ds(at // rows, count // rows)].reshape(count, features)
        t = dot_nt(draws, x_buf[c]) * (2.0 * unit)
        t = t - jnp.concatenate([norm, norm], axis=1)
        e_buf[c, pl.ds(at, count), :] = t
        return jnp.max(t.reshape(count // 8, 8, rows), axis=0)

    def powers(c, top):
        top = jnp.max(top, axis=0, keepdims=True)
        peak[pl.ds(c, 1), :] = top

        def part(r, total):
            at = pl.multiple_of(r * 512, 512)
            v = jnp.exp2(e_buf[c, pl.ds(at, 512), :] - top)
            e_buf[c, pl.ds(at, 512), :] = v
            return total + jnp.sum(v.reshape(64, 8, rows), axis=0)

        total = lax.fori_loop(0, span // 512, part, jnp.zeros((8, rows), F32))
        f_got[0, col, pl.ds(c, 1), :] = top + jnp.log2(jnp.sum(total, axis=0, keepdims=True))

    def pair_at(dy):
        return pl.multiple_of(row_at(dy, False) // 2 * (2 * rows), 2 * rows)

    def early(c, k):
        def part(d, top):
            at = pl.multiple_of(lax.rem(y + 3 + d, 4) * (2 * rows), 2 * rows)
            return jnp.maximum(top, score(c, at, 2 * rows))

        s_buf[k] = lax.fori_loop(0, 3, part, jnp.full((8, rows), -3.0e38, F32))

    def late(c, k):
        powers(c, jnp.maximum(s_buf[k], score(c, pair_at(2), 2 * rows)))

    def block(c, k):
        powers(c, score(c, 0, span))

    near = (-1, 1)
    blocks = ((0, 0), (0, -1), (0, 1), (-1, 0), (1, 0), (-1, -1), (-1, 1), (1, -1), (1, 1),
              (0, 2), (2, 0), (-1, 2), (2, -1), (1, 2), (2, 1), (2, 2))

    def some_blocks(act, first, last):
        def step(k, _):
            dz = jnp.int32(0)
            dx = jnp.int32(0)
            for i in range(first, last):
                dz = jnp.where(k == i, blocks[i][0], dz)
                dx = jnp.where(k == i, blocks[i][1], dx)
            act(lax.rem(z + dz + 8, 4) * 4 + lax.rem(x + dx + 8, 4), k)
            return 0

        lax.fori_loop(first, last, step, 0)

    some_blocks(early, 0, 2)
    y_wait("+f")
    y_start("s0")
    y_wait("-f")
    y_start("s1")
    some_blocks(early, 2, 5)
    y_wait("s0", "s1")
    norms(2)
    some_blocks(late, 0, 5)
    x_wait(("x+", "fA"), ("x-", "fA"))
    x_start(("z+", "A", 2), ("z-", "A", 2))
    x_wait(("z+", "fB"), ("z-", "fB"))
    x_start(("x+", "B", 2), ("x-", "B", 2))
    x_wait(("x+", "fB", 0), ("x-", "fB", 0), ("z+", "fA", 0), ("z-", "fA", 0))
    some_blocks(block, 9, 11)
    for d in near:
        for way in ("x+", "x-"):
            x_wait((way, "B", d))
            x_start((way, "fB", d))
        for way in ("z+", "z-"):
            x_wait((way, "A", d))
            x_start((way, "fA", d))
    some_blocks(block, 5, 9)
    for way in ("x+", "x-"):
        x_wait((way, "B", 2))
        x_start((way, "fB", 2))
    for way in ("z+", "z-"):
        x_wait((way, "A", 2))
        x_start((way, "fA", 2))
    x_wait(("x+", "fB", -1), ("x-", "fB", -1), ("z+", "fA", -1), ("z-", "fA", -1))
    some_blocks(block, 11, 13)
    x_wait(("x+", "fB", 1), ("x-", "fB", 1), ("z+", "fA", 1), ("z-", "fA", 1))
    some_blocks(block, 13, 15)
    x_wait(("x+", "fB", 2), ("x-", "fB", 2), ("z+", "fA", 2), ("z-", "fA", 2))
    some_blocks(block, 15, 16)

    def in_range(v):
        return (v >= LOW) & (v <= HIGH)

    def column_sums(first, last, start, count):
        def body(q, _):
            at = pl.multiple_of(start + q * 256, 256)
            total = jnp.zeros((256, 128), F32) if first == 0 else wide[pl.ds(at, 256), :]
            for c in range(first, last, 2):
                four = [
                    e_buf[d, pl.ds(at, 256), h : h + 128] * scale[d : d + 1, h : h + 128]
                    for d in (c, c + 1)
                    for h in (0, 128)
                ]
                total = total + ((four[0] + four[1]) + (four[2] + four[3]))
            wide[pl.ds(at, 256), :] = total
            return 0

        lax.fori_loop(0, count // 256, body, 0)

    def row_sums(first, last, start, count, acc):
        def body(j, acc):
            at = pl.multiple_of(start + j * 128, 128)
            b = wide[pl.ds(at, 128), :]
            b = jnp.concatenate([b, b], axis=1)
            return tuple(
                acc[c - first] + jnp.sum((e_buf[c, pl.ds(at, 128), :] * b).reshape(16, 8, rows), axis=0)
                for c in range(first, last)
            )

        return lax.fori_loop(0, count // 128, body, acc)

    def log_sum(parts):
        top = parts[0]
        for part in parts[1:]:
            top = jnp.maximum(top, part)
        total = jnp.exp2(parts[0] - top)
        for part in parts[1:]:
            total = total + jnp.exp2(part - top)
        return top + jnp.log2(total)

    def summed(parts):
        total = parts[0]
        for part in parts[1:]:
            total = total + part
        return total

    def f_arrived(it, h):
        each(n_col, lambda k: f_copy(it, k, h).wait_recv())
        lo, hi = h * f_half, (h + 1) * f_half
        parts = [f_got[it, d, lo:hi] for d in range(n_col)]
        if it == 0:
            lse = log_sum(parts)
            rank[lo:hi, :] = lse
            weight = jnp.exp2(peak[lo:hi, :] - lse)
            scale[n_col + lo : n_col + hi, :] = weight
            scale[lo:hi, :] = weight
        else:
            total = summed(parts)
            a = jnp.where(in_range(total), 1.0 / total, jnp.nan)
            scale[lo:hi, :] = a * scale[n_col + lo : n_col + hi, :]
            if it == ITERS - 1:
                rank[n_col + lo : n_col + hi, :] = total

    def g_arrived(it, h):
        each(n_row, lambda k: g_copy(it, k, h).wait_recv())
        return summed([g_got[it, h, d] for d in range(n_row)])

    def g_spread(it, h):
        total = g_arrived(it, h)
        b = jnp.where(in_range(total), 1.0 / total, jnp.nan)
        for r in range(g_half):
            for q in range(2):
                at = (h * g_half + r) * rows + q * 128
                wide[at : at + 128, :] = spread_rows(b[r : r + 1, q * 128 : (q + 1) * 128])

    def f_leave(it, h, acc):
        for i in range(f_half):
            c = h * f_half + i
            f_got[it, col, c : c + 1, :] = (
                jnp.sum(acc[i], axis=0, keepdims=True) * scale[n_col + c : n_col + c + 1, :]
            )
        each(n_col, lambda k: f_copy(it, k, h).start())

    def g_leave(it, h):
        for i in range(g_half):
            at = (h * g_half + i) * rows
            g_got[it, h, row, i : i + 1, :] = turn_to_lanes(wide[at : at + rows, :])
        each(n_row, lambda k: g_copy(it, k, h).start())

    def prepare():
        def fill(q, _):
            at = pl.multiple_of(q * 128, 128)
            total = jnp.zeros((128, features), F32)
            for r in range(n_row):
                total = total + dot_nn(pick[pl.ds(at, 128), r * rows : (r + 1) * rows], y_buf[r])
            send_rows[pl.ds(q * 4, 4)] = total.astype(BF16).reshape(4, 32, features)
            return 0

        lax.fori_loop(0, n_col // 4, fill, 0)
        got_rows[col] = send_rows[col]

    def own_slots():
        mine = asked[pl.ds(col, 1), :]
        anchor = mine // span
        marker = lax.broadcasted_iota(jnp.int32, (n_col, rows), 0) == anchor
        marked = marker.astype(F32)
        spot = jnp.sum(marked * dot_nn(marked.astype(BF16), before), axis=0, keepdims=True)
        return marker, spot, anchor.astype(F32) * 32.0 + spot

    def unpack(h, flat):
        tick = (bucket[:, h * 128 : (h + 1) * 128].astype(F32) + 0.5) / BUCKETS
        lanes = lax.broadcasted_iota(jnp.int32, (128, 32 * n_col), 1).astype(F32)
        flat_h = spread_rows(flat[:, h * 128 : (h + 1) * 128])
        take = (lanes == flat_h[:, :1]).astype(F32).astype(BF16)
        paired = dot_nn(take, got_rows[...].reshape(32 * n_col, features))
        data = x_buf[col, h * 128 : (h + 1) * 128, :].astype(F32)
        t = spread_rows(tick)[:, :1]
        out_i[h * 128 : (h + 1) * 128, :] = ((1.0 - t) * data + t * paired).astype(BF16)
        diff = data - paired
        cost = diff * diff
        square = data * data
        fold_c = cost[:, :128]
        fold_s = square[:, :128]
        for q in range(1, features // 128):
            fold_c = fold_c + cost[:, q * 128 : (q + 1) * 128]
            fold_s = fold_s + square[:, q * 128 : (q + 1) * 128]
        return turn_to_lanes(fold_c) / features, turn_to_lanes(fold_s) / features

    half_span = span // 2
    empty = tuple(jnp.zeros((8, rows), F32) for _ in range(n_col))
    for it in range(ITERS):
        if it == 0:
            for h in range(2):
                each(n_col, lambda k: f_copy(it, k, h).start())
            prepare()
        else:
            g_spread(it - 1, 0)
            acc = row_sums(0, n_col, 0, half_span, empty)
            g_spread(it - 1, 1)
            f_leave(it, 0, row_sums(0, f_half, half_span, half_span, acc[:f_half]))
            f_leave(it, 1, row_sums(f_half, n_col, half_span, half_span, acc[f_half:]))
        if it == ITERS - 1:
            each(n_col, lambda k: p_copy(k).wait_recv())
            marker, spot, flat = own_slots()
            cost_a, square_a = unpack(0, flat)
        f_arrived(it, 0)
        column_sums(0, f_half, 0, span)
        f_arrived(it, 1)
        if it < ITERS - 1:
            for k in col_order[5 * it : 5 * it + 5]:
                p_copy(k).start()
        column_sums(f_half, n_col, 0, half_span)
        g_leave(it, 0)
        column_sums(f_half, n_col, half_span, half_span)
        g_leave(it, 1)
    cost_b, square_b = unpack(1, flat)
    leave_i = pltpu.make_async_copy(out_i, out_all, own_sem.at[4])
    leave_i.start()
    pair_cost = jnp.concatenate([cost_a, cost_b], axis=1)
    norm_x = jnp.concatenate([square_a, square_b], axis=1)
    big_q = jnp.concatenate([g_arrived(ITERS - 1, 0), g_arrived(ITERS - 1, 1)], axis=0)

    fine = jnp.min(jnp.where(in_range(big_q), 1.0, 0.0), axis=(0, 1), keepdims=True)
    g = jnp.where(fine > 0.0, jnp.log(big_q), jnp.nan)
    parts = three_parts(g)
    chosen = jnp.zeros((8, 32 * n_col), F32)
    for r in range(n_row):
        three = jnp.concatenate(
            [p[r : r + 1, :].astype(F32) for p in parts] + [jnp.zeros((5, rows), F32)], axis=0
        ).astype(BF16)
        chosen = chosen + dot_nt(three, pick[:, r * rows : (r + 1) * rows])
    chosen = jnp.sum(chosen, axis=0, keepdims=True)
    for q in range(n_col // 4):
        pg_got[n_col + q] = chosen[:, q * 128 : (q + 1) * 128]
    each(n_col, lambda k: q_copy(k).start())
    pg_got[col] = pg_got[n_col + col // 4]
    log_total = math.log(total_rows)
    lse = rank[pl.ds(col, 1), :]
    own_p = rank[pl.ds(n_col + col, 1), :]
    f_scaled = lse / log2e + jnp.log(own_p) + log_total - norm_x / entropic
    out_lines[0:1, :] = f_scaled
    rank[0:n_row, :] = g
    out_lines[1:2, :] = rank[pl.ds(row, 1), :]
    offset = lax.rem(col, 4) * 32
    grab = (
        lax.broadcasted_iota(jnp.int32, (128, rows), 0).astype(F32) == spot + offset.astype(F32)
    ).astype(F32).astype(BF16)
    each(n_col, lambda k: q_copy(k).wait_recv())
    arrived = jnp.concatenate([pg_got[d] for d in range(n_col)], axis=0)
    paired_g = jnp.zeros((n_col, rows), F32)
    for part in three_parts(arrived):
        paired_g = paired_g + dot_nn(part, grab)
    paired_g = jnp.sum(jnp.where(marker, paired_g, 0.0), axis=0, keepdims=True)
    out_lines[3:4, :] = pair_cost
    out_lines[2:3, :] = f_scaled + paired_g + pair_cost / entropic - log_total
    out_bad[0, 0] = jnp.max(jnp.where(arrived == arrived, 0.0, 1.0)).astype(jnp.int32)

    leave_i.wait()
    for move in y_moves:
        y_copy(move, False).wait_send()
    for move in x_moves:
        x_copy(move, False).wait_send()
    each(n_col, lambda k: p_copy(k).wait_send())
    each(n_col, lambda k: q_copy(k).wait_send())
    for it in range(ITERS):
        for h in range(2):
            each(n_col, lambda k: f_copy(it, k, h).wait_send())
            each(n_row, lambda k: g_copy(it, k, h).wait_send())


def shards(latents, noise, pairing, time_bucket):
    own_rows, features = latents.shape
    n_row = lax.axis_size("row")
    n_col = lax.axis_size("col")
    total_rows = own_rows * n_row * n_col
    span = own_rows * n_row
    vmem = pl.BlockSpec(memory_space=pltpu.VMEM)
    hbm = pl.BlockSpec(memory_space=pl.ANY)
    dma = pltpu.SemaphoreType.DMA
    lines, bad, interpolant = pl.pallas_call(
        functools.partial(kernel, n_row, n_col, features, total_rows),
        out_shape=(
            jax.ShapeDtypeStruct((4, own_rows), F32),
            jax.ShapeDtypeStruct((1, 1), jnp.int32),
            jax.ShapeDtypeStruct((own_rows, features), BF16),
        ),
        in_specs=[hbm, hbm, hbm, hbm],
        out_specs=(vmem, pl.BlockSpec(memory_space=pltpu.SMEM), hbm),
        scratch_shapes=[
            pltpu.VMEM((n_col, own_rows, features), BF16),
            pltpu.VMEM((n_row, own_rows, features), BF16),
            pltpu.VMEM((n_col, span, own_rows), F32),
            pltpu.VMEM((8, 8, own_rows), F32),
            pltpu.VMEM((span, 128), F32),
            pltpu.VMEM((span, 128), F32),
            pltpu.VMEM((32 * n_col, span), BF16),
            pltpu.VMEM((n_col, 32, features), BF16),
            pltpu.VMEM((n_col, 32, features), BF16),
            pltpu.VMEM((ITERS, n_col, n_col, own_rows), F32),
            pltpu.VMEM((ITERS, 2, n_row, n_row // 2, own_rows), F32),
            pltpu.VMEM((n_col + n_col // 4, 1, 128), F32),
            pltpu.VMEM((n_col, own_rows), F32),
            pltpu.VMEM((2 * n_col, own_rows), F32),
            pltpu.VMEM((2 * n_col, own_rows), F32),
            pltpu.VMEM((n_col, own_rows), jnp.int32),
            pltpu.VMEM((2 * n_col, own_rows // 2), jnp.int32),
            pltpu.VMEM((1, own_rows), jnp.int32),
            pltpu.VMEM((own_rows, features), BF16),
            dma((5,)),
            dma((40,)), dma((40,)),
            dma((11,)), dma((11,)),
            dma((ITERS, 2 * n_col)), dma((ITERS, 2 * n_col)),
            dma((ITERS, 2 * n_row)), dma((ITERS, 2 * n_row)),
            dma((n_col,)), dma((n_col,)),
            dma((n_col,)), dma((n_col,)),
        ],
        compiler_params=pltpu.CompilerParams(
            collective_id=0, has_side_effects=True, vmem_limit_bytes=62 * 1024 * 1024
        ),
        name="pairing_plan",
    )(latents, noise, pairing.reshape(2 * n_col, own_rows // 2), time_bucket.reshape(1, own_rows))

    def again():
        exact_f, exact_g, paired_g = log_domain(latents, noise, pairing)
        log_weight = (exact_f + paired_g - lines[3]) / entropic + math.log(total_rows)
        return jnp.stack([exact_f / -entropic, exact_g / -entropic, -log_weight, lines[3]])

    lines = lax.cond(bad[0, 0] > 0, again, lambda: lines)
    return lines[0] * -entropic, lines[1] * -entropic, interpolant, -lines[2]


def solution(mesh):
    placed = (P(("row", "col"), None), P(("col", "row"), None), P("row"), P(("row", "col")))
    return jax.shard_map(
        shards,
        mesh=mesh,
        in_specs=placed,
        out_specs=(
            P(("row", "col")),
            P(("col", "row")),
            P(("row", "col"), None),
            P(("row", "col")),
        ),
        check_vma=False,
    )
```
